256 devices in a mesh: seq: 32 (over y, z), head: 8 (over x, core).
Axes of the slice: x: 4, y: 4, z: 8, core: 2. Of those that a mesh axis runs over, the one named last changes fastest.
Arguments:
- inputs: bfloat16 [65536, 32, 64], P('seq', 'head'), may hold values from -0.3984375 to 0.3984375
- log_decay: float32 [65536, 32], P('seq', 'head'), may hold values from -1.1 to 0, as said below
- in_proj: bfloat16 [65536, 2, 128], P('seq'), may hold values from -0.5 to 0.5
- out_proj: bfloat16 [65536, 2, 128], P('seq'), may hold values from -6 to 6
- upstream: bfloat16 [65536, 32, 64], P('seq', 'head'), may hold values from -0.15917969 to 0.15917969
Outputs:
- grad_inputs: bfloat16 [65536, 32, 64], P('seq', 'head')
- grad_log_decay: float32 [65536, 32], P('seq', 'head')
- grad_in_proj: float32 [65536, 2, 128], P(('seq', 'head'))
- grad_out_proj: float32 [65536, 2, 128], P(('seq', 'head'))
The draws below stay inside these ranges and needn't reach their ends.
Inputs may be any that keep to these rules, and one draw needn't show every extreme that they name: `log_decay`: each entry is negative.
All inputs are finite; a program needn't handle non-finite values.
Results may differ from the reference program's by a relative error of at most 0.0012.
Values sent between devices are 32-bit elements; how exact they have to be, the bound alone decides.
No kernel may reach another device: no remote copies, remote signals or barrier semaphores. Data moves between devices by JAX's collectives and lax.ppermute only.
A program may use at most 128 MiB of HBM per device.

```python
import math
import jax
import jax.numpy as jnp
from jax import lax

CHANNEL_WIDTH = 64
STATE = 128
HEAD_PER_GROUP = 16
SPAN = 128
HEADS = 32
TOK_DEV = 2048
GROUPS = 2
TOKENS = 65536


def draw_log_decay(key, part):
    key = jax.random.fold_in(key, 11)
    keys = jax.random.split(key, 6)
    share = 0.5
    quick = jax.random.uniform(keys[0], (HEADS,)) < share
    initial_shift = jnp.where(quick, jax.random.uniform(keys[1], (HEADS,), minval=1.0 / 40.0, maxval=1.0 / 20.0), 0.5 / TOKENS)
    segment_answer = jnp.exp(jax.random.uniform(keys[2], (TOKENS // TOK_DEV, HEADS), minval=math.log(0.5), maxval=0.0))
    segment_answer = jnp.repeat(segment_answer, TOK_DEV, axis=0)
    rough_guess = jax.random.uniform(keys[3], (TOKENS, HEADS), minval=0.5, maxval=1.5)
    spots = jax.random.randint(keys[4], (2,), 0, TOKENS)
    forgetting_factors = jax.random.uniform(keys[5], (2,), minval=0.22, maxval=0.5)
    paired_locations = (jnp.arange(TOKENS)[:, None] == spots[None, :]).astype(jnp.float32)
    word_groupings = jnp.sum(paired_locations * forgetting_factors[None, :], axis=1)
    return -(initial_shift[None, :] * segment_answer * rough_guess + word_groupings[:, None])


def shard_levels(stream_key, extent, cuts, smallest, top_value):
    gain, own = 1.0, jax.random.fold_in(stream_key, 6)
    for dim, blocks in cuts:
        heights = jnp.exp(jax.random.uniform(jax.random.fold_in(own, dim), (blocks,), jnp.float32, smallest / len(cuts), top_value / len(cuts)))
        gain = gain * jnp.repeat(heights, extent[dim] // blocks).reshape([-1 if axis == dim else 1 for axis in range(len(extent))])
    return gain


def normal_values(key, extent, width, reach, cuts=(), kind=jnp.bfloat16):
    drawn = width * jax.random.normal(key, extent, jnp.float32)
    if cuts:
        drawn = drawn * shard_levels(key, extent, cuts, -0.22, 0.18)
    return jnp.clip(drawn, -reach, reach).astype(kind)


def setup_inputs(seed: int = 0) -> dict:
    arg_keys = jax.random.split(jax.random.key(seed), 6)
    return {
        "inputs": normal_values(arg_keys[0], (TOKENS, HEADS, CHANNEL_WIDTH), 0.05, 0.3984375, ((0, 32), (1, 8))),
        "log_decay": draw_log_decay(jax.random.fold_in(arg_keys[5], 71), 0),
        "in_proj": normal_values(arg_keys[2], (TOKENS, GROUPS, STATE), STATE ** -0.5, 0.5, ((0, 32),)),
        "out_proj": normal_values(arg_keys[3], (TOKENS, GROUPS, STATE), 1.0, 6.0, ((0, 32),)),
        "upstream": normal_values(arg_keys[4], (TOKENS, HEADS, CHANNEL_WIDTH), 0.02, 0.15917969, ((0, 32), (1, 8))),
    }


finest = lax.Precision.HIGHEST

def forward(values, log_rates, in_full, out_full):
    blocks = values.shape[0] // SPAN
    blocked = values.reshape(blocks, SPAN, HEADS, CHANNEL_WIDTH)
    rates = log_rates.reshape(blocks, SPAN, HEADS)
    incoming_segments = in_full.reshape(blocks, SPAN, GROUPS, STATE)
    out_blocks = out_full.reshape(blocks, SPAN, GROUPS, STATE)
    owner = jnp.arange(HEADS) // HEAD_PER_GROUP
    lower = lax.broadcasted_iota(jnp.int32, (SPAN, SPAN), 0) >= lax.broadcasted_iota(jnp.int32, (SPAN, SPAN), 1)

    def advance(carried, item):
        piece, rate, in_piece, out_piece = item
        cumulative = jnp.cumsum(rate, axis=0)
        input_heads = in_piece[:, owner, :]
        out_heads = out_piece[:, owner, :]
        scores = jnp.einsum('ign,jgn->gij', out_piece, in_piece, precision=finest)[owner]
        across = cumulative.T
        spread = across[:, :, None] - across[:, None, :]
        decay = jnp.where(lower, jnp.exp(jnp.where(lower, spread, 0.0)), 0.0)
        within = jnp.einsum('hij,jhp->ihp', scores * decay, piece, precision=finest)
        carried_out = jnp.einsum('ihn,hnp->ihp', out_heads, carried, precision=finest) * jnp.exp(cumulative)[:, :, None]
        tail = jnp.exp(cumulative[-1:] - cumulative)
        fresh = jnp.einsum('jhn,jhp->hnp', input_heads, piece * tail[:, :, None], precision=finest)
        updated = jnp.exp(cumulative[-1])[:, None, None] * carried + fresh
        return (updated, within + carried_out)
    start = jnp.zeros((HEADS, STATE, CHANNEL_WIDTH), jnp.float32)
    final, outputs = lax.scan(jax.checkpoint(advance), start, (blocked, rates, incoming_segments, out_blocks))
    return outputs.reshape(values.shape)

def reference(inputs, log_decay, in_proj, out_proj, upstream):
    values = inputs.astype(jnp.float32)
    in_full = in_proj.astype(jnp.float32)
    out_full = out_proj.astype(jnp.float32)
    outputs, pullback = jax.vjp(forward, values, log_decay, in_full, out_full)
    grad_values, rate_gradient, grad_in, grad_out = pullback(upstream.astype(jnp.float32))
    return (grad_values.astype(jnp.bfloat16), rate_gradient, grad_in, grad_out)
```

```python
import jax
import jax.numpy as jnp
from jax import lax
from jax.experimental import pallas as pl
from jax.experimental.pallas import tpu as pltpu
from jax.sharding import PartitionSpec as P

HEADS_HERE = 4
WIDTH = 64
STATE = 128
SPAN = 128
TOK = 2048
CHUNKS = TOK // SPAN
ROWS = HEADS_HERE * WIDTH
SEQ = 32
SLICE = ROWS // SEQ
F32 = jnp.float32
BF16 = jnp.bfloat16
VMEM_LIMIT = 60 * 1024 * 1024


def dot_nn(a, b):
    return lax.dot_general(a, b, (((1,), (0,)), ((), ())), preferred_element_type=F32)


def dot_nt(a, b):
    return lax.dot_general(a, b, (((1,), (1,)), ((), ())), preferred_element_type=F32)


def split2(x):
    hi = x.astype(BF16)
    return hi, (x - hi.astype(F32)).astype(BF16)


def split3(x):
    a = x.astype(BF16)
    rest = x - a.astype(F32)
    b = rest.astype(BF16)
    return a, b, (rest - b.astype(F32)).astype(BF16)


def cat(parts, axis):
    return jnp.concatenate(parts, axis=axis)


def wide(x):
    hi, lo = split2(x)
    return cat([hi, lo], 1)


def iotas(shape):
    return lax.broadcasted_iota(jnp.int32, shape, 0), lax.broadcasted_iota(jnp.int32, shape, 1)


def ones_where(mask):
    return jnp.where(mask, 1.0, 0.0).astype(BF16)


def pad_heads(x):
    return cat([x, jnp.zeros((8 - HEADS_HERE, x.shape[1]), F32)], 0)


def spread_rows(rows):
    return cat(
        [jnp.broadcast_to(rows[h : h + 1, :], (WIDTH, SPAN)) for h in range(HEADS_HERE)], 0
    )


def head_sums(x):
    return cat(
        [
            jnp.sum(x[h * WIDTH : (h + 1) * WIDTH, :], axis=0, keepdims=True)
            for h in range(HEADS_HERE)
        ],
        0,
    )


def column_sums(log_pad, suffix):
    r, c = iotas((SPAN, SPAN))
    tri = ones_where(c > r) if suffix else ones_where(c <= r)
    return dot_nt(cat([tri] * 3, 1), cat(list(split3(log_pad)), 1))


def spread_cols(cols):
    lane = lax.broadcasted_iota(jnp.int32, (SPAN, 2 * WIDTH), 1)
    out = []
    for q in range(HEADS_HERE // 2):
        first = jnp.broadcast_to(cols[:, 2 * q : 2 * q + 1], (SPAN, 2 * WIDTH))
        second = jnp.broadcast_to(cols[:, 2 * q + 1 : 2 * q + 2], (SPAN, 2 * WIDTH))
        out.append(jnp.where(lane < WIDTH, first, second))
    return cat(out, 1)


PER1 = 4


def first_kernel(info, x_ref, y_ref, b_ref, c_ref, log_ref, msg_ref, bs_ref, cs_ref, rows_ref, state, grad):
    step = pl.program_id(0)

    @pl.when(step == 0)
    def _():
        r, c = iotas((SPAN, SPAN))
        tri = cat([ones_where(r <= c), ones_where(r > c), jnp.ones((SPAN, SPAN), BF16)], 1)
        tri = cat([tri] * 3, 0)
        stacked = cat(
            [
                cat(list(split3(pad_heads(log_ref[:, k * SPAN : (k + 1) * SPAN]))), 1)
                for k in range(CHUNKS)
            ],
            0,
        )
        sums = dot_nn(stacked, tri)
        cin = [sums[8 * k : 8 * k + 8, :SPAN] for k in range(CHUNKS)]
        suf = [sums[8 * k : 8 * k + 8, SPAN : 2 * SPAN] for k in range(CHUNKS)]
        tot = [sums[8 * k : 8 * k + 8, 2 * SPAN :] for k in range(CHUNKS)]
        before = jnp.zeros((8, SPAN), F32)
        for k in range(CHUNKS):
            rows_ref[k, 0:8, :] = cin[k]
            rows_ref[k, 8:16, :] = suf[k]
            rows_ref[k, 16:24, :] = tot[k]
            rows_ref[k, 24:32, :] = jnp.exp(before + cin[k])
            before = before + tot[k]
        after = jnp.zeros((8, SPAN), F32)
        for k in reversed(range(CHUNKS)):
            rows_ref[k, 32:40, :] = jnp.exp(after + suf[k])
            after = after + tot[k]
        msg_ref[:, 2 * SLICE :, :] = spread_rows(jnp.exp(before)).reshape(SEQ, SLICE, STATE)
        state[...] = jnp.zeros((ROWS, STATE), F32)
        grad[...] = jnp.zeros((ROWS, STATE), F32)

    group = info[0]
    r, c = iotas((SPAN, 2 * SPAN))
    pick = ones_where(c == 2 * r + group)
    own = state[...]
    back = grad[...]
    for k in range(PER1):
        here = slice(k * SPAN, (k + 1) * SPAN)
        pairs = slice(2 * k * SPAN, 2 * (k + 1) * SPAN)
        b = dot_nn(pick, b_ref[pairs, :]).astype(BF16)
        c = dot_nn(pick, c_ref[pairs, :]).astype(BF16)
        bs_ref[here, :] = b
        cs_ref[here, :] = c
        ea = rows_ref[step * PER1 + k, 24:32, :]
        er = rows_ref[step * PER1 + k, 32:40, :]
        own = own + dot_nn(wide(x_ref[:, here].astype(F32) * spread_rows(er)), cat([b, b], 0))
        back = back + dot_nn(wide(y_ref[:, here].astype(F32) * spread_rows(ea)), cat([c, c], 0))
    state[...] = own
    grad[...] = back

    @pl.when(step == pl.num_programs(0) - 1)
    def _():
        msg_ref[:, :SLICE, :] = own.reshape(SEQ, SLICE, STATE)
        msg_ref[:, SLICE : 2 * SLICE, :] = back.reshape(SEQ, SLICE, STATE)


def first_pass(info, x, y, b, c, log):
    width = PER1 * SPAN
    return pl.pallas_call(
        first_kernel,
        grid_spec=pltpu.PrefetchScalarGridSpec(
            num_scalar_prefetch=1,
            grid=(CHUNKS // PER1,),
            in_specs=[
                pl.BlockSpec((ROWS, width), lambda i, s: (0, i)),
                pl.BlockSpec((ROWS, width), lambda i, s: (0, i)),
                pl.BlockSpec((2 * width, STATE), lambda i, s: (i, 0)),
                pl.BlockSpec((2 * width, STATE), lambda i, s: (i, 0)),
                pl.BlockSpec((HEADS_HERE, TOK), lambda i, s: (0, 0)),
            ],
            out_specs=[
                pl.BlockSpec((SEQ, 3 * SLICE, STATE), lambda i, s: (0, 0, 0)),
                pl.BlockSpec((width, STATE), lambda i, s: (i, 0)),
                pl.BlockSpec((width, STATE), lambda i, s: (i, 0)),
                pl.BlockSpec((CHUNKS, 40, SPAN), lambda i, s: (0, 0, 0)),
            ],
            scratch_shapes=[pltpu.VMEM((ROWS, STATE), F32), pltpu.VMEM((ROWS, STATE), F32)],
        ),
        out_shape=[
            jax.ShapeDtypeStruct((SEQ, 3 * SLICE, STATE), F32),
            jax.ShapeDtypeStruct((TOK, STATE), BF16),
            jax.ShapeDtypeStruct((TOK, STATE), BF16),
            jax.ShapeDtypeStruct((CHUNKS, 40, SPAN), F32),
        ],
        compiler_params=pltpu.CompilerParams(vmem_limit_bytes=VMEM_LIMIT),
        cost_estimate=pl.CostEstimate(flops=800_000_000, bytes_accessed=6_000_000, transcendentals=20_000),
        name="own_states",
    )(info, x, y, b, c, log)


def scan_kernel(got_ref, after_ref, out_ref):
    carry = jnp.zeros((SLICE, STATE), F32)
    for k in range(SEQ):
        out_ref[k, :SLICE, :] = carry
        if k < SEQ - 1:
            carry = carry * got_ref[k, 2 * SLICE :, :] + got_ref[k, :SLICE, :]
    carry = jnp.zeros((SLICE, STATE), F32)
    for k in reversed(range(SEQ)):
        out_ref[k, SLICE:, :] = carry
        if k > 0:
            carry = carry * got_ref[k, 2 * SLICE :, :] + got_ref[k, SLICE : 2 * SLICE, :]


def scan_blocks(got, after):
    return pl.pallas_call(
        scan_kernel,
        in_specs=[pl.BlockSpec(memory_space=pltpu.VMEM), pl.BlockSpec(memory_space=pl.ANY)],
        out_shape=jax.ShapeDtypeStruct((SEQ, 2 * SLICE, STATE), F32),
        compiler_params=pltpu.CompilerParams(vmem_limit_bytes=VMEM_LIMIT),
        name="scan_blocks",
    )(got, after)


def forward_kernel(x_ref, y_ref, b_ref, c_ref, log_ref, rows_ref, dx_ref, db_ref, dc_ref, v_ref, next_ref, yw_ref, state):
    step = pl.program_id(0)

    @pl.when(step == 0)
    def _():
        state[...] = jnp.zeros((ROWS, STATE), F32)

    x, y, b, c = x_ref[...], y_ref[...], b_ref[...], c_ref[...]
    cin, suf, tot = rows_ref[0, 0:8, :], rows_ref[0, 8:16, :], rows_ref[0, 16:24, :]
    cols = column_sums(pad_heads(log_ref[...]), False)
    scores = dot_nt(b, c)
    xt, yt = x.T, y.T
    r, l = iotas((SPAN, SPAN))
    mask = l >= r
    total = jnp.zeros((SPAN, SPAN), F32)
    zero = jnp.zeros((WIDTH, SPAN), BF16)
    v = []
    for q in range(HEADS_HERE // 2):
        top, low = y[2 * q * WIDTH : (2 * q + 1) * WIDTH, :], y[(2 * q + 1) * WIDTH : (2 * q + 2) * WIDTH, :]
        both = cat([cat([top, zero], 1), cat([zero, low], 1)], 0)
        pair = dot_nn(xt[:, 2 * q * WIDTH : 2 * (q + 1) * WIDTH], both)
        for e in range(2):
            h = 2 * q + e
            mine = slice(h * WIDTH, (h + 1) * WIDTH)
            cross = pair[:, e * SPAN : (e + 1) * SPAN]
            gap = jnp.broadcast_to(cin[h : h + 1, :], (SPAN, SPAN)) - jnp.broadcast_to(
                cols[:, h : h + 1], (SPAN, SPAN)
            )
            decay = jnp.exp(jnp.where(mask, gap, -1e30))
            weight = scores * decay
            total = total + cross * decay
            yh = y[mine, :]
            dx = dot_nt(cat([yh, yh], 1), wide(weight))
            dx_ref[mine, :] = dx
            v.append(
                jnp.sum(weight * cross, axis=0, keepdims=True)
                - jnp.sum(x[mine, :].astype(F32) * dx, axis=0, keepdims=True)
            )
    db_ref[...] = dot_nn(wide(total), cat([c, c], 0))
    dc = dot_nn(wide(total.T), cat([b, b], 0))
    s = state[...]
    shi, slo = split2(s)
    z = dot_nt(cat([shi, slo], 1), cat([c, c], 1))
    carried = jnp.exp(cin[:HEADS_HERE]) * head_sums(z * y.astype(F32))
    v_ref[0, :HEADS_HERE, :] = cat(v, 0) + carried
    v_ref[0, HEADS_HERE:, :] = jnp.zeros((8 - HEADS_HERE, SPAN), F32)
    ytf = yt.astype(F32)
    near = jnp.exp(spread_cols(cols))
    yhi, ylo = split2(ytf * near)
    dc_ref[...] = dc + dot_nn(cat([yhi, ylo, yhi], 1), cat([shi, shi, slo], 0))
    s = s * jnp.exp(spread_rows(tot)) + dot_nn(
        wide(x.astype(F32) * jnp.exp(spread_rows(suf))), cat([b, b], 0)
    )
    state[...] = s
    next_ref[...] = s
    whi, wlo = split2((y.astype(F32) * spread_rows(rows_ref[0, 24:32, :])).T)
    yw_ref[...] = cat([whi, wlo], 1)


def chunk_specs(order):
    return [
        pl.BlockSpec((ROWS, SPAN), lambda i: (0, order(i))),
        pl.BlockSpec((ROWS, SPAN), lambda i: (0, order(i))),
        pl.BlockSpec((SPAN, STATE), lambda i: (order(i), 0)),
        pl.BlockSpec((SPAN, STATE), lambda i: (order(i), 0)),
        pl.BlockSpec((HEADS_HERE, SPAN), lambda i: (0, order(i))),
        pl.BlockSpec((1, 40, SPAN), lambda i: (order(i), 0, 0)),
    ]


def forward_pass(x, y, b, c, log, rows):
    order = lambda i: i
    return pl.pallas_call(
        forward_kernel,
        grid=(CHUNKS,),
        in_specs=chunk_specs(order),
        out_specs=[
            pl.BlockSpec((ROWS, SPAN), lambda i: (0, i)),
            pl.BlockSpec((SPAN, STATE), lambda i: (i, 0)),
            pl.BlockSpec((SPAN, STATE), lambda i: (i, 0)),
            pl.BlockSpec((1, 8, SPAN), lambda i: (i, 0, 0)),
            pl.BlockSpec((ROWS, STATE), lambda i: (i, 0)),
            pl.BlockSpec((SPAN, 2 * ROWS), lambda i: (i, 0)),
        ],
        out_shape=[
            jax.ShapeDtypeStruct((ROWS, TOK), F32),
            jax.ShapeDtypeStruct((TOK, STATE), F32),
            jax.ShapeDtypeStruct((TOK, STATE), F32),
            jax.ShapeDtypeStruct((CHUNKS, 8, SPAN), F32),
            jax.ShapeDtypeStruct((CHUNKS * ROWS, STATE), F32),
            jax.ShapeDtypeStruct((TOK, 2 * ROWS), BF16),
        ],
        scratch_shapes=[pltpu.VMEM((ROWS, STATE), F32)],
        compiler_params=pltpu.CompilerParams(vmem_limit_bytes=VMEM_LIMIT),
        cost_estimate=pl.CostEstimate(flops=3_000_000_000, bytes_accessed=16_000_000, transcendentals=3_000_000),
        name="local_forward",
    )(x, y, b, c, log, rows)


def suffix_and_all():
    r, c = iotas((SPAN, SPAN))
    tri = cat([ones_where(r >= c), jnp.ones((SPAN, SPAN), BF16)], 1)
    return cat([tri] * 3, 0)


def backward_kernel(x_ref, y_ref, b_ref, c_ref, log_ref, rows_ref, dxp_ref, dbp_ref, v_ref, next_ref, dx_ref, db_ref, dl_ref, xw_ref, grad):
    step = pl.program_id(0)

    @pl.when(step == 0)
    def _():
        grad[...] = jnp.zeros((ROWS, STATE), F32)

    x, y, b, c = x_ref[...], y_ref[...], b_ref[...], c_ref[...]
    cin, suf, tot = rows_ref[0, 0:8, :], rows_ref[0, 8:16, :], rows_ref[0, 16:24, :]
    d = grad[...]
    dhi, dlo = split2(d)
    xf = x.astype(F32)
    u = dot_nt(cat([dhi, dlo], 1), cat([b, b], 1)) * jnp.exp(spread_rows(suf))
    dx_ref[...] = dxp_ref[...] + u
    pending = v_ref[0, :HEADS_HERE, :] - head_sums(xf * u)
    constant = head_sums(next_ref[...] * d)
    sums = dot_nn(cat(list(split3(cat([pending, constant], 0))), 1), suffix_and_all())
    dl_ref[...] = sums[:HEADS_HERE, :SPAN] + sums[HEADS_HERE:, SPAN:]
    tails = column_sums(pad_heads(log_ref[...]), True)
    xt = x.T.astype(F32)
    xhi, xlo = split2(xt * jnp.exp(spread_cols(tails)))
    db_ref[...] = dbp_ref[...] + dot_nn(cat([xhi, xlo, xhi], 1), cat([dhi, dhi, dlo], 0))
    grad[...] = d * jnp.exp(spread_rows(tot)) + dot_nn(
        wide(y.astype(F32) * jnp.exp(spread_rows(cin))), cat([c, c], 0)
    )
    whi, wlo = split2((xf * spread_rows(rows_ref[0, 32:40, :])).T)
    xw_ref[...] = cat([whi, wlo], 1)


def backward_pass(x, y, b, c, log, rows, dxp, dbp, v, following):
    order = lambda i: CHUNKS - 1 - i
    return pl.pallas_call(
        backward_kernel,
        grid=(CHUNKS,),
        in_specs=chunk_specs(order)
        + [
            pl.BlockSpec((ROWS, SPAN), lambda i: (0, order(i))),
            pl.BlockSpec((SPAN, STATE), lambda i: (order(i), 0)),
            pl.BlockSpec((1, 8, SPAN), lambda i: (order(i), 0, 0)),
            pl.BlockSpec((ROWS, STATE), lambda i: (order(i), 0)),
        ],
        out_specs=[
            pl.BlockSpec((ROWS, SPAN), lambda i: (0, order(i))),
            pl.BlockSpec((SPAN, STATE), lambda i: (order(i), 0)),
            pl.BlockSpec((HEADS_HERE, SPAN), lambda i: (0, order(i))),
            pl.BlockSpec((SPAN, 2 * ROWS), lambda i: (order(i), 0)),
        ],
        out_shape=[
            jax.ShapeDtypeStruct((ROWS, TOK), F32),
            jax.ShapeDtypeStruct((TOK, STATE), F32),
            jax.ShapeDtypeStruct((HEADS_HERE, TOK), F32),
            jax.ShapeDtypeStruct((TOK, 2 * ROWS), BF16),
        ],
        scratch_shapes=[pltpu.VMEM((ROWS, STATE), F32)],
        compiler_params=pltpu.CompilerParams(vmem_limit_bytes=VMEM_LIMIT),
        cost_estimate=pl.CostEstimate(flops=2_000_000_000, bytes_accessed=16_000_000, transcendentals=1_000_000),
        name="local_backward",
    )(x, y, b, c, log, rows, dxp, dbp, v, following)


HALF = 256


def thrice(x):
    hi, lo = split2(x)
    return cat([hi, hi, lo], 0)


def triple(w):
    return cat([w, w[:, :ROWS]], 1)


def projections(bound_ref, xw_ref, yw_ref, db_ref, dc_ref):
    entering = bound_ref[:, :SLICE, :].reshape(ROWS, STATE)
    leaving = bound_ref[:, SLICE:, :].reshape(ROWS, STATE)
    db = db_ref[...] + dot_nn(triple(xw_ref[...]), thrice(leaving))
    dc = dc_ref[...] + dot_nn(triple(yw_ref[...]), thrice(entering))
    return db, dc


def send_kernel(ids, bound_ref, xw_ref, yw_ref, db_ref, dc_ref, out_ref):
    db, dc = projections(bound_ref, xw_ref, yw_ref, db_ref, dc_ref)
    out_ref[0, 0] = db
    out_ref[0, 1] = dc


def keep_kernel(ids, bound_ref, xw_ref, yw_ref, db_ref, dc_ref, got_ref, *outs):
    db, dc = projections(bound_ref, xw_ref, yw_ref, db_ref, dc_ref)
    db = db + got_ref[0, 0]
    dc = dc + got_ref[0, 1]
    for m in range(4):

        @pl.when(pl.program_id(0) == m)
        def _():
            outs[m][0] = db
            outs[m][1] = dc


def projection_specs():
    return [
        pl.BlockSpec((SEQ, 2 * SLICE, STATE), lambda i, ids: (0, 0, 0)),
        pl.BlockSpec((HALF, 2 * ROWS), lambda i, ids: (ids[i], 0)),
        pl.BlockSpec((HALF, 2 * ROWS), lambda i, ids: (ids[i], 0)),
        pl.BlockSpec((HALF, STATE), lambda i, ids: (ids[i], 0)),
        pl.BlockSpec((HALF, STATE), lambda i, ids: (ids[i], 0)),
    ]


def send_part(ids, bound, xw, yw, db, dc):
    return pl.pallas_call(
        send_kernel,
        grid_spec=pltpu.PrefetchScalarGridSpec(
            num_scalar_prefetch=1,
            grid=(4,),
            in_specs=projection_specs(),
            out_specs=pl.BlockSpec((1, 2, HALF, STATE), lambda i, ids: (i, 0, 0, 0)),
        ),
        out_shape=jax.ShapeDtypeStruct((4, 2, HALF, STATE), F32),
        compiler_params=pltpu.CompilerParams(vmem_limit_bytes=VMEM_LIMIT),
        name="projections_send",
    )(ids, bound, xw, yw, db, dc)


def keep_part(ids, bound, xw, yw, db, dc, got):
    return pl.pallas_call(
        keep_kernel,
        grid_spec=pltpu.PrefetchScalarGridSpec(
            num_scalar_prefetch=1,
            grid=(4,),
            in_specs=projection_specs()
            + [pl.BlockSpec((1, 2, HALF, STATE), lambda i, ids: (i, 0, 0, 0))],
            out_specs=[pl.BlockSpec((2, HALF, STATE), lambda i, ids: (0, 0, 0))] * 4,
        ),
        out_shape=[jax.ShapeDtypeStruct((2, HALF, STATE), F32)] * 4,
        compiler_params=pltpu.CompilerParams(vmem_limit_bytes=VMEM_LIMIT),
        name="projections_keep",
    )(ids, bound, xw, yw, db, dc, got)


def last_kernel(x_ref, y_ref, b_ref, c_ref, bound_ref, rows_ref, dx_ref, dlp_ref, out_ref, dl_ref, pend):
    step = pl.program_id(0)
    x, y, b, c = (
        x_ref[...].astype(F32),
        y_ref[...].astype(F32),
        b_ref[...],
        c_ref[...],
    )
    entering = bound_ref[:, :SLICE, :].reshape(ROWS, STATE)
    leaving = bound_ref[:, SLICE:, :].reshape(ROWS, STATE)
    u = dot_nt(wide(leaving), cat([b, b], 1)) * spread_rows(rows_ref[0, 32:40, :])
    out_ref[...] = (dx_ref[...] + u).astype(BF16)
    z = dot_nt(wide(entering), cat([c, c], 1))
    pend[step, :HEADS_HERE, :] = rows_ref[0, 24 : 24 + HEADS_HERE, :] * head_sums(z * y)
    pend[step, HEADS_HERE:, :] = head_sums(x * u)

    @pl.when(step == CHUNKS - 1)
    def _():
        sums = dot_nn(
            cat(
                [cat(list(split3(pend[k])), 1) for k in range(CHUNKS)]
                + [cat(list(split3(pad_heads(head_sums(entering * leaving)))), 1)],
                0,
            ),
            suffix_and_all(),
        )
        whole = jnp.exp(jnp.zeros((HEADS_HERE, SPAN), F32))
        last = rows_ref[0, 24 : 24 + HEADS_HERE, SPAN - 1 : SPAN]
        whole = whole * last
        through = sums[8 * CHUNKS : 8 * CHUNKS + HEADS_HERE, SPAN:] * whole
        after = through
        for k in reversed(range(CHUNKS)):
            here = slice(k * SPAN, (k + 1) * SPAN)
            mine = sums[8 * k : 8 * k + 8, :]
            dl_ref[:, here] = dlp_ref[:, here] + after + mine[:HEADS_HERE, :SPAN]
            after = after + mine[:HEADS_HERE, SPAN:]
        before = jnp.zeros((HEADS_HERE, SPAN), F32)
        for k in range(CHUNKS):
            here = slice(k * SPAN, (k + 1) * SPAN)
            mine = sums[8 * k : 8 * k + 8, :]
            before = before + mine[HEADS_HERE:, SPAN:]
            dl_ref[:, here] = dl_ref[:, here] + before - mine[HEADS_HERE:, :SPAN]


def last_pass(x, y, b, c, bound, rows, dx, dl):
    return pl.pallas_call(
        last_kernel,
        grid=(CHUNKS,),
        in_specs=[
            pl.BlockSpec((ROWS, SPAN), lambda i: (0, i)),
            pl.BlockSpec((ROWS, SPAN), lambda i: (0, i)),
            pl.BlockSpec((SPAN, STATE), lambda i: (i, 0)),
            pl.BlockSpec((SPAN, STATE), lambda i: (i, 0)),
            pl.BlockSpec((SEQ, 2 * SLICE, STATE), lambda i: (0, 0, 0)),
            pl.BlockSpec((1, 40, SPAN), lambda i: (i, 0, 0)),
            pl.BlockSpec((ROWS, SPAN), lambda i: (0, i)),
            pl.BlockSpec((HEADS_HERE, TOK), lambda i: (0, 0)),
        ],
        out_specs=[
            pl.BlockSpec((ROWS, SPAN), lambda i: (0, i)),
            pl.BlockSpec((HEADS_HERE, TOK), lambda i: (0, 0)),
        ],
        out_shape=[
            jax.ShapeDtypeStruct((ROWS, TOK), BF16),
            jax.ShapeDtypeStruct((HEADS_HERE, TOK), F32),
        ],
        scratch_shapes=[pltpu.VMEM((CHUNKS, 8, SPAN), F32)],
        compiler_params=pltpu.CompilerParams(vmem_limit_bytes=VMEM_LIMIT),
        cost_estimate=pl.CostEstimate(flops=1_000_000_000, bytes_accessed=8_000_000, transcendentals=0),
        name="inputs_and_decay",
    )(x, y, b, c, bound, rows, dx, dl)


def merge_kernel(info, own_ref, near_ref, far_ref, side_ref, in_ref, out_ref):
    group = info[0]
    for t, ref in enumerate((in_ref, out_ref)):
        ref[pl.ds(group, HALF, stride=2), :] = own_ref[t] + near_ref[t]
        ref[pl.ds(1 - group, HALF, stride=2), :] = far_ref[t] + side_ref[t]


def merge(info, own, near, far, side):
    spec = pl.BlockSpec(memory_space=pltpu.VMEM)
    return pl.pallas_call(
        merge_kernel,
        in_specs=[pl.BlockSpec(memory_space=pltpu.SMEM)] + [spec] * 4,
        out_specs=[spec] * 2,
        out_shape=[jax.ShapeDtypeStruct((2 * HALF, STATE), F32)] * 2,
        compiler_params=pltpu.CompilerParams(vmem_limit_bytes=VMEM_LIMIT),
        name="merge",
    )(info, own, near, far, side)


def local(inputs, log_decay, in_proj, out_proj, upstream):
    place = lax.axis_index("head")
    chip, core = place // 2, place % 2
    info = jnp.reshape(place // 4, (1,)).astype(jnp.int32)
    order = jnp.bitwise_xor(jnp.arange(4, dtype=jnp.int32), chip)
    keep_ids = 2 * order + core
    send_ids = 2 * order + (1 - core)
    x = jnp.transpose(inputs, (1, 2, 0)).reshape(ROWS, TOK)
    y = jnp.transpose(upstream, (1, 2, 0)).reshape(ROWS, TOK)
    log = jnp.transpose(log_decay)
    b2 = in_proj.reshape(2 * TOK, STATE)
    c2 = out_proj.reshape(2 * TOK, STATE)
    message, b, c, rows = first_pass(info, x, y, b2, c2, log)
    got = lax.all_to_all(message, "seq", 0, 0)
    dxp, dbp, dc, v, following, yw = forward_pass(x, y, b, c, log, rows)
    bound = lax.all_to_all(scan_blocks(got, v), "seq", 0, 0)
    dx, db, dl, xw = backward_pass(x, y, b, c, log, rows, dxp, dbp, v, following)
    send = send_part(send_ids, bound, xw, yw, db, dc)
    other = lax.ppermute(send, "head", [(i, i ^ 1) for i in range(8)])
    parts = keep_part(keep_ids, bound, xw, yw, db, dc, other)
    moved = [
        lax.ppermute(parts[m], "head", [(i, i ^ (2 * m)) for i in range(8)]) for m in (1, 2, 3)
    ]
    grad_x, grad_log = last_pass(x, y, b, c, bound, rows, dx, dl)
    grad_in, grad_out = merge(info, parts[0], *moved)
    return (
        jnp.transpose(grad_x.reshape(HEADS_HERE, WIDTH, TOK), (2, 0, 1)),
        jnp.transpose(grad_log),
        grad_in.reshape(HALF, 2, STATE),
        grad_out.reshape(HALF, 2, STATE),
    )


def solution(mesh):
    in_specs = (
        P("seq", "head", None),
        P("seq", "head"),
        P("seq", None, None),
        P("seq", None, None),
        P("seq", "head", None),
    )
    out_specs = (
        P("seq", "head", None),
        P("seq", "head"),
        P(("seq", "head"), None, None),
        P(("seq", "head"), None, None),
    )
    return jax.shard_map(local, mesh=mesh, in_specs=in_specs, out_specs=out_specs, check_vma=False)
```

```python
import functools

import jax
import jax.numpy as jnp
from jax import lax
from jax.experimental import pallas as pl
from jax.experimental.pallas import tpu as pltpu
from jax.sharding import PartitionSpec as P

HEADS_HERE = 4
WIDTH = 64
STATE = 128
SPAN = 128
TOK = 2048
CHUNKS = TOK // SPAN
ROWS = HEADS_HERE * WIDTH
SEQ = 32
SLICE = ROWS // SEQ
F32 = jnp.float32
BF16 = jnp.bfloat16
FIRST_LIMIT = 60 * 1024 * 1024
PART_LIMIT = 40 * 1024 * 1024
LAST_LIMIT = 40 * 1024 * 1024
CHUNK_LIMIT = 60 * 1024 * 1024
VMEM_LIMIT = 24 * 1024 * 1024


def dot_nn(a, b):
    return lax.dot_general(a, b, (((1,), (0,)), ((), ())), preferred_element_type=F32)


def dot_nt(a, b):
    return lax.dot_general(a, b, (((1,), (1,)), ((), ())), preferred_element_type=F32)


def split2(x):
    hi = x.astype(BF16)
    return hi, (x - hi.astype(F32)).astype(BF16)


def split3(x):
    a = x.astype(BF16)
    rest = x - a.astype(F32)
    b = rest.astype(BF16)
    return a, b, (rest - b.astype(F32)).astype(BF16)


def cat(parts, axis):
    return jnp.concatenate(parts, axis=axis)


def wide(x):
    hi, lo = split2(x)
    return cat([hi, lo], 1)


def iotas(shape):
    return lax.broadcasted_iota(jnp.int32, shape, 0), lax.broadcasted_iota(jnp.int32, shape, 1)


def ones_where(mask):
    return jnp.where(mask, 1.0, 0.0).astype(BF16)


def pad_heads(x):
    return cat([x, jnp.zeros((8 - HEADS_HERE, x.shape[1]), F32)], 0)


def spread_rows(rows):
    return cat(
        [jnp.broadcast_to(rows[h : h + 1, :], (WIDTH, SPAN)) for h in range(HEADS_HERE)], 0
    )


def head_sums(x):
    return cat(
        [
            jnp.sum(x[h * WIDTH : (h + 1) * WIDTH, :], axis=0, keepdims=True)
            for h in range(HEADS_HERE)
        ],
        0,
    )


def by_head(rows):
    lane = lax.broadcasted_iota(jnp.int32, (1, 2 * WIDTH), 1)
    return cat(
        [
            jnp.where(lane < WIDTH, rows[2 * q : 2 * q + 1, :], rows[2 * q + 1 : 2 * q + 2, :])
            for q in range(HEADS_HERE // 2)
        ],
        1,
    )


def to_slices(x, ref, place):
    for a in range(STATE // SLICE):
        for q in range(2):
            ref[2 * a + q, place : place + SLICE, :] = x[
                a * SLICE : (a + 1) * SLICE, q * STATE : (q + 1) * STATE
            ]


def from_slices(ref, place):
    return cat(
        [
            cat([ref[2 * a + q, place : place + SLICE, :] for q in range(2)], 1)
            for a in range(STATE // SLICE)
        ],
        0,
    )


ROWSET = 32


def choose(x, ref, group):
    ref[...] = x.astype(F32)
    return ref[pl.ds(group, SPAN, stride=2), :].astype(BF16)


def row_tables(log_ref, rows_ref, edge_ref, lanes_ref, msg_ref):
    r, c = iotas((SPAN, SPAN))
    tri = cat([ones_where(r <= c), ones_where(r > c), jnp.ones((SPAN, SPAN), BF16)], 1)
    tri = cat([tri] * 3, 0)
    stacked = cat(
        [
            cat(list(split3(pad_heads(log_ref[:, k * SPAN : (k + 1) * SPAN]))), 1)
            for k in range(CHUNKS)
        ],
        0,
    )
    sums = dot_nn(stacked, tri)
    tot = [sums[8 * k : 8 * k + 8, 2 * SPAN :] for k in range(CHUNKS)]
    before = jnp.zeros((8, SPAN), F32)
    for k in range(CHUNKS):
        cin = sums[8 * k : 8 * k + 8, :SPAN]
        rows_ref[k, 0:8, :] = cin
        rows_ref[k, 8:16, :] = jnp.exp(cin)
        rows_ref[k, 16:24, :] = jnp.exp(sums[8 * k : 8 * k + 8, SPAN : 2 * SPAN])
        whole = jnp.exp(tot[k])
        rows_ref[k, 24:32, :] = whole
        edge_ref[k, 0:8, :] = jnp.exp(before + cin)
        lanes_ref[k, 0:1, :] = by_head(whole)
        lanes_ref[k, 1:2, :] = by_head(jnp.exp(before))
        before = before + tot[k]
    after = jnp.zeros((8, SPAN), F32)
    for k in reversed(range(CHUNKS)):
        edge_ref[k, 8:16, :] = jnp.exp(after + sums[8 * k : 8 * k + 8, SPAN : 2 * SPAN])
        lanes_ref[k, 2:3, :] = by_head(jnp.exp(after))
        lanes_ref[k, 3:8, :] = jnp.zeros((5, ROWS), F32)
        after = after + tot[k]
    to_slices(jnp.broadcast_to(by_head(jnp.exp(before)), (STATE, ROWS)), msg_ref, 2 * SLICE)


def first_kernel(
    x_hbm, y_hbm, b_hbm, c_hbm, log_hbm, msg_hbm, rows_hbm, edge_hbm, lanes_hbm, bs_hbm, cs_hbm,
    x_ref, y_ref, b_ref, c_ref, log_ref, msg_ref, rows_ref, edge_ref, lanes_ref, bs_ref, cs_ref, wide_ref,
    get_sem, put_sem
):
    top, low = pl.ds(0, ROWS // 2), pl.ds(ROWS // 2, ROWS // 2)
    gets = [
        pltpu.make_async_copy(src, dst, get_sem.at[n])
        for n, (src, dst) in enumerate(
            (
                (log_hbm, log_ref),
                (b_hbm, b_ref),
                (x_hbm, x_ref),
                (c_hbm, c_ref),
                (y_hbm.at[top, :], y_ref.at[top, :]),
                (y_hbm.at[low, :], y_ref.at[low, :]),
            )
        )
    ]
    for copy in gets:
        copy.start()
    puts = []

    def put(src, dst):
        copy = pltpu.make_async_copy(src, dst, put_sem.at[len(puts)])
        copy.start()
        puts.append(copy)

    def put_message(place):
        part = pl.ds(place, SLICE)
        put(msg_ref.at[:, part, :], msg_hbm.at[:, part, :])

    group = lax.axis_index("head") // 4
    gets[0].wait()
    row_tables(log_ref, rows_ref, edge_ref, lanes_ref, msg_ref)
    put(rows_ref, rows_hbm)
    put(edge_ref, edge_hbm)
    put(lanes_ref, lanes_hbm)
    put_message(2 * SLICE)

    def select(src, dst, base):
        out = []
        for k in range(CHUNKS):
            got = choose(src[2 * k * SPAN : 2 * (k + 1) * SPAN, :], wide_ref.at[base + k], group)
            dst[k * SPAN : (k + 1) * SPAN, :] = got
            turned = got.T
            out.append(cat([turned, turned], 1))
        return out

    def gather(turned, src, row, first, heads):
        total = jnp.zeros((STATE, heads * WIDTH), F32)
        for k in range(CHUNKS):
            scale = edge_ref[k, row : row + 8, :]
            scale = cat(
                [
                    jnp.broadcast_to(scale[h : h + 1, :], (WIDTH, SPAN))
                    for h in range(first, first + heads)
                ],
                0,
            )
            part = src[first * WIDTH : (first + heads) * WIDTH, k * SPAN : (k + 1) * SPAN]
            total = total + dot_nt(turned[k], wide(part.astype(F32) * scale))
        return total

    gets[1].wait()
    turned = select(b_ref, bs_ref, 0)
    put(bs_ref, bs_hbm)
    gets[2].wait()
    to_slices(gather(turned, x_ref, 8, 0, HEADS_HERE), msg_ref, 0)
    put_message(0)
    gets[3].wait()
    turned = select(c_ref, cs_ref, CHUNKS)
    put(cs_ref, cs_hbm)
    halves = []
    for q in range(2):
        gets[4 + q].wait()
        halves.append(gather(turned, y_ref, 0, 2 * q, 2))
    to_slices(cat(halves, 1), msg_ref, SLICE)
    put_message(SLICE)
    for copy in puts:
        copy.wait()


def first_pass(x, y, b, c, log):
    hbm = pl.BlockSpec(memory_space=pltpu.HBM)
    return pl.pallas_call(
        first_kernel,
        in_specs=[hbm] * 5,
        out_specs=[hbm] * 6,
        out_shape=[
            jax.ShapeDtypeStruct((SEQ, 3 * SLICE, STATE), F32),
            jax.ShapeDtypeStruct((CHUNKS, ROWSET, SPAN), F32),
            jax.ShapeDtypeStruct((CHUNKS, 16, SPAN), F32),
            jax.ShapeDtypeStruct((CHUNKS, 8, ROWS), F32),
            jax.ShapeDtypeStruct((TOK, STATE), BF16),
            jax.ShapeDtypeStruct((TOK, STATE), BF16),
        ],
        scratch_shapes=[
            pltpu.VMEM((ROWS, TOK), BF16),
            pltpu.VMEM((ROWS, TOK), BF16),
            pltpu.VMEM((2 * TOK, STATE), BF16),
            pltpu.VMEM((2 * TOK, STATE), BF16),
            pltpu.VMEM((HEADS_HERE, TOK), F32),
            pltpu.VMEM((SEQ, 3 * SLICE, STATE), F32),
            pltpu.VMEM((CHUNKS, ROWSET, SPAN), F32),
            pltpu.VMEM((CHUNKS, 16, SPAN), F32),
            pltpu.VMEM((CHUNKS, 8, ROWS), F32),
            pltpu.VMEM((TOK, STATE), BF16),
            pltpu.VMEM((TOK, STATE), BF16),
            pltpu.VMEM((2 * CHUNKS, 2 * SPAN, STATE), F32),
            pltpu.SemaphoreType.DMA((6,)),
            pltpu.SemaphoreType.DMA((8,)),
        ],
        compiler_params=pltpu.CompilerParams(vmem_limit_bytes=FIRST_LIMIT),
        cost_estimate=pl.CostEstimate(flops=800_000_000, bytes_accessed=6_000_000, transcendentals=20_000),
        name="own_states",
    )(x, y, b, c, log)


def scan_kernel(got_ref, out_ref):
    carry = jnp.zeros((SLICE, STATE), F32)
    for k in range(SEQ):
        out_ref[k, :SLICE, :] = carry
        if k < SEQ - 1:
            carry = carry * got_ref[k, 2 * SLICE :, :] + got_ref[k, :SLICE, :]
    carry = jnp.zeros((SLICE, STATE), F32)
    for k in reversed(range(SEQ)):
        out_ref[k, SLICE:, :] = carry
        if k > 0:
            carry = carry * got_ref[k, 2 * SLICE :, :] + got_ref[k, SLICE : 2 * SLICE, :]


def scan_blocks(got):
    return pl.pallas_call(
        scan_kernel,
        in_specs=[pl.BlockSpec(memory_space=pltpu.VMEM)],
        out_shape=jax.ShapeDtypeStruct((SEQ, 2 * SLICE, STATE), F32),
        compiler_params=pltpu.CompilerParams(vmem_limit_bytes=VMEM_LIMIT),
        name="scan_blocks",
    )(got)


def decays(rows_ref, k, mask):
    cin = rows_ref[k, 0:8, :]
    cols = cin.T
    out = []
    for h in range(HEADS_HERE):
        gap = jnp.broadcast_to(cin[h : h + 1, :], (SPAN, SPAN)) - jnp.broadcast_to(
            cols[:, h : h + 1], (SPAN, SPAN)
        )
        out.append(jnp.exp(jnp.where(mask, gap, -1e30)))
    return out


def crosses(xt, y):
    zero = jnp.zeros((WIDTH, SPAN), BF16)
    out = []
    for q in range(HEADS_HERE // 2):
        top = y[2 * q * WIDTH : (2 * q + 1) * WIDTH, :]
        low = y[(2 * q + 1) * WIDTH : (2 * q + 2) * WIDTH, :]
        both = cat([cat([top, zero], 1), cat([zero, low], 1)], 0)
        pair = dot_nn(xt[:, 2 * q * WIDTH : 2 * (q + 1) * WIDTH], both)
        out += [pair[:, :SPAN], pair[:, SPAN:]]
    return out


def inter(near_hi, near_lo, state):
    hi, lo = split2(state)
    return dot_nn(cat([hi, hi, lo], 1), cat([near_hi, near_lo, near_hi], 0))


PER2 = 8


def ascend_kernel(x_ref, y_ref, b_ref, c_ref, rows_ref, lanes_ref, db_ref, dc_ref, s_ref, state):
    @pl.when(pl.program_id(0) == 0)
    def _():
        state[...] = jnp.zeros((STATE, ROWS), F32)

    r, l = iotas((SPAN, SPAN))
    mask = l >= r
    own = state[...]
    for k in range(PER2):
        here = slice(k * SPAN, (k + 1) * SPAN)
        x = x_ref[:, here]
        bt, ct = b_ref[here, :].T, c_ref[here, :].T
        twice = cat([bt, bt], 1)
        total = jnp.zeros((SPAN, SPAN), F32)
        for cross, decay in zip(crosses(x.T, y_ref[:, here]), decays(rows_ref, k, mask)):
            total = total + cross * decay
        hi, lo = split2(total)
        db_ref[:, here] = dot_nt(cat([ct, ct], 1), cat([hi, lo], 1))
        yhi, ylo = split2(y_ref[:, here].astype(F32) * spread_rows(rows_ref[k, 8:16, :]))
        dc_ref[:, here] = dot_nn(twice, cat([hi, lo], 0)) + inter(yhi, ylo, own)
        s_ref[k * STATE : (k + 1) * STATE, :] = own
        own = own * lanes_ref[k, 0:1, :] + dot_nt(
            twice, wide(x.astype(F32) * spread_rows(rows_ref[k, 16:24, :]))
        )
    state[...] = own


def chunk_specs(per, order):
    return [
        pl.BlockSpec((ROWS, per * SPAN), lambda i: (0, order(i))),
        pl.BlockSpec((ROWS, per * SPAN), lambda i: (0, order(i))),
        pl.BlockSpec((per * SPAN, STATE), lambda i: (order(i), 0)),
        pl.BlockSpec((per * SPAN, STATE), lambda i: (order(i), 0)),
        pl.BlockSpec((per, ROWSET, SPAN), lambda i: (order(i), 0, 0)),
        pl.BlockSpec((per, 8, ROWS), lambda i: (order(i), 0, 0)),
    ]


def ascend(x, y, b, c, rows, lanes):
    tokens = pl.BlockSpec((STATE, PER2 * SPAN), lambda i: (0, i))
    return pl.pallas_call(
        ascend_kernel,
        grid=(CHUNKS // PER2,),
        in_specs=chunk_specs(PER2, lambda i: i),
        out_specs=[
            tokens,
            tokens,
            pl.BlockSpec((PER2 * STATE, ROWS), lambda i: (i, 0)),
        ],
        out_shape=[jax.ShapeDtypeStruct((STATE, TOK), F32)] * 2
        + [
            jax.ShapeDtypeStruct((CHUNKS * STATE, ROWS), F32),
        ],
        scratch_shapes=[pltpu.VMEM((STATE, ROWS), F32)],
        compiler_params=pltpu.CompilerParams(vmem_limit_bytes=CHUNK_LIMIT),
        cost_estimate=pl.CostEstimate(flops=3_000_000_000, bytes_accessed=8_000_000, transcendentals=1_000_000),
        name="chunks_ascending",
    )(x, y, b, c, rows, lanes)


PER3 = 8


def descend_kernel(x_ref, y_ref, c_ref, rows_ref, lanes_ref, dbp_ref, db_ref, d_ref, grad):
    @pl.when(pl.program_id(0) == 0)
    def _():
        grad[...] = jnp.zeros((STATE, ROWS), F32)

    back = grad[...]
    for k in reversed(range(PER3)):
        here = slice(k * SPAN, (k + 1) * SPAN)
        xhi, xlo = split2(x_ref[:, here].astype(F32) * spread_rows(rows_ref[k, 16:24, :]))
        db_ref[:, here] = dbp_ref[:, here] + inter(xhi, xlo, back)
        d_ref[k * STATE : (k + 1) * STATE, :] = back
        ct = c_ref[here, :].T
        back = back * lanes_ref[k, 0:1, :] + dot_nt(
            cat([ct, ct], 1), wide(y_ref[:, here].astype(F32) * spread_rows(rows_ref[k, 8:16, :]))
        )
    grad[...] = back


def descend(x, y, c, rows, lanes, dbp):
    steps = CHUNKS // PER3
    order = lambda i: steps - 1 - i
    specs = chunk_specs(PER3, order)
    tokens = pl.BlockSpec((STATE, PER3 * SPAN), lambda i: (0, order(i)))
    states = pl.BlockSpec((PER3 * STATE, ROWS), lambda i: (order(i), 0))
    return pl.pallas_call(
        descend_kernel,
        grid=(steps,),
        in_specs=specs[:2] + specs[3:] + [tokens],
        out_specs=[tokens, states],
        out_shape=[
            jax.ShapeDtypeStruct((STATE, TOK), F32),
            jax.ShapeDtypeStruct((CHUNKS * STATE, ROWS), F32),
        ],
        scratch_shapes=[pltpu.VMEM((STATE, ROWS), F32)],
        compiler_params=pltpu.CompilerParams(vmem_limit_bytes=CHUNK_LIMIT),
        cost_estimate=pl.CostEstimate(flops=3_000_000_000, bytes_accessed=8_000_000, transcendentals=0),
        name="chunks_descending",
    )(x, y, c, rows, lanes, dbp)


HALF = 256


def part_kernel(
    side, bound_ref, edge_hbm, x_hbm, y_hbm, db_hbm, dc_hbm, out_hbm,
    edge_ref, x_ref, y_ref, both_ref, out_ref, get_sem, put_sem
):
    place = lax.axis_index("head")
    chip, core = place // 2, place % 2
    gets = []
    for i in range(4):
        block = 2 * jnp.bitwise_xor(chip, i) + jnp.bitwise_xor(core, side)
        cols = pl.ds(pl.multiple_of(block * HALF, HALF), HALF)
        gets.append(
            [
                pltpu.make_async_copy(
                    edge_hbm.at[pl.ds(2 * block, 2)], edge_ref.at[i], get_sem.at[i, 0]
                ),
                pltpu.make_async_copy(x_hbm.at[:, cols], x_ref.at[i], get_sem.at[i, 1]),
                pltpu.make_async_copy(y_hbm.at[:, cols], y_ref.at[i], get_sem.at[i, 2]),
                pltpu.make_async_copy(db_hbm.at[:, cols], both_ref.at[i, 0], get_sem.at[i, 3]),
                pltpu.make_async_copy(dc_hbm.at[:, cols], both_ref.at[i, 1], get_sem.at[i, 4]),
            ]
        )
        for copy in gets[i]:
            copy.start()
    edges = [split2(from_slices(bound_ref, place)) for place in (SLICE, 0)]
    stacks = [cat(list(edge), 0) for edge in edges]
    puts = []
    for i in range(4):
        for copy in gets[i]:
            copy.wait()
        for t, (row, src) in enumerate(((8, x_ref), (0, y_ref))):
            scale = cat(
                [spread_rows(edge_ref[i, k, row : row + 8, :]) for k in range(HALF // SPAN)], 1
            )
            near_hi, near_lo = split2(src[i].astype(F32) * scale)
            first = dot_nn(stacks[t], near_hi)
            out_ref[i, t] = both_ref[i, t] + (
                first[:STATE] + (first[STATE:] + dot_nn(edges[t][0], near_lo))
            )
        copy = pltpu.make_async_copy(out_ref.at[i], out_hbm.at[i], put_sem.at[i])
        copy.start()
        puts.append(copy)
    for copy in puts:
        copy.wait()


def part_pass(name, side, bound, edge, x, y, db, dc):
    hbm = pl.BlockSpec(memory_space=pltpu.HBM)
    return pl.pallas_call(
        functools.partial(part_kernel, side),
        in_specs=[pl.BlockSpec(memory_space=pltpu.VMEM)] + [hbm] * 5,
        out_specs=hbm,
        out_shape=jax.ShapeDtypeStruct((4, 2, STATE, HALF), F32),
        scratch_shapes=[
            pltpu.VMEM((4, 2, 16, SPAN), F32),
            pltpu.VMEM((4, ROWS, HALF), BF16),
            pltpu.VMEM((4, ROWS, HALF), BF16),
            pltpu.VMEM((4, 2, STATE, HALF), F32),
            pltpu.VMEM((4, 2, STATE, HALF), F32),
            pltpu.SemaphoreType.DMA((4, 5)),
            pltpu.SemaphoreType.DMA((4,)),
        ],
        compiler_params=pltpu.CompilerParams(vmem_limit_bytes=PART_LIMIT),
        cost_estimate=pl.CostEstimate(flops=500_000_000, bytes_accessed=3_000_000, transcendentals=0),
        name=name,
    )(bound, edge, x, y, db, dc)


def sum_kernel(kept_ref, got_ref, *outs):
    for m in range(4):
        outs[m][...] = kept_ref[m] + got_ref[m]


def sum_pass(kept, got):
    vmem = pl.BlockSpec(memory_space=pltpu.VMEM)
    return pl.pallas_call(
        sum_kernel,
        in_specs=[vmem, vmem],
        out_specs=[vmem] * 4,
        out_shape=[jax.ShapeDtypeStruct((2, STATE, HALF), F32)] * 4,
        compiler_params=pltpu.CompilerParams(vmem_limit_bytes=VMEM_LIMIT),
        name="sum_cores",
    )(kept, got)


PER5 = 4


def last_kernel(x_ref, y_ref, b_ref, c_ref, rows_ref, lanes_ref, bound_ref, s_ref, d_ref, dx_ref, dl_ref):
    entering = from_slices(bound_ref, 0)
    leaving = from_slices(bound_ref, SLICE)
    r, l = iotas((SPAN, SPAN))
    mask = l >= r
    later = cat([ones_where(r >= l)] * 3, 0)
    every = jnp.ones((3 * (SPAN + ROWS), SPAN), BF16)
    owner_row, owner_lane = iotas((HEADS_HERE, ROWS))
    owned = owner_lane // WIDTH == owner_row
    for k in range(PER5):
        here = slice(k * SPAN, (k + 1) * SPAN)
        states = slice(k * STATE, (k + 1) * STATE)
        x, y, b, c = x_ref[:, here], y_ref[:, here], b_ref[here, :], c_ref[here, :]
        scores = dot_nt(b, c)
        s = s_ref[states, :] + lanes_ref[k, 1:2, :] * entering
        d = d_ref[states, :] + lanes_ref[k, 2:3, :] * leaving
        dhi, dlo = split2(d)
        shi, slo = split2(s)
        u = dot_nt(cat([dhi.T, dlo.T], 1), cat([b, b], 1)) * spread_rows(rows_ref[k, 16:24, :])
        z = dot_nt(cat([shi.T, slo.T], 1), cat([c, c], 1))
        row, inner = [], []
        for h, (cross, decay) in enumerate(zip(crosses(x.T, y), decays(rows_ref, k, mask))):
            weight = scores * decay
            yh = y[h * WIDTH : (h + 1) * WIDTH, :]
            inner.append(dot_nt(cat([yh, yh], 1), wide(weight)))
            row.append(jnp.sum(weight * cross, axis=0, keepdims=True))
        dx = cat(inner, 0) + u
        dx_ref[:, here] = dx.astype(BF16)
        xf = x.astype(F32)
        pending = (
            cat(row, 0)
            + rows_ref[k, 8 : 8 + HEADS_HERE, :] * head_sums(z * y.astype(F32))
            - head_sums(xf * dx)
        )
        meet = jnp.where(owned, jnp.sum(s * d, axis=0, keepdims=True), 0.0) * cat(
            [rows_ref[k, 24 : 24 + HEADS_HERE, :]] * 2, 1
        )
        through = cat([head_sums(xf * u), meet], 1)
        dl_ref[:, here] = dot_nn(cat(list(split3(pending)), 1), later) + dot_nn(
            cat(list(split3(through)), 1), every
        )


def last_pass(x, y, b, c, rows, lanes, bound, s, d):
    states = pl.BlockSpec((PER5 * STATE, ROWS), lambda i: (i, 0))
    return pl.pallas_call(
        last_kernel,
        grid=(CHUNKS // PER5,),
        in_specs=chunk_specs(PER5, lambda i: i)
        + [
            pl.BlockSpec((SEQ, 2 * SLICE, STATE), lambda i: (0, 0, 0)),
            states,
            states,
        ],
        out_specs=[
            pl.BlockSpec((ROWS, PER5 * SPAN), lambda i: (0, i)),
            pl.BlockSpec((HEADS_HERE, PER5 * SPAN), lambda i: (0, i)),
        ],
        out_shape=[
            jax.ShapeDtypeStruct((ROWS, TOK), BF16),
            jax.ShapeDtypeStruct((HEADS_HERE, TOK), F32),
        ],
        compiler_params=pltpu.CompilerParams(vmem_limit_bytes=LAST_LIMIT),
        cost_estimate=pl.CostEstimate(flops=6_000_000_000, bytes_accessed=12_000_000, transcendentals=1_000_000),
        name="inputs_and_decay",
    )(x, y, b, c, rows, lanes, bound, s, d)


def merge_kernel(own_ref, near_ref, far_ref, side_ref, in_ref, out_ref):
    group = lax.axis_index("head") // 4
    for t, ref in enumerate((in_ref, out_ref)):
        ref[pl.ds(group, HALF, stride=2), :] = (own_ref[t] + near_ref[t]).T
        ref[pl.ds(1 - group, HALF, stride=2), :] = (far_ref[t] + side_ref[t]).T


def merge(own, near, far, side):
    spec = pl.BlockSpec(memory_space=pltpu.VMEM)
    return pl.pallas_call(
        merge_kernel,
        in_specs=[spec] * 4,
        out_specs=[spec] * 2,
        out_shape=[jax.ShapeDtypeStruct((2 * HALF, STATE), F32)] * 2,
        compiler_params=pltpu.CompilerParams(vmem_limit_bytes=VMEM_LIMIT),
        name="merge",
    )(own, near, far, side)


def local(inputs, log_decay, in_proj, out_proj, upstream):
    x = jnp.transpose(inputs, (1, 2, 0)).reshape(ROWS, TOK)
    y = jnp.transpose(upstream, (1, 2, 0)).reshape(ROWS, TOK)
    log = jnp.transpose(log_decay)
    b2 = in_proj.reshape(2 * TOK, STATE)
    c2 = out_proj.reshape(2 * TOK, STATE)
    message, rows, edge, lanes, b, c = first_pass(x, y, b2, c2, log)
    got = lax.all_to_all(message, "seq", 0, 0)
    dbp, dc, s = ascend(x, y, b, c, rows, lanes)
    got, dbp = lax.optimization_barrier((got, dbp))
    bound = lax.all_to_all(scan_blocks(got), "seq", 0, 0)
    db, d = descend(x, y, c, rows, lanes, dbp)
    sent = part_pass("projections_send", 1, bound, edge, x, y, db, dc)
    other = lax.ppermute(sent, "head", [(i, i ^ 1) for i in range(8)])
    kept = part_pass("projections_keep", 0, bound, edge, x, y, db, dc)
    parts = sum_pass(kept, other)
    moved = [
        lax.ppermute(parts[m], "head", [(i, i ^ (2 * m)) for i in range(8)]) for m in (1, 2, 3)
    ]
    grad_x, grad_log = last_pass(x, y, b, c, rows, lanes, bound, s, d)
    grad_in, grad_out = merge(parts[0], *moved)
    return (
        jnp.transpose(grad_x.reshape(HEADS_HERE, WIDTH, TOK), (2, 0, 1)),
        jnp.transpose(grad_log),
        grad_in.reshape(HALF, 2, STATE),
        grad_out.reshape(HALF, 2, STATE),
    )


def solution(mesh):
    in_specs = (
        P("seq", "head", None),
        P("seq", "head"),
        P("seq", None, None),
        P("seq", None, None),
        P("seq", "head", None),
    )
    out_specs = (
        P("seq", "head", None),
        P("seq", "head"),
        P(("seq", "head"), None, None),
        P(("seq", "head"), None, None),
    )
    return jax.shard_map(local, mesh=mesh, in_specs=in_specs, out_specs=out_specs, check_vma=False)
```

```python
import functools

import jax
import jax.numpy as jnp
from jax import lax
from jax.experimental import pallas as pl
from jax.experimental.pallas import tpu as pltpu
from jax.sharding import PartitionSpec as P

HEADS_HERE = 4
WIDTH = 64
STATE = 128
SPAN = 128
TOK = 2048
CHUNKS = TOK // SPAN
ROWS = HEADS_HERE * WIDTH
SEQ = 32
SLICE = ROWS // SEQ
F32 = jnp.float32
BF16 = jnp.bfloat16
FIRST_LIMIT = 60 * 1024 * 1024
PART_LIMIT = 40 * 1024 * 1024
LAST_LIMIT = 40 * 1024 * 1024
CHUNK_LIMIT = 60 * 1024 * 1024
DOWN_LIMIT = 60 * 1024 * 1024
VMEM_LIMIT = 24 * 1024 * 1024


def dot_nn(a, b):
    return lax.dot_general(a, b, (((1,), (0,)), ((), ())), preferred_element_type=F32)


def dot_nt(a, b):
    return lax.dot_general(a, b, (((1,), (1,)), ((), ())), preferred_element_type=F32)


def split2(x):
    hi = x.astype(BF16)
    return hi, (x - hi.astype(F32)).astype(BF16)


def split3(x):
    a = x.astype(BF16)
    rest = x - a.astype(F32)
    b = rest.astype(BF16)
    return a, b, (rest - b.astype(F32)).astype(BF16)


def cat(parts, axis):
    return jnp.concatenate(parts, axis=axis)


def wide(x):
    hi, lo = split2(x)
    return cat([hi, lo], 1)


def iotas(shape):
    return lax.broadcasted_iota(jnp.int32, shape, 0), lax.broadcasted_iota(jnp.int32, shape, 1)


def ones_where(mask):
    return jnp.where(mask, 1.0, 0.0).astype(BF16)


def pad_heads(x):
    return cat([x, jnp.zeros((8 - HEADS_HERE, x.shape[1]), F32)], 0)


def spread_rows(rows):
    return cat(
        [jnp.broadcast_to(rows[h : h + 1, :], (WIDTH, SPAN)) for h in range(HEADS_HERE)], 0
    )


def head_sums(x):
    return cat(
        [
            jnp.sum(x[h * WIDTH : (h + 1) * WIDTH, :], axis=0, keepdims=True)
            for h in range(HEADS_HERE)
        ],
        0,
    )


def by_head(rows):
    lane = lax.broadcasted_iota(jnp.int32, (1, 2 * WIDTH), 1)
    return cat(
        [
            jnp.where(lane < WIDTH, rows[2 * q : 2 * q + 1, :], rows[2 * q + 1 : 2 * q + 2, :])
            for q in range(HEADS_HERE // 2)
        ],
        1,
    )


def to_slices(x, ref, place):
    for a in range(STATE // SLICE):
        for q in range(2):
            ref[2 * a + q, place : place + SLICE, :] = x[
                a * SLICE : (a + 1) * SLICE, q * STATE : (q + 1) * STATE
            ]


def from_slices(ref, place):
    return cat(
        [
            cat([ref[2 * a + q, place : place + SLICE, :] for q in range(2)], 1)
            for a in range(STATE // SLICE)
        ],
        0,
    )


ROWSET = 32


def choose(x, ref, group):
    ref[...] = x.astype(F32)
    return ref[pl.ds(group, SPAN, stride=2), :].astype(BF16)


def row_tables(log_ref, rows_ref, edge_ref, lanes_ref, msg_ref):
    r, c = iotas((SPAN, SPAN))
    tri = cat([ones_where(r <= c), ones_where(r > c), jnp.ones((SPAN, SPAN), BF16)], 1)
    tri = cat([tri] * 3, 0)
    stacked = cat(
        [
            cat(list(split3(pad_heads(log_ref[:, k * SPAN : (k + 1) * SPAN]))), 1)
            for k in range(CHUNKS)
        ],
        0,
    )
    sums = dot_nn(stacked, tri)
    tot = [sums[8 * k : 8 * k + 8, 2 * SPAN :] for k in range(CHUNKS)]
    before = jnp.zeros((8, SPAN), F32)
    for k in range(CHUNKS):
        cin = sums[8 * k : 8 * k + 8, :SPAN]
        rows_ref[k, 0:8, :] = cin
        rows_ref[k, 8:16, :] = jnp.exp(cin)
        rows_ref[k, 16:24, :] = jnp.exp(sums[8 * k : 8 * k + 8, SPAN : 2 * SPAN])
        whole = jnp.exp(tot[k])
        rows_ref[k, 24:32, :] = whole
        edge_ref[k, :HEADS_HERE, :] = jnp.exp(before + cin)[:HEADS_HERE]
        lanes_ref[k, 0:1, :] = by_head(whole)
        lanes_ref[k, 1:2, :] = by_head(jnp.exp(before))
        before = before + tot[k]
    after = jnp.zeros((8, SPAN), F32)
    for k in reversed(range(CHUNKS)):
        edge_ref[k, HEADS_HERE:, :] = jnp.exp(after + sums[8 * k : 8 * k + 8, SPAN : 2 * SPAN])[
            :HEADS_HERE
        ]
        lanes_ref[k, 2:3, :] = by_head(jnp.exp(after))
        lanes_ref[k, 3:8, :] = jnp.zeros((5, ROWS), F32)
        after = after + tot[k]
    to_slices(jnp.broadcast_to(by_head(jnp.exp(before)), (STATE, ROWS)), msg_ref, 2 * SLICE)


def first_kernel(
    x_hbm, y_hbm, b_hbm, c_hbm, log_hbm, msg_hbm, rows_hbm, edge_hbm, lanes_hbm, bs_hbm, cs_hbm,
    x_ref, y_ref, b_ref, c_ref, log_ref, msg_ref, rows_ref, edge_ref, lanes_ref, bs_ref, cs_ref, wide_ref,
    get_sem, put_sem
):
    gets = [pltpu.make_async_copy(log_hbm, log_ref, get_sem.at[0])]
    for q in range(2):
        rows, cols = pl.ds(q * TOK, TOK), pl.ds(q * TOK // 2, TOK // 2)
        for src, dst, part in (
            (b_hbm, b_ref, (rows, slice(None))),
            (x_hbm, x_ref, (slice(None), cols)),
            (c_hbm, c_ref, (rows, slice(None))),
            (y_hbm, y_ref, (slice(None), cols)),
        ):
            gets.append(
                pltpu.make_async_copy(src.at[part], dst.at[part], get_sem.at[len(gets)])
            )
    for copy in gets:
        copy.start()
    puts = []

    def put(src, dst):
        copy = pltpu.make_async_copy(src, dst, put_sem.at[len(puts)])
        copy.start()
        puts.append(copy)

    def put_message(place):
        part = pl.ds(place, SLICE)
        put(msg_ref.at[:, part, :], msg_hbm.at[:, part, :])

    group = lax.axis_index("head") // 4
    gets[0].wait()
    row_tables(log_ref, rows_ref, edge_ref, lanes_ref, msg_ref)
    put(rows_ref, rows_hbm)
    put(edge_ref, edge_hbm)
    put(lanes_ref, lanes_hbm)
    put_message(2 * SLICE)

    def gather(total, base, k, pairs_ref, chosen_ref, src, row):
        got = choose(pairs_ref[2 * k * SPAN : 2 * (k + 1) * SPAN, :], wide_ref.at[base + k], group)
        chosen_ref[k * SPAN : (k + 1) * SPAN, :] = got
        turned = got.T
        near = src[:, k * SPAN : (k + 1) * SPAN].astype(F32) * spread_rows(
            edge_ref[k, row : row + HEADS_HERE, :]
        )
        return total + dot_nt(cat([turned, turned], 1), wide(near))

    own = jnp.zeros((STATE, ROWS), F32)
    back = jnp.zeros((STATE, ROWS), F32)
    for q in range(2):
        chunks = range(q * CHUNKS // 2, (q + 1) * CHUNKS // 2)
        gets[4 * q + 1].wait()
        gets[4 * q + 2].wait()
        for k in chunks:
            own = gather(own, 0, k, b_ref, bs_ref, x_ref, HEADS_HERE)
        if q == 1:
            put(bs_ref, bs_hbm)
            to_slices(own, msg_ref, 0)
            put_message(0)
        gets[4 * q + 3].wait()
        gets[4 * q + 4].wait()
        for k in chunks:
            back = gather(back, CHUNKS, k, c_ref, cs_ref, y_ref, 0)
    put(cs_ref, cs_hbm)
    to_slices(back, msg_ref, SLICE)
    put_message(SLICE)
    for copy in puts:
        copy.wait()


def first_pass(x, y, b, c, log):
    hbm = pl.BlockSpec(memory_space=pltpu.HBM)
    return pl.pallas_call(
        first_kernel,
        in_specs=[hbm] * 5,
        out_specs=[hbm] * 6,
        out_shape=[
            jax.ShapeDtypeStruct((SEQ, 3 * SLICE, STATE), F32),
            jax.ShapeDtypeStruct((CHUNKS, ROWSET, SPAN), F32),
            jax.ShapeDtypeStruct((CHUNKS, 8, SPAN), F32),
            jax.ShapeDtypeStruct((CHUNKS, 8, ROWS), F32),
            jax.ShapeDtypeStruct((TOK, STATE), BF16),
            jax.ShapeDtypeStruct((TOK, STATE), BF16),
        ],
        scratch_shapes=[
            pltpu.VMEM((ROWS, TOK), BF16),
            pltpu.VMEM((ROWS, TOK), BF16),
            pltpu.VMEM((2 * TOK, STATE), BF16),
            pltpu.VMEM((2 * TOK, STATE), BF16),
            pltpu.VMEM((HEADS_HERE, TOK), F32),
            pltpu.VMEM((SEQ, 3 * SLICE, STATE), F32),
            pltpu.VMEM((CHUNKS, ROWSET, SPAN), F32),
            pltpu.VMEM((CHUNKS, 8, SPAN), F32),
            pltpu.VMEM((CHUNKS, 8, ROWS), F32),
            pltpu.VMEM((TOK, STATE), BF16),
            pltpu.VMEM((TOK, STATE), BF16),
            pltpu.VMEM((2 * CHUNKS, 2 * SPAN, STATE), F32),
            pltpu.SemaphoreType.DMA((9,)),
            pltpu.SemaphoreType.DMA((8,)),
        ],
        compiler_params=pltpu.CompilerParams(vmem_limit_bytes=FIRST_LIMIT),
        cost_estimate=pl.CostEstimate(flops=800_000_000, bytes_accessed=6_000_000, transcendentals=20_000),
        name="own_states",
    )(x, y, b, c, log)


def scan_kernel(got_ref, out_ref):
    carry = jnp.zeros((SLICE, STATE), F32)
    for k in range(SEQ):
        out_ref[k, :SLICE, :] = carry
        if k < SEQ - 1:
            carry = carry * got_ref[k, 2 * SLICE :, :] + got_ref[k, :SLICE, :]
    carry = jnp.zeros((SLICE, STATE), F32)
    for k in reversed(range(SEQ)):
        out_ref[k, SLICE:, :] = carry
        if k > 0:
            carry = carry * got_ref[k, 2 * SLICE :, :] + got_ref[k, SLICE : 2 * SLICE, :]


def scan_blocks(got):
    return pl.pallas_call(
        scan_kernel,
        in_specs=[pl.BlockSpec(memory_space=pltpu.VMEM)],
        out_shape=jax.ShapeDtypeStruct((SEQ, 2 * SLICE, STATE), F32),
        compiler_params=pltpu.CompilerParams(vmem_limit_bytes=VMEM_LIMIT),
        name="scan_blocks",
    )(got)


def decays(rows_ref, k, mask):
    cin = rows_ref[k, 0:8, :]
    cols = cin.T
    out = []
    for h in range(HEADS_HERE):
        gap = jnp.broadcast_to(cin[h : h + 1, :], (SPAN, SPAN)) - jnp.broadcast_to(
            cols[:, h : h + 1], (SPAN, SPAN)
        )
        out.append(jnp.exp(jnp.where(mask, gap, -1e30)))
    return out


def crosses(xt, y):
    zero = jnp.zeros((WIDTH, SPAN), BF16)
    out = []
    for q in range(HEADS_HERE // 2):
        top = y[2 * q * WIDTH : (2 * q + 1) * WIDTH, :]
        low = y[(2 * q + 1) * WIDTH : (2 * q + 2) * WIDTH, :]
        both = cat([cat([top, zero], 1), cat([zero, low], 1)], 0)
        pair = dot_nn(xt[:, 2 * q * WIDTH : 2 * (q + 1) * WIDTH], both)
        out += [pair[:, :SPAN], pair[:, SPAN:]]
    return out


def inter(near_hi, near_lo, state):
    hi, lo = split2(state)
    return dot_nn(cat([hi, hi, lo], 1), cat([near_hi, near_lo, near_hi], 0))


PER2 = 8


HALF = 256


def by_side(blocks, send_ref, keep_ref):
    second = lax.axis_index("head") % 2 == 1
    for a in range(len(blocks) // 2):
        even, odd = blocks[2 * a], blocks[2 * a + 1]
        send_ref[a] = jnp.where(second, even, odd)
        keep_ref[a] = jnp.where(second, odd, even)


def halves(chunks):
    return [cat([chunks[2 * j], chunks[2 * j + 1]], 1) for j in range(len(chunks) // 2)]


def ascend_kernel(x_ref, y_ref, b_ref, c_ref, rows_ref, lanes_ref, db_ref, send_ref, keep_ref, s_ref, state):
    @pl.when(pl.program_id(0) == 0)
    def _():
        state[...] = jnp.zeros((STATE, ROWS), F32)

    r, l = iotas((SPAN, SPAN))
    mask = l >= r
    own = state[...]
    chunks = []
    for k in range(PER2):
        here = slice(k * SPAN, (k + 1) * SPAN)
        x = x_ref[:, here]
        bt, ct = b_ref[here, :].T, c_ref[here, :].T
        twice = cat([bt, bt], 1)
        total = jnp.zeros((SPAN, SPAN), F32)
        for cross, decay in zip(crosses(x.T, y_ref[:, here]), decays(rows_ref, k, mask)):
            total = total + cross * decay
        hi, lo = split2(total)
        db_ref[:, here] = dot_nt(cat([ct, ct], 1), cat([hi, lo], 1))
        yhi, ylo = split2(y_ref[:, here].astype(F32) * spread_rows(rows_ref[k, 8:16, :]))
        chunks.append(dot_nn(twice, cat([hi, lo], 0)) + inter(yhi, ylo, own))
        s_ref[k * STATE : (k + 1) * STATE, :] = own
        own = own * lanes_ref[k, 0:1, :] + dot_nt(
            twice, wide(x.astype(F32) * spread_rows(rows_ref[k, 16:24, :]))
        )
    state[...] = own
    by_side(halves(chunks), send_ref, keep_ref)


def chunk_specs(per, order):
    return [
        pl.BlockSpec((ROWS, per * SPAN), lambda i: (0, order(i))),
        pl.BlockSpec((ROWS, per * SPAN), lambda i: (0, order(i))),
        pl.BlockSpec((per * SPAN, STATE), lambda i: (order(i), 0)),
        pl.BlockSpec((per * SPAN, STATE), lambda i: (order(i), 0)),
        pl.BlockSpec((per, ROWSET, SPAN), lambda i: (order(i), 0, 0)),
        pl.BlockSpec((per, 8, ROWS), lambda i: (order(i), 0, 0)),
    ]


def side_specs(per, order):
    return [pl.BlockSpec((per // 4, STATE, HALF), lambda i: (order(i), 0, 0))] * 2


def ascend(x, y, b, c, rows, lanes):
    return pl.pallas_call(
        ascend_kernel,
        grid=(CHUNKS // PER2,),
        in_specs=chunk_specs(PER2, lambda i: i),
        out_specs=[pl.BlockSpec((STATE, PER2 * SPAN), lambda i: (0, i))]
        + side_specs(PER2, lambda i: i)
        + [pl.BlockSpec((PER2 * STATE, ROWS), lambda i: (i, 0))],
        out_shape=[jax.ShapeDtypeStruct((STATE, TOK), F32)]
        + [jax.ShapeDtypeStruct((4, STATE, HALF), F32)] * 2
        + [jax.ShapeDtypeStruct((CHUNKS * STATE, ROWS), F32)],
        scratch_shapes=[pltpu.VMEM((STATE, ROWS), F32)],
        compiler_params=pltpu.CompilerParams(vmem_limit_bytes=CHUNK_LIMIT),
        cost_estimate=pl.CostEstimate(flops=3_000_000_000, bytes_accessed=8_000_000, transcendentals=1_000_000),
        name="chunks_ascending",
    )(x, y, b, c, rows, lanes)


PER3 = 8


def descend_kernel(x_ref, y_ref, c_ref, rows_ref, lanes_ref, dbp_ref, send_ref, keep_ref, d_ref, grad):
    @pl.when(pl.program_id(0) == 0)
    def _():
        grad[...] = jnp.zeros((STATE, ROWS), F32)

    back = grad[...]
    chunks = [None] * PER3
    for k in reversed(range(PER3)):
        here = slice(k * SPAN, (k + 1) * SPAN)
        xhi, xlo = split2(x_ref[:, here].astype(F32) * spread_rows(rows_ref[k, 16:24, :]))
        chunks[k] = dbp_ref[:, here] + inter(xhi, xlo, back)
        d_ref[k * STATE : (k + 1) * STATE, :] = back
        ct = c_ref[here, :].T
        back = back * lanes_ref[k, 0:1, :] + dot_nt(
            cat([ct, ct], 1), wide(y_ref[:, here].astype(F32) * spread_rows(rows_ref[k, 8:16, :]))
        )
    grad[...] = back
    by_side(halves(chunks), send_ref, keep_ref)


def descend(x, y, c, rows, lanes, dbp):
    steps = CHUNKS // PER3
    order = lambda i: steps - 1 - i
    specs = chunk_specs(PER3, order)
    tokens = pl.BlockSpec((STATE, PER3 * SPAN), lambda i: (0, order(i)))
    states = pl.BlockSpec((PER3 * STATE, ROWS), lambda i: (order(i), 0))
    return pl.pallas_call(
        descend_kernel,
        grid=(steps,),
        in_specs=specs[:2] + specs[3:] + [tokens],
        out_specs=side_specs(PER3, order) + [states],
        out_shape=[
            jax.ShapeDtypeStruct((4, STATE, HALF), F32),
            jax.ShapeDtypeStruct((4, STATE, HALF), F32),
            jax.ShapeDtypeStruct((CHUNKS * STATE, ROWS), F32),
        ],
        scratch_shapes=[pltpu.VMEM((STATE, ROWS), F32)],
        compiler_params=pltpu.CompilerParams(vmem_limit_bytes=DOWN_LIMIT),
        cost_estimate=pl.CostEstimate(flops=3_000_000_000, bytes_accessed=8_000_000, transcendentals=0),
        name="chunks_descending",
    )(x, y, c, rows, lanes, dbp)


def part_kernel(side, bound_ref, edge_ref, x_ref, y_ref, db_ref, dc_ref, out_ref):
    index = lax.axis_index("head")
    chip, core = index // 2, index % 2
    for t, (place, row, src, held) in enumerate(
        ((SLICE, HEADS_HERE, x_ref, db_ref), (0, 0, y_ref, dc_ref))
    ):
        edge = split2(from_slices(bound_ref, place))
        stack = cat(list(edge), 0)
        for i in range(4):
            to = jnp.bitwise_xor(chip, i)
            block = 2 * to + jnp.bitwise_xor(core, side)
            cols = pl.ds(pl.multiple_of(block * HALF, HALF), HALF)
            scale = cat(
                [spread_rows(edge_ref[2 * block + k, row : row + HEADS_HERE, :]) for k in range(2)], 1
            )
            near_hi, near_lo = split2(src[:, cols].astype(F32) * scale)
            first = dot_nn(stack, near_hi)
            out_ref[i, t] = held[to] + (first[:STATE] + (first[STATE:] + dot_nn(edge[0], near_lo)))


def part_pass(name, side, bound, edge, x, y, db, dc):
    vmem = pl.BlockSpec(memory_space=pltpu.VMEM)
    return pl.pallas_call(
        functools.partial(part_kernel, side),
        in_specs=[vmem] * 6,
        out_specs=vmem,
        out_shape=jax.ShapeDtypeStruct((4, 2, STATE, HALF), F32),
        compiler_params=pltpu.CompilerParams(vmem_limit_bytes=PART_LIMIT),
        cost_estimate=pl.CostEstimate(flops=500_000_000, bytes_accessed=3_000_000, transcendentals=0),
        name=name,
    )(bound, edge, x, y, db, dc)


def sum_kernel(kept_ref, got_ref, *outs):
    for m in range(4):
        outs[m][...] = kept_ref[m] + got_ref[m]


def sum_pass(kept, got):
    vmem = pl.BlockSpec(memory_space=pltpu.VMEM)
    return pl.pallas_call(
        sum_kernel,
        in_specs=[vmem, vmem],
        out_specs=[vmem] * 4,
        out_shape=[jax.ShapeDtypeStruct((2, STATE, HALF), F32)] * 4,
        compiler_params=pltpu.CompilerParams(vmem_limit_bytes=VMEM_LIMIT),
        name="sum_cores",
    )(kept, got)


PER5 = 4


def last_kernel(x_ref, y_ref, b_ref, c_ref, rows_ref, lanes_ref, bound_ref, s_ref, d_ref, dx_ref, dl_ref):
    entering = from_slices(bound_ref, 0)
    leaving = from_slices(bound_ref, SLICE)
    r, l = iotas((SPAN, SPAN))
    mask = l >= r
    later = cat([ones_where(r >= l)] * 3, 0)
    every = jnp.ones((3 * (SPAN + ROWS), SPAN), BF16)
    owner_row, owner_lane = iotas((HEADS_HERE, ROWS))
    owned = owner_lane // WIDTH == owner_row
    for k in range(PER5):
        here = slice(k * SPAN, (k + 1) * SPAN)
        states = slice(k * STATE, (k + 1) * STATE)
        x, y, b, c = x_ref[:, here], y_ref[:, here], b_ref[here, :], c_ref[here, :]
        scores = dot_nt(b, c)
        s = s_ref[states, :] + lanes_ref[k, 1:2, :] * entering
        d = d_ref[states, :] + lanes_ref[k, 2:3, :] * leaving
        dhi, dlo = split2(d)
        shi, slo = split2(s)
        u = dot_nt(cat([dhi.T, dlo.T], 1), cat([b, b], 1)) * spread_rows(rows_ref[k, 16:24, :])
        z = dot_nt(cat([shi.T, slo.T], 1), cat([c, c], 1))
        row, inner = [], []
        for h, (cross, decay) in enumerate(zip(crosses(x.T, y), decays(rows_ref, k, mask))):
            weight = scores * decay
            yh = y[h * WIDTH : (h + 1) * WIDTH, :]
            inner.append(dot_nt(cat([yh, yh], 1), wide(weight)))
            row.append(jnp.sum(weight * cross, axis=0, keepdims=True))
        dx = cat(inner, 0) + u
        dx_ref[:, here] = dx.astype(BF16)
        xf = x.astype(F32)
        pending = (
            cat(row, 0)
            + rows_ref[k, 8 : 8 + HEADS_HERE, :] * head_sums(z * y.astype(F32))
            - head_sums(xf * dx)
        )
        meet = jnp.where(owned, jnp.sum(s * d, axis=0, keepdims=True), 0.0) * cat(
            [rows_ref[k, 24 : 24 + HEADS_HERE, :]] * 2, 1
        )
        through = cat([head_sums(xf * u), meet], 1)
        dl_ref[:, here] = dot_nn(cat(list(split3(pending)), 1), later) + dot_nn(
            cat(list(split3(through)), 1), every
        )


def last_pass(x, y, b, c, rows, lanes, bound, s, d):
    states = pl.BlockSpec((PER5 * STATE, ROWS), lambda i: (i, 0))
    return pl.pallas_call(
        last_kernel,
        grid=(CHUNKS // PER5,),
        in_specs=chunk_specs(PER5, lambda i: i)
        + [
            pl.BlockSpec((SEQ, 2 * SLICE, STATE), lambda i: (0, 0, 0)),
            states,
            states,
        ],
        out_specs=[
            pl.BlockSpec((ROWS, PER5 * SPAN), lambda i: (0, i)),
            pl.BlockSpec((HEADS_HERE, PER5 * SPAN), lambda i: (0, i)),
        ],
        out_shape=[
            jax.ShapeDtypeStruct((ROWS, TOK), BF16),
            jax.ShapeDtypeStruct((HEADS_HERE, TOK), F32),
        ],
        compiler_params=pltpu.CompilerParams(vmem_limit_bytes=LAST_LIMIT),
        cost_estimate=pl.CostEstimate(flops=6_000_000_000, bytes_accessed=12_000_000, transcendentals=1_000_000),
        name="inputs_and_decay",
    )(x, y, b, c, rows, lanes, bound, s, d)


def merge_kernel(own_ref, near_ref, far_ref, side_ref, in_ref, out_ref):
    group = lax.axis_index("head") // 4
    for t, ref in enumerate((in_ref, out_ref)):
        ref[pl.ds(group, HALF, stride=2), :] = (own_ref[t] + near_ref[t]).T
        ref[pl.ds(1 - group, HALF, stride=2), :] = (far_ref[t] + side_ref[t]).T


def merge(own, near, far, side):
    spec = pl.BlockSpec(memory_space=pltpu.VMEM)
    return pl.pallas_call(
        merge_kernel,
        in_specs=[spec] * 4,
        out_specs=[spec] * 2,
        out_shape=[jax.ShapeDtypeStruct((2 * HALF, STATE), F32)] * 2,
        compiler_params=pltpu.CompilerParams(vmem_limit_bytes=VMEM_LIMIT),
        name="merge",
    )(own, near, far, side)


def local(inputs, log_decay, in_proj, out_proj, upstream):
    x = jnp.transpose(inputs, (1, 2, 0)).reshape(ROWS, TOK)
    y = jnp.transpose(upstream, (1, 2, 0)).reshape(ROWS, TOK)
    log = jnp.transpose(log_decay)
    b2 = in_proj.reshape(2 * TOK, STATE)
    c2 = out_proj.reshape(2 * TOK, STATE)
    message, rows, edge, lanes, b, c = first_pass(x, y, b2, c2, log)
    got = lax.all_to_all(message, "seq", 0, 0)
    dbp, dc_send, dc_keep, s = ascend(x, y, b, c, rows, lanes)
    got, dbp = lax.optimization_barrier((got, dbp))
    bound = lax.all_to_all(scan_blocks(got), "seq", 0, 0)
    db_send, db_keep, d = descend(x, y, c, rows, lanes, dbp)
    sent = part_pass("projections_send", 1, bound, edge, x, y, db_send, dc_send)
    other = lax.ppermute(sent, "head", [(i, i ^ 1) for i in range(8)])
    kept = part_pass("projections_keep", 0, bound, edge, x, y, db_keep, dc_keep)
    parts = sum_pass(kept, other)
    moved = [
        lax.ppermute(parts[m], "head", [(i, i ^ (2 * m)) for i in range(8)]) for m in (1, 2, 3)
    ]
    grad_x, grad_log = last_pass(x, y, b, c, rows, lanes, bound, s, d)
    grad_in, grad_out = merge(parts[0], *moved)
    return (
        jnp.transpose(grad_x.reshape(HEADS_HERE, WIDTH, TOK), (2, 0, 1)),
        jnp.transpose(grad_log),
        grad_in.reshape(HALF, 2, STATE),
        grad_out.reshape(HALF, 2, STATE),
    )


def solution(mesh):
    in_specs = (
        P("seq", "head", None),
        P("seq", "head"),
        P("seq", None, None),
        P("seq", None, None),
        P("seq", "head", None),
    )
    out_specs = (
        P("seq", "head", None),
        P("seq", "head"),
        P(("seq", "head"), None, None),
        P(("seq", "head"), None, None),
    )
    return jax.shard_map(local, mesh=mesh, in_specs=in_specs, out_specs=out_specs, check_vma=False)
```

```python
import functools

import jax
import jax.numpy as jnp
from jax import lax
from jax.experimental import pallas as pl
from jax.experimental.pallas import tpu as pltpu
from jax.sharding import PartitionSpec as P

HEADS_HERE = 4
WIDTH = 64
STATE = 128
SPAN = 128
TOK = 2048
CHUNKS = TOK // SPAN
ROWS = HEADS_HERE * WIDTH
SEQ = 32
SLICE = ROWS // SEQ
F32 = jnp.float32
BF16 = jnp.bfloat16
FIRST_LIMIT = 60 * 1024 * 1024
PART_LIMIT = 40 * 1024 * 1024
LAST_LIMIT = 40 * 1024 * 1024
CHUNK_LIMIT = 60 * 1024 * 1024
DOWN_LIMIT = 60 * 1024 * 1024
VMEM_LIMIT = 24 * 1024 * 1024


def dot_nn(a, b):
    return lax.dot_general(a, b, (((1,), (0,)), ((), ())), preferred_element_type=F32)


def dot_nt(a, b):
    return lax.dot_general(a, b, (((1,), (1,)), ((), ())), preferred_element_type=F32)


def split2(x):
    hi = x.astype(BF16)
    return hi, (x - hi.astype(F32)).astype(BF16)


def split3(x):
    a = x.astype(BF16)
    rest = x - a.astype(F32)
    b = rest.astype(BF16)
    return a, b, (rest - b.astype(F32)).astype(BF16)


def cat(parts, axis):
    return jnp.concatenate(parts, axis=axis)


def wide(x):
    hi, lo = split2(x)
    return cat([hi, lo], 1)


def iotas(shape):
    return lax.broadcasted_iota(jnp.int32, shape, 0), lax.broadcasted_iota(jnp.int32, shape, 1)


def ones_where(mask):
    return jnp.where(mask, 1.0, 0.0).astype(BF16)


def pad_heads(x):
    return cat([x, jnp.zeros((8 - HEADS_HERE, x.shape[1]), F32)], 0)


def spread_rows(rows):
    return cat(
        [jnp.broadcast_to(rows[h : h + 1, :], (WIDTH, SPAN)) for h in range(HEADS_HERE)], 0
    )


def head_sums(x):
    return cat(
        [
            jnp.sum(x[h * WIDTH : (h + 1) * WIDTH, :], axis=0, keepdims=True)
            for h in range(HEADS_HERE)
        ],
        0,
    )


def by_head(rows):
    lane = lax.broadcasted_iota(jnp.int32, (1, 2 * WIDTH), 1)
    return cat(
        [
            jnp.where(lane < WIDTH, rows[2 * q : 2 * q + 1, :], rows[2 * q + 1 : 2 * q + 2, :])
            for q in range(HEADS_HERE // 2)
        ],
        1,
    )


def to_slices(x, ref, place):
    for a in range(STATE // SLICE):
        for q in range(2):
            ref[2 * a + q, place : place + SLICE, :] = x[
                a * SLICE : (a + 1) * SLICE, q * STATE : (q + 1) * STATE
            ]


def from_slices(ref, place):
    return cat(
        [
            cat([ref[2 * a + q, place : place + SLICE, :] for q in range(2)], 1)
            for a in range(STATE // SLICE)
        ],
        0,
    )


ROWSET = 32


def choose(x, ref, group):
    ref[...] = x.astype(F32)
    return ref[pl.ds(group, SPAN, stride=2), :].astype(BF16)


def row_tables(log_ref, rows_ref, edge_ref, lanes_ref, msg_ref):
    r, c = iotas((SPAN, SPAN))
    tri = cat([ones_where(r <= c), ones_where(r > c), jnp.ones((SPAN, SPAN), BF16)], 1)
    tri = cat([tri] * 3, 0)
    stacked = cat(
        [
            cat(list(split3(pad_heads(log_ref[:, k * SPAN : (k + 1) * SPAN]))), 1)
            for k in range(CHUNKS)
        ],
        0,
    )
    sums = dot_nn(stacked, tri)
    tot = [sums[8 * k : 8 * k + 8, 2 * SPAN :] for k in range(CHUNKS)]
    before = jnp.zeros((8, SPAN), F32)
    for k in range(CHUNKS):
        cin = sums[8 * k : 8 * k + 8, :SPAN]
        rows_ref[k, 0:8, :] = cin
        rows_ref[k, 8:16, :] = jnp.exp(cin)
        rows_ref[k, 16:24, :] = jnp.exp(sums[8 * k : 8 * k + 8, SPAN : 2 * SPAN])
        whole = jnp.exp(tot[k])
        rows_ref[k, 24:32, :] = whole
        edge_ref[k, :HEADS_HERE, :] = jnp.exp(before + cin)[:HEADS_HERE]
        lanes_ref[k, 0:1, :] = by_head(whole)
        lanes_ref[k, 1:2, :] = by_head(jnp.exp(before))
        before = before + tot[k]
    after = jnp.zeros((8, SPAN), F32)
    for k in reversed(range(CHUNKS)):
        edge_ref[k, HEADS_HERE:, :] = jnp.exp(after + sums[8 * k : 8 * k + 8, SPAN : 2 * SPAN])[
            :HEADS_HERE
        ]
        lanes_ref[k, 2:3, :] = by_head(jnp.exp(after))
        lanes_ref[k, 3:8, :] = jnp.zeros((5, ROWS), F32)
        after = after + tot[k]
    to_slices(jnp.broadcast_to(by_head(jnp.exp(before)), (STATE, ROWS)), msg_ref, 2 * SLICE)


def first_kernel(
    x_hbm, y_hbm, b_hbm, c_hbm, log_hbm, msg_hbm, rows_hbm, edge_hbm, lanes_hbm, bs_hbm, cs_hbm,
    x_ref, y_ref, b_ref, c_ref, log_ref, msg_ref, rows_ref, edge_ref, lanes_ref, bs_ref, cs_ref, wide_ref,
    get_sem, put_sem
):
    gets = [pltpu.make_async_copy(log_hbm, log_ref, get_sem.at[0])]
    for q in range(2):
        rows, cols = pl.ds(q * TOK, TOK), pl.ds(q * TOK // 2, TOK // 2)
        for src, dst, part in (
            (b_hbm, b_ref, (rows, slice(None))),
            (x_hbm, x_ref, (slice(None), cols)),
            (c_hbm, c_ref, (rows, slice(None))),
            (y_hbm, y_ref, (slice(None), cols)),
        ):
            gets.append(
                pltpu.make_async_copy(src.at[part], dst.at[part], get_sem.at[len(gets)])
            )
    for copy in gets:
        copy.start()
    puts = []

    def put(src, dst):
        copy = pltpu.make_async_copy(src, dst, put_sem.at[len(puts)])
        copy.start()
        puts.append(copy)

    def put_message(place):
        part = pl.ds(place, SLICE)
        put(msg_ref.at[:, part, :], msg_hbm.at[:, part, :])

    group = lax.axis_index("head") // 4
    gets[0].wait()
    row_tables(log_ref, rows_ref, edge_ref, lanes_ref, msg_ref)
    put(rows_ref, rows_hbm)
    put(edge_ref, edge_hbm)
    put(lanes_ref, lanes_hbm)
    put_message(2 * SLICE)

    def gather(total, base, k, pairs_ref, chosen_ref, src, row):
        got = choose(pairs_ref[2 * k * SPAN : 2 * (k + 1) * SPAN, :], wide_ref.at[base + k], group)
        chosen_ref[k * SPAN : (k + 1) * SPAN, :] = got
        turned = got.T
        near = src[:, k * SPAN : (k + 1) * SPAN].astype(F32) * spread_rows(
            edge_ref[k, row : row + HEADS_HERE, :]
        )
        return total + dot_nt(cat([turned, turned], 1), wide(near))

    own = jnp.zeros((STATE, ROWS), F32)
    back = jnp.zeros((STATE, ROWS), F32)
    for q in range(2):
        chunks = range(q * CHUNKS // 2, (q + 1) * CHUNKS // 2)
        gets[4 * q + 1].wait()
        gets[4 * q + 2].wait()
        for k in chunks:
            own = gather(own, 0, k, b_ref, bs_ref, x_ref, HEADS_HERE)
        if q == 1:
            put(bs_ref, bs_hbm)
            to_slices(own, msg_ref, 0)
            put_message(0)
        gets[4 * q + 3].wait()
        gets[4 * q + 4].wait()
        for k in chunks:
            back = gather(back, CHUNKS, k, c_ref, cs_ref, y_ref, 0)
    put(cs_ref, cs_hbm)
    to_slices(back, msg_ref, SLICE)
    put_message(SLICE)
    for copy in puts:
        copy.wait()


def first_pass(x, y, b, c, log):
    hbm = pl.BlockSpec(memory_space=pltpu.HBM)
    return pl.pallas_call(
        first_kernel,
        in_specs=[hbm] * 5,
        out_specs=[hbm] * 6,
        out_shape=[
            jax.ShapeDtypeStruct((SEQ, 3 * SLICE, STATE), F32),
            jax.ShapeDtypeStruct((CHUNKS, ROWSET, SPAN), F32),
            jax.ShapeDtypeStruct((CHUNKS, 8, SPAN), F32),
            jax.ShapeDtypeStruct((CHUNKS, 8, ROWS), F32),
            jax.ShapeDtypeStruct((TOK, STATE), BF16),
            jax.ShapeDtypeStruct((TOK, STATE), BF16),
        ],
        scratch_shapes=[
            pltpu.VMEM((ROWS, TOK), BF16),
            pltpu.VMEM((ROWS, TOK), BF16),
            pltpu.VMEM((2 * TOK, STATE), BF16),
            pltpu.VMEM((2 * TOK, STATE), BF16),
            pltpu.VMEM((HEADS_HERE, TOK), F32),
            pltpu.VMEM((SEQ, 3 * SLICE, STATE), F32),
            pltpu.VMEM((CHUNKS, ROWSET, SPAN), F32),
            pltpu.VMEM((CHUNKS, 8, SPAN), F32),
            pltpu.VMEM((CHUNKS, 8, ROWS), F32),
            pltpu.VMEM((TOK, STATE), BF16),
            pltpu.VMEM((TOK, STATE), BF16),
            pltpu.VMEM((2 * CHUNKS, 2 * SPAN, STATE), F32),
            pltpu.SemaphoreType.DMA((9,)),
            pltpu.SemaphoreType.DMA((8,)),
        ],
        compiler_params=pltpu.CompilerParams(vmem_limit_bytes=FIRST_LIMIT),
        cost_estimate=pl.CostEstimate(flops=800_000_000, bytes_accessed=6_000_000, transcendentals=20_000),
        name="own_states",
    )(x, y, b, c, log)


def scan_kernel(got_ref, out_ref):
    carry = jnp.zeros((SLICE, STATE), F32)
    for k in range(SEQ):
        out_ref[k, :SLICE, :] = carry
        if k < SEQ - 1:
            carry = carry * got_ref[k, 2 * SLICE :, :] + got_ref[k, :SLICE, :]
    carry = jnp.zeros((SLICE, STATE), F32)
    for k in reversed(range(SEQ)):
        out_ref[k, SLICE:, :] = carry
        if k > 0:
            carry = carry * got_ref[k, 2 * SLICE :, :] + got_ref[k, SLICE : 2 * SLICE, :]


def scan_blocks(got):
    return pl.pallas_call(
        scan_kernel,
        in_specs=[pl.BlockSpec(memory_space=pltpu.VMEM)],
        out_shape=jax.ShapeDtypeStruct((SEQ, 2 * SLICE, STATE), F32),
        compiler_params=pltpu.CompilerParams(vmem_limit_bytes=VMEM_LIMIT),
        name="scan_blocks",
    )(got)


def decays(rows_ref, k, mask):
    cin = rows_ref[k, 0:8, :]
    cols = cin.T
    out = []
    for h in range(HEADS_HERE):
        gap = jnp.broadcast_to(cin[h : h + 1, :], (SPAN, SPAN)) - jnp.broadcast_to(
            cols[:, h : h + 1], (SPAN, SPAN)
        )
        out.append(jnp.exp(jnp.where(mask, gap, -1e30)))
    return out


def crosses(xt, y):
    zero = jnp.zeros((WIDTH, SPAN), BF16)
    out = []
    for q in range(HEADS_HERE // 2):
        top = y[2 * q * WIDTH : (2 * q + 1) * WIDTH, :]
        low = y[(2 * q + 1) * WIDTH : (2 * q + 2) * WIDTH, :]
        both = cat([cat([top, zero], 1), cat([zero, low], 1)], 0)
        pair = dot_nn(xt[:, 2 * q * WIDTH : 2 * (q + 1) * WIDTH], both)
        out += [pair[:, :SPAN], pair[:, SPAN:]]
    return out


def inter(near_hi, near_lo, state):
    hi, lo = split2(state)
    return dot_nn(cat([hi, hi, lo], 1), cat([near_hi, near_lo, near_hi], 0))


PER2 = 8


HALF = 256


def by_side(blocks, send_ref, keep_ref):
    second = lax.axis_index("head") % 2 == 1
    for a in range(len(blocks) // 2):
        even, odd = blocks[2 * a], blocks[2 * a + 1]
        send_ref[a] = jnp.where(second, even, odd)
        keep_ref[a] = jnp.where(second, odd, even)


def halves(chunks):
    return [cat([chunks[2 * j], chunks[2 * j + 1]], 1) for j in range(len(chunks) // 2)]


def ascend_kernel(x_ref, y_ref, b_ref, c_ref, rows_ref, lanes_ref, db_ref, send_ref, keep_ref, s_ref, state):
    @pl.when(pl.program_id(0) == 0)
    def _():
        state[...] = jnp.zeros((STATE, ROWS), F32)

    r, l = iotas((SPAN, SPAN))
    mask = l >= r
    own = state[...]
    chunks = []
    for k in range(PER2):
        here = slice(k * SPAN, (k + 1) * SPAN)
        x = x_ref[:, here]
        bt, ct = b_ref[here, :].T, c_ref[here, :].T
        twice = cat([bt, bt], 1)
        total = jnp.zeros((SPAN, SPAN), F32)
        for cross, decay in zip(crosses(x.T, y_ref[:, here]), decays(rows_ref, k, mask)):
            total = total + cross * decay
        hi, lo = split2(total)
        db_ref[:, here] = dot_nt(cat([ct, ct], 1), cat([hi, lo], 1))
        yhi, ylo = split2(y_ref[:, here].astype(F32) * spread_rows(rows_ref[k, 8:16, :]))
        chunks.append(dot_nn(twice, cat([hi, lo], 0)) + inter(yhi, ylo, own))
        s_ref[k * STATE : (k + 1) * STATE, :] = own
        own = own * lanes_ref[k, 0:1, :] + dot_nt(
            twice, wide(x.astype(F32) * spread_rows(rows_ref[k, 16:24, :]))
        )
    state[...] = own
    by_side(halves(chunks), send_ref, keep_ref)


def chunk_specs(per, order):
    return [
        pl.BlockSpec((ROWS, per * SPAN), lambda i: (0, order(i))),
        pl.BlockSpec((ROWS, per * SPAN), lambda i: (0, order(i))),
        pl.BlockSpec((per * SPAN, STATE), lambda i: (order(i), 0)),
        pl.BlockSpec((per * SPAN, STATE), lambda i: (order(i), 0)),
        pl.BlockSpec((per, ROWSET, SPAN), lambda i: (order(i), 0, 0)),
        pl.BlockSpec((per, 8, ROWS), lambda i: (order(i), 0, 0)),
    ]


def side_specs(per, order):
    return [pl.BlockSpec((per // 4, STATE, HALF), lambda i: (order(i), 0, 0))] * 2


def ascend(x, y, b, c, rows, lanes):
    return pl.pallas_call(
        ascend_kernel,
        grid=(CHUNKS // PER2,),
        in_specs=chunk_specs(PER2, lambda i: i),
        out_specs=[pl.BlockSpec((STATE, PER2 * SPAN), lambda i: (0, i))]
        + side_specs(PER2, lambda i: i)
        + [pl.BlockSpec((PER2 * STATE, ROWS), lambda i: (i, 0))],
        out_shape=[jax.ShapeDtypeStruct((STATE, TOK), F32)]
        + [jax.ShapeDtypeStruct((4, STATE, HALF), F32)] * 2
        + [jax.ShapeDtypeStruct((CHUNKS * STATE, ROWS), F32)],
        scratch_shapes=[pltpu.VMEM((STATE, ROWS), F32)],
        compiler_params=pltpu.CompilerParams(vmem_limit_bytes=CHUNK_LIMIT),
        cost_estimate=pl.CostEstimate(flops=3_000_000_000, bytes_accessed=8_000_000, transcendentals=1_000_000),
        name="chunks_ascending",
    )(x, y, b, c, rows, lanes)


PER3 = 8


def descend_kernel(x_ref, y_ref, c_ref, rows_ref, lanes_ref, dbp_ref, send_ref, keep_ref, d_ref, grad):
    @pl.when(pl.program_id(0) == 0)
    def _():
        grad[...] = jnp.zeros((STATE, ROWS), F32)

    back = grad[...]
    chunks = [None] * PER3
    for k in reversed(range(PER3)):
        here = slice(k * SPAN, (k + 1) * SPAN)
        xhi, xlo = split2(x_ref[:, here].astype(F32) * spread_rows(rows_ref[k, 16:24, :]))
        chunks[k] = dbp_ref[:, here] + inter(xhi, xlo, back)
        d_ref[k * STATE : (k + 1) * STATE, :] = back
        ct = c_ref[here, :].T
        back = back * lanes_ref[k, 0:1, :] + dot_nt(
            cat([ct, ct], 1), wide(y_ref[:, here].astype(F32) * spread_rows(rows_ref[k, 8:16, :]))
        )
    grad[...] = back
    by_side(halves(chunks), send_ref, keep_ref)


def descend(x, y, c, rows, lanes, dbp):
    steps = CHUNKS // PER3
    order = lambda i: steps - 1 - i
    specs = chunk_specs(PER3, order)
    tokens = pl.BlockSpec((STATE, PER3 * SPAN), lambda i: (0, order(i)))
    states = pl.BlockSpec((PER3 * STATE, ROWS), lambda i: (order(i), 0))
    return pl.pallas_call(
        descend_kernel,
        grid=(steps,),
        in_specs=specs[:2] + specs[3:] + [tokens],
        out_specs=side_specs(PER3, order) + [states],
        out_shape=[
            jax.ShapeDtypeStruct((4, STATE, HALF), F32),
            jax.ShapeDtypeStruct((4, STATE, HALF), F32),
            jax.ShapeDtypeStruct((CHUNKS * STATE, ROWS), F32),
        ],
        scratch_shapes=[pltpu.VMEM((STATE, ROWS), F32)],
        compiler_params=pltpu.CompilerParams(vmem_limit_bytes=DOWN_LIMIT),
        cost_estimate=pl.CostEstimate(flops=3_000_000_000, bytes_accessed=8_000_000, transcendentals=0),
        name="chunks_descending",
    )(x, y, c, rows, lanes, dbp)


def blocks_of(side, place, row, bound_ref, edge_ref, src, held):
    index = lax.axis_index("head")
    chip, core = index // 2, index % 2
    edge = split2(from_slices(bound_ref, place))
    stack = cat(list(edge), 0)
    for i in range(4):
        to = jnp.bitwise_xor(chip, i)
        block = 2 * to + jnp.bitwise_xor(core, side)
        cols = pl.ds(pl.multiple_of(block * HALF, HALF), HALF)
        scale = cat(
            [spread_rows(edge_ref[2 * block + k, row : row + HEADS_HERE, :]) for k in range(2)], 1
        )
        near_hi, near_lo = split2(src[:, cols].astype(F32) * scale)
        first = dot_nn(stack, near_hi)
        yield i, held[to] + (first[:STATE] + (first[STATE:] + dot_nn(edge[0], near_lo)))


def send_out_kernel(bound_ref, edge_ref, y_ref, held_ref, out_ref):
    for i, block in blocks_of(1, 0, 0, bound_ref, edge_ref, y_ref, held_ref):
        out_ref[i] = block


def send_in_kernel(bound_ref, edge_ref, x_ref, held_ref, far_ref, own_ref):
    for i, block in blocks_of(1, SLICE, HEADS_HERE, bound_ref, edge_ref, x_ref, held_ref):
        if i == 0:
            own_ref[...] = block
        else:
            far_ref[i - 1] = block


def keep_kernel(bound_ref, edge_ref, x_ref, y_ref, in_ref, out_ref, kept_ref):
    for i, block in blocks_of(0, SLICE, HEADS_HERE, bound_ref, edge_ref, x_ref, in_ref):
        kept_ref[i, 0] = block
    for i, block in blocks_of(0, 0, 0, bound_ref, edge_ref, y_ref, out_ref):
        kept_ref[i, 1] = block


def sum_kernel(kept_ref, out_ref, in_ref, *outs):
    for m in range(4):
        outs[m][0] = kept_ref[m, 0] + in_ref[m - 1] if m else kept_ref[m, 0]
        outs[m][1] = kept_ref[m, 1] + out_ref[m]


def in_vmem(name, kernel, shapes, *operands):
    vmem = pl.BlockSpec(memory_space=pltpu.VMEM)
    return pl.pallas_call(
        kernel,
        in_specs=[vmem] * len(operands),
        out_specs=[vmem] * len(shapes),
        out_shape=[jax.ShapeDtypeStruct(shape, F32) for shape in shapes],
        compiler_params=pltpu.CompilerParams(vmem_limit_bytes=PART_LIMIT),
        cost_estimate=pl.CostEstimate(flops=500_000_000, bytes_accessed=3_000_000, transcendentals=0),
        name=name,
    )(*operands)


PER5 = 4


def last_kernel(x_ref, y_ref, b_ref, c_ref, rows_ref, lanes_ref, bound_ref, s_ref, d_ref, dx_ref, dl_ref):
    entering = from_slices(bound_ref, 0)
    leaving = from_slices(bound_ref, SLICE)
    r, l = iotas((SPAN, SPAN))
    mask = l >= r
    later = cat([ones_where(r >= l)] * 3, 0)
    every = jnp.ones((3 * (SPAN + ROWS), SPAN), BF16)
    owner_row, owner_lane = iotas((HEADS_HERE, ROWS))
    owned = owner_lane // WIDTH == owner_row
    for k in range(PER5):
        here = slice(k * SPAN, (k + 1) * SPAN)
        states = slice(k * STATE, (k + 1) * STATE)
        x, y, b, c = x_ref[:, here], y_ref[:, here], b_ref[here, :], c_ref[here, :]
        scores = dot_nt(b, c)
        s = s_ref[states, :] + lanes_ref[k, 1:2, :] * entering
        d = d_ref[states, :] + lanes_ref[k, 2:3, :] * leaving
        dhi, dlo = split2(d)
        shi, slo = split2(s)
        u = dot_nt(cat([dhi.T, dlo.T], 1), cat([b, b], 1)) * spread_rows(rows_ref[k, 16:24, :])
        z = dot_nt(cat([shi.T, slo.T], 1), cat([c, c], 1))
        row, inner = [], []
        for h, (cross, decay) in enumerate(zip(crosses(x.T, y), decays(rows_ref, k, mask))):
            weight = scores * decay
            yh = y[h * WIDTH : (h + 1) * WIDTH, :]
            inner.append(dot_nt(cat([yh, yh], 1), wide(weight)))
            row.append(jnp.sum(weight * cross, axis=0, keepdims=True))
        dx = cat(inner, 0) + u
        dx_ref[:, here] = dx.astype(BF16)
        xf = x.astype(F32)
        pending = (
            cat(row, 0)
            + rows_ref[k, 8 : 8 + HEADS_HERE, :] * head_sums(z * y.astype(F32))
            - head_sums(xf * dx)
        )
        meet = jnp.where(owned, jnp.sum(s * d, axis=0, keepdims=True), 0.0) * cat(
            [rows_ref[k, 24 : 24 + HEADS_HERE, :]] * 2, 1
        )
        through = cat([head_sums(xf * u), meet], 1)
        dl_ref[:, here] = dot_nn(cat(list(split3(pending)), 1), later) + dot_nn(
            cat(list(split3(through)), 1), every
        )


def last_pass(x, y, b, c, rows, lanes, bound, s, d):
    states = pl.BlockSpec((PER5 * STATE, ROWS), lambda i: (i, 0))
    return pl.pallas_call(
        last_kernel,
        grid=(CHUNKS // PER5,),
        in_specs=chunk_specs(PER5, lambda i: i)
        + [
            pl.BlockSpec((SEQ, 2 * SLICE, STATE), lambda i: (0, 0, 0)),
            states,
            states,
        ],
        out_specs=[
            pl.BlockSpec((ROWS, PER5 * SPAN), lambda i: (0, i)),
            pl.BlockSpec((HEADS_HERE, PER5 * SPAN), lambda i: (0, i)),
        ],
        out_shape=[
            jax.ShapeDtypeStruct((ROWS, TOK), BF16),
            jax.ShapeDtypeStruct((HEADS_HERE, TOK), F32),
        ],
        compiler_params=pltpu.CompilerParams(vmem_limit_bytes=LAST_LIMIT),
        cost_estimate=pl.CostEstimate(flops=6_000_000_000, bytes_accessed=12_000_000, transcendentals=1_000_000),
        name="inputs_and_decay",
    )(x, y, b, c, rows, lanes, bound, s, d)


def merge_kernel(own_ref, late_ref, near_ref, far_ref, side_ref, in_ref, out_ref):
    group = lax.axis_index("head") // 4
    for t, ref in enumerate((in_ref, out_ref)):
        own = own_ref[t] + near_ref[t]
        if t == 0:
            own = own + late_ref[...]
        ref[pl.ds(group, HALF, stride=2), :] = own.T
        ref[pl.ds(1 - group, HALF, stride=2), :] = (far_ref[t] + side_ref[t]).T


def local(inputs, log_decay, in_proj, out_proj, upstream):
    x = jnp.transpose(inputs, (1, 2, 0)).reshape(ROWS, TOK)
    y = jnp.transpose(upstream, (1, 2, 0)).reshape(ROWS, TOK)
    log = jnp.transpose(log_decay)
    b2 = in_proj.reshape(2 * TOK, STATE)
    c2 = out_proj.reshape(2 * TOK, STATE)
    message, rows, edge, lanes, b, c = first_pass(x, y, b2, c2, log)
    got = lax.all_to_all(message, "seq", 0, 0)
    dbp, dc_send, dc_keep, s = ascend(x, y, b, c, rows, lanes)
    got, dbp = lax.optimization_barrier((got, dbp))
    bound = lax.all_to_all(scan_blocks(got), "seq", 0, 0)
    db_send, db_keep, d = descend(x, y, c, rows, lanes, dbp)
    bound, d = lax.optimization_barrier((bound, d))
    pair = [(i, i ^ 1) for i in range(8)]
    block = (STATE, HALF)
    (sent_out,) = in_vmem("out_send", send_out_kernel, [(4, *block)], bound, edge, y, dc_send)
    got_out = lax.ppermute(sent_out, "head", pair)
    db_send, sent_out = lax.optimization_barrier((db_send, sent_out))
    sent_in, sent_own = in_vmem(
        "in_send", send_in_kernel, [(3, *block), block], bound, edge, x, db_send
    )
    got_in = lax.ppermute(sent_in, "head", pair)
    late = lax.ppermute(sent_own, "head", pair)
    dc_keep, sent_in = lax.optimization_barrier((dc_keep, sent_in))
    (kept,) = in_vmem(
        "keep", keep_kernel, [(4, 2, *block)], bound, edge, x, y, db_keep, dc_keep
    )
    parts = in_vmem("sum_cores", sum_kernel, [(2, *block)] * 4, kept, got_out, got_in)
    moved = [
        lax.ppermute(parts[m], "head", [(i, i ^ (2 * m)) for i in range(8)]) for m in (1, 2, 3)
    ]
    grad_x, grad_log = last_pass(x, y, b, c, rows, lanes, bound, s, d)
    grad_in, grad_out = in_vmem(
        "merge", merge_kernel, [(2 * HALF, STATE)] * 2, parts[0], late, *moved
    )
    return (
        jnp.transpose(grad_x.reshape(HEADS_HERE, WIDTH, TOK), (2, 0, 1)),
        jnp.transpose(grad_log),
        grad_in.reshape(HALF, 2, STATE),
        grad_out.reshape(HALF, 2, STATE),
    )


def solution(mesh):
    in_specs = (
        P("seq", "head", None),
        P("seq", "head"),
        P("seq", None, None),
        P("seq", None, None),
        P("seq", "head", None),
    )
    out_specs = (
        P("seq", "head", None),
        P("seq", "head"),
        P(("seq", "head"), None, None),
        P(("seq", "head"), None, None),
    )
    return jax.shard_map(local, mesh=mesh, in_specs=in_specs, out_specs=out_specs, check_vma=False)
```

```python
import functools

import jax
import jax.numpy as jnp
from jax import lax
from jax.experimental import pallas as pl
from jax.experimental.pallas import tpu as pltpu
from jax.sharding import PartitionSpec as P

HEADS_HERE = 4
WIDTH = 64
STATE = 128
SPAN = 128
TOK = 2048
CHUNKS = TOK // SPAN
ROWS = HEADS_HERE * WIDTH
SEQ = 32
SLICE = ROWS // SEQ
F32 = jnp.float32
BF16 = jnp.bfloat16
FIRST_LIMIT = 60 * 1024 * 1024
PART_LIMIT = 40 * 1024 * 1024
LAST_LIMIT = 40 * 1024 * 1024
CHUNK_LIMIT = 60 * 1024 * 1024
DOWN_LIMIT = 60 * 1024 * 1024
VMEM_LIMIT = 24 * 1024 * 1024


def dot_nn(a, b):
    return lax.dot_general(a, b, (((1,), (0,)), ((), ())), preferred_element_type=F32)


def dot_nt(a, b):
    return lax.dot_general(a, b, (((1,), (1,)), ((), ())), preferred_element_type=F32)


def split2(x):
    hi = x.astype(BF16)
    return hi, (x - hi.astype(F32)).astype(BF16)


def split3(x):
    a = x.astype(BF16)
    rest = x - a.astype(F32)
    b = rest.astype(BF16)
    return a, b, (rest - b.astype(F32)).astype(BF16)


def cat(parts, axis):
    return jnp.concatenate(parts, axis=axis)


def wide(x):
    hi, lo = split2(x)
    return cat([hi, lo], 1)


def iotas(shape):
    return lax.broadcasted_iota(jnp.int32, shape, 0), lax.broadcasted_iota(jnp.int32, shape, 1)


def ones_where(mask):
    return jnp.where(mask, 1.0, 0.0).astype(BF16)


def pad_heads(x):
    return cat([x, jnp.zeros((8 - HEADS_HERE, x.shape[1]), F32)], 0)


def spread_rows(rows):
    return cat(
        [jnp.broadcast_to(rows[h : h + 1, :], (WIDTH, SPAN)) for h in range(HEADS_HERE)], 0
    )


def head_sums(x):
    return cat(
        [
            jnp.sum(x[h * WIDTH : (h + 1) * WIDTH, :], axis=0, keepdims=True)
            for h in range(HEADS_HERE)
        ],
        0,
    )


def by_head(rows):
    lane = lax.broadcasted_iota(jnp.int32, (1, 2 * WIDTH), 1)
    return cat(
        [
            jnp.where(lane < WIDTH, rows[2 * q : 2 * q + 1, :], rows[2 * q + 1 : 2 * q + 2, :])
            for q in range(HEADS_HERE // 2)
        ],
        1,
    )


def to_slices(x, ref, place):
    for a in range(STATE // SLICE):
        for q in range(2):
            ref[2 * a + q, place : place + SLICE, :] = x[
                a * SLICE : (a + 1) * SLICE, q * STATE : (q + 1) * STATE
            ]


def from_slices(ref, place):
    return cat(
        [
            cat([ref[2 * a + q, place : place + SLICE, :] for q in range(2)], 1)
            for a in range(STATE // SLICE)
        ],
        0,
    )


ROWSET = 32


def choose(x, ref, group):
    ref[...] = x.astype(F32)
    return ref[pl.ds(group, SPAN, stride=2), :].astype(BF16)


def row_tables(log_ref, rows_ref, edge_ref, lanes_ref, msg_ref):
    r, c = iotas((SPAN, SPAN))
    tri = cat([ones_where(r <= c), ones_where(r > c), jnp.ones((SPAN, SPAN), BF16)], 1)
    tri = cat([tri] * 3, 0)
    stacked = cat(
        [
            cat(list(split3(pad_heads(log_ref[:, k * SPAN : (k + 1) * SPAN]))), 1)
            for k in range(CHUNKS)
        ],
        0,
    )
    sums = dot_nn(stacked, tri)
    tot = [sums[8 * k : 8 * k + 8, 2 * SPAN :] for k in range(CHUNKS)]
    before = jnp.zeros((8, SPAN), F32)
    for k in range(CHUNKS):
        cin = sums[8 * k : 8 * k + 8, :SPAN]
        rows_ref[k, 0:8, :] = cin
        rows_ref[k, 8:16, :] = jnp.exp(cin)
        rows_ref[k, 16:24, :] = jnp.exp(sums[8 * k : 8 * k + 8, SPAN : 2 * SPAN])
        whole = jnp.exp(tot[k])
        rows_ref[k, 24:32, :] = whole
        edge_ref[k, :HEADS_HERE, :] = jnp.exp(before + cin)[:HEADS_HERE]
        lanes_ref[k, 0:1, :] = by_head(whole)
        lanes_ref[k, 1:2, :] = by_head(jnp.exp(before))
        before = before + tot[k]
    after = jnp.zeros((8, SPAN), F32)
    for k in reversed(range(CHUNKS)):
        edge_ref[k, HEADS_HERE:, :] = jnp.exp(after + sums[8 * k : 8 * k + 8, SPAN : 2 * SPAN])[
            :HEADS_HERE
        ]
        lanes_ref[k, 2:3, :] = by_head(jnp.exp(after))
        lanes_ref[k, 3:8, :] = jnp.zeros((5, ROWS), F32)
        after = after + tot[k]
    to_slices(jnp.broadcast_to(by_head(jnp.exp(before)), (STATE, ROWS)), msg_ref, 2 * SLICE)


def first_kernel(
    x_hbm, y_hbm, b_hbm, c_hbm, log_hbm, msg_hbm, rows_hbm, edge_hbm, lanes_hbm, bs_hbm, cs_hbm,
    x_ref, y_ref, b_ref, c_ref, log_ref, msg_ref, rows_ref, edge_ref, lanes_ref, bs_ref, cs_ref, wide_ref,
    get_sem, put_sem
):
    gets = [pltpu.make_async_copy(log_hbm, log_ref, get_sem.at[0])]
    for q in range(2):
        rows, cols = pl.ds(q * TOK, TOK), pl.ds(q * TOK // 2, TOK // 2)
        for src, dst, part in (
            (b_hbm, b_ref, (rows, slice(None))),
            (x_hbm, x_ref, (slice(None), cols)),
            (c_hbm, c_ref, (rows, slice(None))),
            (y_hbm, y_ref, (slice(None), cols)),
        ):
            gets.append(
                pltpu.make_async_copy(src.at[part], dst.at[part], get_sem.at[len(gets)])
            )
    for copy in gets:
        copy.start()
    puts = []

    def put(src, dst):
        copy = pltpu.make_async_copy(src, dst, put_sem.at[len(puts)])
        copy.start()
        puts.append(copy)

    def put_message(place):
        part = pl.ds(place, SLICE)
        put(msg_ref.at[:, part, :], msg_hbm.at[:, part, :])

    group = lax.axis_index("head") // 4
    gets[0].wait()
    row_tables(log_ref, rows_ref, edge_ref, lanes_ref, msg_ref)
    put(rows_ref, rows_hbm)
    put(edge_ref, edge_hbm)
    put(lanes_ref, lanes_hbm)
    put_message(2 * SLICE)

    def gather(total, base, k, pairs_ref, chosen_ref, src, row):
        got = choose(pairs_ref[2 * k * SPAN : 2 * (k + 1) * SPAN, :], wide_ref.at[base + k], group)
        chosen_ref[k * SPAN : (k + 1) * SPAN, :] = got
        turned = got.T
        near = src[:, k * SPAN : (k + 1) * SPAN].astype(F32) * spread_rows(
            edge_ref[k, row : row + HEADS_HERE, :]
        )
        return total + dot_nt(cat([turned, turned], 1), wide(near))

    own = jnp.zeros((STATE, ROWS), F32)
    back = jnp.zeros((STATE, ROWS), F32)
    for q in range(2):
        chunks = range(q * CHUNKS // 2, (q + 1) * CHUNKS // 2)
        gets[4 * q + 1].wait()
        gets[4 * q + 2].wait()
        for k in chunks:
            own = gather(own, 0, k, b_ref, bs_ref, x_ref, HEADS_HERE)
        if q == 1:
            put(bs_ref, bs_hbm)
            to_slices(own, msg_ref, 0)
            put_message(0)
        gets[4 * q + 3].wait()
        gets[4 * q + 4].wait()
        for k in chunks:
            back = gather(back, CHUNKS, k, c_ref, cs_ref, y_ref, 0)
    put(cs_ref, cs_hbm)
    to_slices(back, msg_ref, SLICE)
    put_message(SLICE)
    for copy in puts:
        copy.wait()


def first_pass(x, y, b, c, log):
    hbm = pl.BlockSpec(memory_space=pltpu.HBM)
    return pl.pallas_call(
        first_kernel,
        in_specs=[hbm] * 5,
        out_specs=[hbm] * 6,
        out_shape=[
            jax.ShapeDtypeStruct((SEQ, 3 * SLICE, STATE), F32),
            jax.ShapeDtypeStruct((CHUNKS, ROWSET, SPAN), F32),
            jax.ShapeDtypeStruct((CHUNKS, 8, SPAN), F32),
            jax.ShapeDtypeStruct((CHUNKS, 8, ROWS), F32),
            jax.ShapeDtypeStruct((TOK, STATE), BF16),
            jax.ShapeDtypeStruct((TOK, STATE), BF16),
        ],
        scratch_shapes=[
            pltpu.VMEM((ROWS, TOK), BF16),
            pltpu.VMEM((ROWS, TOK), BF16),
            pltpu.VMEM((2 * TOK, STATE), BF16),
            pltpu.VMEM((2 * TOK, STATE), BF16),
            pltpu.VMEM((HEADS_HERE, TOK), F32),
            pltpu.VMEM((SEQ, 3 * SLICE, STATE), F32),
            pltpu.VMEM((CHUNKS, ROWSET, SPAN), F32),
            pltpu.VMEM((CHUNKS, 8, SPAN), F32),
            pltpu.VMEM((CHUNKS, 8, ROWS), F32),
            pltpu.VMEM((TOK, STATE), BF16),
            pltpu.VMEM((TOK, STATE), BF16),
            pltpu.VMEM((2 * CHUNKS, 2 * SPAN, STATE), F32),
            pltpu.SemaphoreType.DMA((9,)),
            pltpu.SemaphoreType.DMA((8,)),
        ],
        compiler_params=pltpu.CompilerParams(vmem_limit_bytes=FIRST_LIMIT),
        cost_estimate=pl.CostEstimate(flops=800_000_000, bytes_accessed=6_000_000, transcendentals=20_000),
        name="own_states",
    )(x, y, b, c, log)


def scan_kernel(got_ref, out_ref):
    carry = jnp.zeros((SLICE, STATE), F32)
    for k in range(SEQ):
        out_ref[k, :SLICE, :] = carry
        if k < SEQ - 1:
            carry = carry * got_ref[k, 2 * SLICE :, :] + got_ref[k, :SLICE, :]
    carry = jnp.zeros((SLICE, STATE), F32)
    for k in reversed(range(SEQ)):
        out_ref[k, SLICE:, :] = carry
        if k > 0:
            carry = carry * got_ref[k, 2 * SLICE :, :] + got_ref[k, SLICE : 2 * SLICE, :]


def scan_blocks(got):
    return pl.pallas_call(
        scan_kernel,
        in_specs=[pl.BlockSpec(memory_space=pltpu.VMEM)],
        out_shape=jax.ShapeDtypeStruct((SEQ, 2 * SLICE, STATE), F32),
        compiler_params=pltpu.CompilerParams(vmem_limit_bytes=VMEM_LIMIT),
        name="scan_blocks",
    )(got)


def decays(rows_ref, k, mask):
    cin = rows_ref[k, 0:8, :]
    cols = cin.T
    out = []
    for h in range(HEADS_HERE):
        gap = jnp.broadcast_to(cin[h : h + 1, :], (SPAN, SPAN)) - jnp.broadcast_to(
            cols[:, h : h + 1], (SPAN, SPAN)
        )
        out.append(jnp.exp(jnp.where(mask, gap, -1e30)))
    return out


def crosses(xt, y):
    zero = jnp.zeros((WIDTH, SPAN), BF16)
    out = []
    for q in range(HEADS_HERE // 2):
        top = y[2 * q * WIDTH : (2 * q + 1) * WIDTH, :]
        low = y[(2 * q + 1) * WIDTH : (2 * q + 2) * WIDTH, :]
        both = cat([cat([top, zero], 1), cat([zero, low], 1)], 0)
        pair = dot_nn(xt[:, 2 * q * WIDTH : 2 * (q + 1) * WIDTH], both)
        out += [pair[:, :SPAN], pair[:, SPAN:]]
    return out


def inter(near_hi, near_lo, state):
    hi, lo = split2(state)
    return dot_nn(cat([hi, hi, lo], 1), cat([near_hi, near_lo, near_hi], 0))


PER2 = 8


HALF = 256


def by_side(blocks, send_ref, keep_ref):
    second = lax.axis_index("head") % 2 == 1
    for a in range(len(blocks) // 2):
        even, odd = blocks[2 * a], blocks[2 * a + 1]
        send_ref[a] = jnp.where(second, even, odd)
        keep_ref[a] = jnp.where(second, odd, even)


def halves(chunks):
    return [cat([chunks[2 * j], chunks[2 * j + 1]], 1) for j in range(len(chunks) // 2)]


def ascend_kernel(x_ref, y_ref, b_ref, c_ref, rows_ref, lanes_ref, db_ref, send_ref, keep_ref, s_ref, state):
    @pl.when(pl.program_id(0) == 0)
    def _():
        state[...] = jnp.zeros((STATE, ROWS), F32)

    r, l = iotas((SPAN, SPAN))
    mask = l >= r
    own = state[...]
    chunks = []
    for k in range(PER2):
        here = slice(k * SPAN, (k + 1) * SPAN)
        x = x_ref[:, here]
        bt, ct = b_ref[here, :].T, c_ref[here, :].T
        twice = cat([bt, bt], 1)
        total = jnp.zeros((SPAN, SPAN), F32)
        for cross, decay in zip(crosses(x.T, y_ref[:, here]), decays(rows_ref, k, mask)):
            total = total + cross * decay
        hi, lo = split2(total)
        db_ref[:, here] = dot_nt(cat([ct, ct], 1), cat([hi, lo], 1))
        yhi, ylo = split2(y_ref[:, here].astype(F32) * spread_rows(rows_ref[k, 8:16, :]))
        chunks.append(dot_nn(twice, cat([hi, lo], 0)) + inter(yhi, ylo, own))
        s_ref[k * STATE : (k + 1) * STATE, :] = own
        own = own * lanes_ref[k, 0:1, :] + dot_nt(
            twice, wide(x.astype(F32) * spread_rows(rows_ref[k, 16:24, :]))
        )
    state[...] = own
    by_side(halves(chunks), send_ref, keep_ref)


def chunk_specs(per, order):
    return [
        pl.BlockSpec((ROWS, per * SPAN), lambda i: (0, order(i))),
        pl.BlockSpec((ROWS, per * SPAN), lambda i: (0, order(i))),
        pl.BlockSpec((per * SPAN, STATE), lambda i: (order(i), 0)),
        pl.BlockSpec((per * SPAN, STATE), lambda i: (order(i), 0)),
        pl.BlockSpec((per, ROWSET, SPAN), lambda i: (order(i), 0, 0)),
        pl.BlockSpec((per, 8, ROWS), lambda i: (order(i), 0, 0)),
    ]


def side_specs(per, order):
    return [pl.BlockSpec((per // 4, STATE, HALF), lambda i: (order(i), 0, 0))] * 2


def ascend(x, y, b, c, rows, lanes):
    return pl.pallas_call(
        ascend_kernel,
        grid=(CHUNKS // PER2,),
        in_specs=chunk_specs(PER2, lambda i: i),
        out_specs=[pl.BlockSpec((STATE, PER2 * SPAN), lambda i: (0, i))]
        + side_specs(PER2, lambda i: i)
        + [pl.BlockSpec((PER2 * STATE, ROWS), lambda i: (i, 0))],
        out_shape=[jax.ShapeDtypeStruct((STATE, TOK), F32)]
        + [jax.ShapeDtypeStruct((4, STATE, HALF), F32)] * 2
        + [jax.ShapeDtypeStruct((CHUNKS * STATE, ROWS), F32)],
        scratch_shapes=[pltpu.VMEM((STATE, ROWS), F32)],
        compiler_params=pltpu.CompilerParams(vmem_limit_bytes=CHUNK_LIMIT),
        cost_estimate=pl.CostEstimate(flops=3_000_000_000, bytes_accessed=8_000_000, transcendentals=1_000_000),
        name="chunks_ascending",
    )(x, y, b, c, rows, lanes)


PER3 = 8


def descend_kernel(x_ref, y_ref, c_ref, rows_ref, lanes_ref, dbp_ref, send_ref, keep_ref, d_ref, grad):
    @pl.when(pl.program_id(0) == 0)
    def _():
        grad[...] = jnp.zeros((STATE, ROWS), F32)

    back = grad[...]
    chunks = [None] * PER3
    for k in reversed(range(PER3)):
        here = slice(k * SPAN, (k + 1) * SPAN)
        xhi, xlo = split2(x_ref[:, here].astype(F32) * spread_rows(rows_ref[k, 16:24, :]))
        chunks[k] = dbp_ref[:, here] + inter(xhi, xlo, back)
        d_ref[k * STATE : (k + 1) * STATE, :] = back
        ct = c_ref[here, :].T
        back = back * lanes_ref[k, 0:1, :] + dot_nt(
            cat([ct, ct], 1), wide(y_ref[:, here].astype(F32) * spread_rows(rows_ref[k, 8:16, :]))
        )
    grad[...] = back
    by_side(halves(chunks), send_ref, keep_ref)


def descend(x, y, c, rows, lanes, dbp):
    steps = CHUNKS // PER3
    order = lambda i: steps - 1 - i
    specs = chunk_specs(PER3, order)
    tokens = pl.BlockSpec((STATE, PER3 * SPAN), lambda i: (0, order(i)))
    states = pl.BlockSpec((PER3 * STATE, ROWS), lambda i: (order(i), 0))
    return pl.pallas_call(
        descend_kernel,
        grid=(steps,),
        in_specs=specs[:2] + specs[3:] + [tokens],
        out_specs=side_specs(PER3, order) + [states],
        out_shape=[
            jax.ShapeDtypeStruct((4, STATE, HALF), F32),
            jax.ShapeDtypeStruct((4, STATE, HALF), F32),
            jax.ShapeDtypeStruct((CHUNKS * STATE, ROWS), F32),
        ],
        scratch_shapes=[pltpu.VMEM((STATE, ROWS), F32)],
        compiler_params=pltpu.CompilerParams(vmem_limit_bytes=DOWN_LIMIT),
        cost_estimate=pl.CostEstimate(flops=3_000_000_000, bytes_accessed=8_000_000, transcendentals=0),
        name="chunks_descending",
    )(x, y, c, rows, lanes, dbp)


def blocks_of(side, place, row, bound_ref, edge_ref, src, held):
    index = lax.axis_index("head")
    chip, core = index // 2, index % 2
    edge = split2(from_slices(bound_ref, place))
    stack = cat(list(edge), 0)
    for i in range(4):
        to = jnp.bitwise_xor(chip, i)
        block = 2 * to + jnp.bitwise_xor(core, side)
        cols = pl.ds(pl.multiple_of(block * HALF, HALF), HALF)
        scale = cat(
            [spread_rows(edge_ref[2 * block + k, row : row + HEADS_HERE, :]) for k in range(2)], 1
        )
        near_hi, near_lo = split2(src[:, cols].astype(F32) * scale)
        first = dot_nn(stack, near_hi)
        yield i, held[to] + (first[:STATE] + (first[STATE:] + dot_nn(edge[0], near_lo)))


def send_out_kernel(bound_ref, edge_ref, y_ref, held_ref, out_ref):
    for i, block in blocks_of(1, 0, 0, bound_ref, edge_ref, y_ref, held_ref):
        out_ref[i] = block


def send_in_kernel(bound_ref, edge_ref, x_ref, held_ref, far_ref, own_ref):
    for i, block in blocks_of(1, SLICE, HEADS_HERE, bound_ref, edge_ref, x_ref, held_ref):
        if i == 0:
            own_ref[...] = block
        else:
            far_ref[i - 1] = block


def keep_kernel(bound_ref, edge_ref, x_ref, y_ref, in_ref, out_ref, kept_ref):
    for i, block in blocks_of(0, SLICE, HEADS_HERE, bound_ref, edge_ref, x_ref, in_ref):
        kept_ref[i, 0] = block
    for i, block in blocks_of(0, 0, 0, bound_ref, edge_ref, y_ref, out_ref):
        kept_ref[i, 1] = block


def sum_kernel(kept_ref, out_ref, in_ref, *outs):
    second = lax.axis_index("head") % 2
    own_ref, rest = outs[0], outs[1:]
    own_ref[0] = kept_ref[0, 0]
    own_ref[1] = kept_ref[0, 1] + out_ref[0]
    for ref, m in zip(rest, (1 + 2 * second, 3 - 2 * second, 2)):
        ref[0] = kept_ref[m, 0] + in_ref[m - 1]
        ref[1] = kept_ref[m, 1] + out_ref[m]


def in_vmem(name, kernel, shapes, *operands):
    vmem = pl.BlockSpec(memory_space=pltpu.VMEM)
    return pl.pallas_call(
        kernel,
        in_specs=[vmem] * len(operands),
        out_specs=[vmem] * len(shapes),
        out_shape=[jax.ShapeDtypeStruct(shape, F32) for shape in shapes],
        compiler_params=pltpu.CompilerParams(vmem_limit_bytes=PART_LIMIT),
        cost_estimate=pl.CostEstimate(flops=500_000_000, bytes_accessed=3_000_000, transcendentals=0),
        name=name,
    )(*operands)


PER5 = 4


def last_kernel(x_ref, y_ref, b_ref, c_ref, rows_ref, lanes_ref, bound_ref, s_ref, d_ref, dx_ref, dl_ref):
    entering = from_slices(bound_ref, 0)
    leaving = from_slices(bound_ref, SLICE)
    r, l = iotas((SPAN, SPAN))
    mask = l >= r
    later = cat([ones_where(r >= l)] * 3, 0)
    every = jnp.ones((3 * (SPAN + ROWS), SPAN), BF16)
    owner_row, owner_lane = iotas((HEADS_HERE, ROWS))
    owned = owner_lane // WIDTH == owner_row
    for k in range(PER5):
        here = slice(k * SPAN, (k + 1) * SPAN)
        states = slice(k * STATE, (k + 1) * STATE)
        x, y, b, c = x_ref[:, here], y_ref[:, here], b_ref[here, :], c_ref[here, :]
        scores = dot_nt(b, c)
        s = s_ref[states, :] + lanes_ref[k, 1:2, :] * entering
        d = d_ref[states, :] + lanes_ref[k, 2:3, :] * leaving
        dhi, dlo = split2(d)
        shi, slo = split2(s)
        u = dot_nt(cat([dhi.T, dlo.T], 1), cat([b, b], 1)) * spread_rows(rows_ref[k, 16:24, :])
        z = dot_nt(cat([shi.T, slo.T], 1), cat([c, c], 1))
        row, inner = [], []
        for h, (cross, decay) in enumerate(zip(crosses(x.T, y), decays(rows_ref, k, mask))):
            weight = scores * decay
            yh = y[h * WIDTH : (h + 1) * WIDTH, :]
            inner.append(dot_nt(cat([yh, yh], 1), wide(weight)))
            row.append(jnp.sum(weight * cross, axis=0, keepdims=True))
        dx = cat(inner, 0) + u
        dx_ref[:, here] = dx.astype(BF16)
        xf = x.astype(F32)
        pending = (
            cat(row, 0)
            + rows_ref[k, 8 : 8 + HEADS_HERE, :] * head_sums(z * y.astype(F32))
            - head_sums(xf * dx)
        )
        meet = jnp.where(owned, jnp.sum(s * d, axis=0, keepdims=True), 0.0) * cat(
            [rows_ref[k, 24 : 24 + HEADS_HERE, :]] * 2, 1
        )
        through = cat([head_sums(xf * u), meet], 1)
        dl_ref[:, here] = dot_nn(cat(list(split3(pending)), 1), later) + dot_nn(
            cat(list(split3(through)), 1), every
        )


def last_pass(x, y, b, c, rows, lanes, bound, s, d):
    states = pl.BlockSpec((PER5 * STATE, ROWS), lambda i: (i, 0))
    return pl.pallas_call(
        last_kernel,
        grid=(CHUNKS // PER5,),
        in_specs=chunk_specs(PER5, lambda i: i)
        + [
            pl.BlockSpec((SEQ, 2 * SLICE, STATE), lambda i: (0, 0, 0)),
            states,
            states,
        ],
        out_specs=[
            pl.BlockSpec((ROWS, PER5 * SPAN), lambda i: (0, i)),
            pl.BlockSpec((HEADS_HERE, PER5 * SPAN), lambda i: (0, i)),
        ],
        out_shape=[
            jax.ShapeDtypeStruct((ROWS, TOK), BF16),
            jax.ShapeDtypeStruct((HEADS_HERE, TOK), F32),
        ],
        compiler_params=pltpu.CompilerParams(vmem_limit_bytes=LAST_LIMIT),
        cost_estimate=pl.CostEstimate(flops=6_000_000_000, bytes_accessed=12_000_000, transcendentals=1_000_000),
        name="inputs_and_decay",
    )(x, y, b, c, rows, lanes, bound, s, d)


def merge_kernel(own_ref, late_ref, one_ref, two_ref, far_ref, in_ref, out_ref):
    index = lax.axis_index("head")
    group, second = index // 4, index % 2 == 1
    for t, ref in enumerate((in_ref, out_ref)):
        one, two = one_ref[t], two_ref[t]
        own = own_ref[t] + jnp.where(second, two, one)
        if t == 0:
            own = own + late_ref[...]
        ref[pl.ds(group, HALF, stride=2), :] = own.T
        ref[pl.ds(1 - group, HALF, stride=2), :] = (far_ref[t] + jnp.where(second, one, two)).T


def local(inputs, log_decay, in_proj, out_proj, upstream):
    x = jnp.transpose(inputs, (1, 2, 0)).reshape(ROWS, TOK)
    y = jnp.transpose(upstream, (1, 2, 0)).reshape(ROWS, TOK)
    log = jnp.transpose(log_decay)
    b2 = in_proj.reshape(2 * TOK, STATE)
    c2 = out_proj.reshape(2 * TOK, STATE)
    message, rows, edge, lanes, b, c = first_pass(x, y, b2, c2, log)
    got = lax.all_to_all(message, "seq", 0, 0)
    dbp, dc_send, dc_keep, s = ascend(x, y, b, c, rows, lanes)
    got, dbp = lax.optimization_barrier((got, dbp))
    bound = lax.all_to_all(scan_blocks(got), "seq", 0, 0)
    db_send, db_keep, d = descend(x, y, c, rows, lanes, dbp)
    bound, d = lax.optimization_barrier((bound, d))
    pair = [(i, i ^ 1) for i in range(8)]
    block = (STATE, HALF)
    (sent_out,) = in_vmem("out_send", send_out_kernel, [(4, *block)], bound, edge, y, dc_send)
    got_out = lax.ppermute(sent_out, "head", pair)
    db_send, sent_out = lax.optimization_barrier((db_send, sent_out))
    sent_in, sent_own = in_vmem(
        "in_send", send_in_kernel, [(3, *block), block], bound, edge, x, db_send
    )
    got_in = lax.ppermute(sent_in, "head", pair)
    late = lax.ppermute(sent_own, "head", pair)
    dc_keep, sent_in = lax.optimization_barrier((dc_keep, sent_in))
    (kept,) = in_vmem(
        "keep", keep_kernel, [(4, 2, *block)], bound, edge, x, y, db_keep, dc_keep
    )
    parts = in_vmem("sum_cores", sum_kernel, [(2, *block)] * 4, kept, got_out, got_in)
    hops = [(2, 6), (6, 2), (4, 4)]
    moved = [
        lax.ppermute(part, "head", [(i, i ^ hop[i % 2]) for i in range(8)])
        for part, hop in zip(parts[1:], hops)
    ]
    grad_x, grad_log = last_pass(x, y, b, c, rows, lanes, bound, s, d)
    grad_in, grad_out = in_vmem(
        "merge", merge_kernel, [(2 * HALF, STATE)] * 2, parts[0], late, *moved
    )
    return (
        jnp.transpose(grad_x.reshape(HEADS_HERE, WIDTH, TOK), (2, 0, 1)),
        jnp.transpose(grad_log),
        grad_in.reshape(HALF, 2, STATE),
        grad_out.reshape(HALF, 2, STATE),
    )


def solution(mesh):
    in_specs = (
        P("seq", "head", None),
        P("seq", "head"),
        P("seq", None, None),
        P("seq", None, None),
        P("seq", "head", None),
    )
    out_specs = (
        P("seq", "head", None),
        P("seq", "head"),
        P(("seq", "head"), None, None),
        P(("seq", "head"), None, None),
    )
    return jax.shard_map(local, mesh=mesh, in_specs=in_specs, out_specs=out_specs, check_vma=False)
```

```python
import functools

import jax
import jax.numpy as jnp
from jax import lax
from jax.experimental import pallas as pl
from jax.experimental.pallas import tpu as pltpu
from jax.sharding import PartitionSpec as P

HEADS_HERE = 4
WIDTH = 64
STATE = 128
SPAN = 128
TOK = 2048
CHUNKS = TOK // SPAN
ROWS = HEADS_HERE * WIDTH
SEQ = 32
SLICE = ROWS // SEQ
F32 = jnp.float32
BF16 = jnp.bfloat16
FIRST_LIMIT = 60 * 1024 * 1024
PART_LIMIT = 40 * 1024 * 1024
LAST_LIMIT = 40 * 1024 * 1024
CHUNK_LIMIT = 60 * 1024 * 1024
DOWN_LIMIT = 60 * 1024 * 1024
VMEM_LIMIT = 24 * 1024 * 1024


def dot_nn(a, b):
    return lax.dot_general(a, b, (((1,), (0,)), ((), ())), preferred_element_type=F32)


def dot_nt(a, b):
    return lax.dot_general(a, b, (((1,), (1,)), ((), ())), preferred_element_type=F32)


def split2(x):
    hi = x.astype(BF16)
    return hi, (x - hi.astype(F32)).astype(BF16)


def split3(x):
    a = x.astype(BF16)
    rest = x - a.astype(F32)
    b = rest.astype(BF16)
    return a, b, (rest - b.astype(F32)).astype(BF16)


def cat(parts, axis):
    return jnp.concatenate(parts, axis=axis)


def wide(x):
    hi, lo = split2(x)
    return cat([hi, lo], 1)


def iotas(shape):
    return lax.broadcasted_iota(jnp.int32, shape, 0), lax.broadcasted_iota(jnp.int32, shape, 1)


def ones_where(mask):
    return jnp.where(mask, 1.0, 0.0).astype(BF16)


def pad_heads(x):
    return cat([x, jnp.zeros((8 - HEADS_HERE, x.shape[1]), F32)], 0)


def spread_rows(rows):
    return cat(
        [jnp.broadcast_to(rows[h : h + 1, :], (WIDTH, SPAN)) for h in range(HEADS_HERE)], 0
    )


def head_sums(x):
    return cat(
        [
            jnp.sum(x[h * WIDTH : (h + 1) * WIDTH, :], axis=0, keepdims=True)
            for h in range(HEADS_HERE)
        ],
        0,
    )


def by_head(rows):
    lane = lax.broadcasted_iota(jnp.int32, (1, 2 * WIDTH), 1)
    return cat(
        [
            jnp.where(lane < WIDTH, rows[2 * q : 2 * q + 1, :], rows[2 * q + 1 : 2 * q + 2, :])
            for q in range(HEADS_HERE // 2)
        ],
        1,
    )


def to_slices(x, ref, place):
    for a in range(STATE // SLICE):
        for q in range(2):
            ref[2 * a + q, place : place + SLICE, :] = x[
                a * SLICE : (a + 1) * SLICE, q * STATE : (q + 1) * STATE
            ]


def from_slices(ref, place):
    return cat(
        [
            cat([ref[2 * a + q, place : place + SLICE, :] for q in range(2)], 1)
            for a in range(STATE // SLICE)
        ],
        0,
    )


ROWSET = 32


def choose(x, ref, group):
    ref[...] = x.astype(F32)
    return ref[pl.ds(group, SPAN, stride=2), :].astype(BF16)


def row_tables(log_ref, rows_ref, edge_ref, lanes_ref, msg_ref):
    r, c = iotas((SPAN, SPAN))
    tri = cat([ones_where(r <= c), ones_where(r > c), jnp.ones((SPAN, SPAN), BF16)], 1)
    tri = cat([tri] * 3, 0)
    stacked = cat(
        [
            cat(list(split3(pad_heads(log_ref[:, k * SPAN : (k + 1) * SPAN]))), 1)
            for k in range(CHUNKS)
        ],
        0,
    )
    sums = dot_nn(stacked, tri)
    tot = [sums[8 * k : 8 * k + 8, 2 * SPAN :] for k in range(CHUNKS)]
    before = jnp.zeros((8, SPAN), F32)
    for k in range(CHUNKS):
        cin = sums[8 * k : 8 * k + 8, :SPAN]
        rows_ref[k, 0:8, :] = cin
        rows_ref[k, 8:16, :] = jnp.exp(cin)
        rows_ref[k, 16:24, :] = jnp.exp(sums[8 * k : 8 * k + 8, SPAN : 2 * SPAN])
        whole = jnp.exp(tot[k])
        rows_ref[k, 24:32, :] = whole
        edge_ref[k, :HEADS_HERE, :] = jnp.exp(before + cin)[:HEADS_HERE]
        lanes_ref[k, 0:1, :] = by_head(whole)
        lanes_ref[k, 1:2, :] = by_head(jnp.exp(before))
        before = before + tot[k]
    after = jnp.zeros((8, SPAN), F32)
    for k in reversed(range(CHUNKS)):
        edge_ref[k, HEADS_HERE:, :] = jnp.exp(after + sums[8 * k : 8 * k + 8, SPAN : 2 * SPAN])[
            :HEADS_HERE
        ]
        lanes_ref[k, 2:3, :] = by_head(jnp.exp(after))
        lanes_ref[k, 3:8, :] = jnp.zeros((5, ROWS), F32)
        after = after + tot[k]
    to_slices(jnp.broadcast_to(by_head(jnp.exp(before)), (STATE, ROWS)), msg_ref, 2 * SLICE)


def first_kernel(
    x_hbm, y_hbm, b_hbm, c_hbm, log_hbm, msg_hbm, rows_hbm, edge_hbm, lanes_hbm, bs_hbm, cs_hbm,
    x_ref, y_ref, b_ref, c_ref, log_ref, msg_ref, rows_ref, edge_ref, lanes_ref, bs_ref, cs_ref, wide_ref,
    get_sem, put_sem
):
    gets = [pltpu.make_async_copy(log_hbm, log_ref, get_sem.at[0])]
    for q in range(2):
        rows, cols = pl.ds(q * TOK, TOK), pl.ds(q * TOK // 2, TOK // 2)
        for src, dst, part in (
            (b_hbm, b_ref, (rows, slice(None))),
            (x_hbm, x_ref, (slice(None), cols)),
            (c_hbm, c_ref, (rows, slice(None))),
            (y_hbm, y_ref, (slice(None), cols)),
        ):
            gets.append(
                pltpu.make_async_copy(src.at[part], dst.at[part], get_sem.at[len(gets)])
            )
    for copy in gets:
        copy.start()
    puts = []

    def put(src, dst):
        copy = pltpu.make_async_copy(src, dst, put_sem.at[len(puts)])
        copy.start()
        puts.append(copy)

    def put_message(place):
        part = pl.ds(place, SLICE)
        put(msg_ref.at[:, part, :], msg_hbm.at[:, part, :])

    group = lax.axis_index("head") // 4
    gets[0].wait()
    row_tables(log_ref, rows_ref, edge_ref, lanes_ref, msg_ref)
    put(rows_ref, rows_hbm)
    put(edge_ref, edge_hbm)
    put(lanes_ref, lanes_hbm)
    put_message(2 * SLICE)

    def gather(total, base, k, pairs_ref, chosen_ref, src, row):
        got = choose(pairs_ref[2 * k * SPAN : 2 * (k + 1) * SPAN, :], wide_ref.at[base + k], group)
        chosen_ref[k * SPAN : (k + 1) * SPAN, :] = got
        turned = got.T
        near = src[:, k * SPAN : (k + 1) * SPAN].astype(F32) * spread_rows(
            edge_ref[k, row : row + HEADS_HERE, :]
        )
        return total + dot_nt(cat([turned, turned], 1), wide(near))

    own = jnp.zeros((STATE, ROWS), F32)
    back = jnp.zeros((STATE, ROWS), F32)
    for q in range(2):
        chunks = range(q * CHUNKS // 2, (q + 1) * CHUNKS // 2)
        gets[4 * q + 1].wait()
        gets[4 * q + 2].wait()
        for k in chunks:
            own = gather(own, 0, k, b_ref, bs_ref, x_ref, HEADS_HERE)
        if q == 1:
            put(bs_ref, bs_hbm)
            to_slices(own, msg_ref, 0)
            put_message(0)
        gets[4 * q + 3].wait()
        gets[4 * q + 4].wait()
        for k in chunks:
            back = gather(back, CHUNKS, k, c_ref, cs_ref, y_ref, 0)
    put(cs_ref, cs_hbm)
    to_slices(back, msg_ref, SLICE)
    put_message(SLICE)
    for copy in puts:
        copy.wait()


def first_pass(x, y, b, c, log):
    hbm = pl.BlockSpec(memory_space=pltpu.HBM)
    return pl.pallas_call(
        first_kernel,
        in_specs=[hbm] * 5,
        out_specs=[hbm] * 6,
        out_shape=[
            jax.ShapeDtypeStruct((SEQ, 3 * SLICE, STATE), F32),
            jax.ShapeDtypeStruct((CHUNKS, ROWSET, SPAN), F32),
            jax.ShapeDtypeStruct((CHUNKS, 8, SPAN), F32),
            jax.ShapeDtypeStruct((CHUNKS, 8, ROWS), F32),
            jax.ShapeDtypeStruct((TOK, STATE), BF16),
            jax.ShapeDtypeStruct((TOK, STATE), BF16),
        ],
        scratch_shapes=[
            pltpu.VMEM((ROWS, TOK), BF16),
            pltpu.VMEM((ROWS, TOK), BF16),
            pltpu.VMEM((2 * TOK, STATE), BF16),
            pltpu.VMEM((2 * TOK, STATE), BF16),
            pltpu.VMEM((HEADS_HERE, TOK), F32),
            pltpu.VMEM((SEQ, 3 * SLICE, STATE), F32),
            pltpu.VMEM((CHUNKS, ROWSET, SPAN), F32),
            pltpu.VMEM((CHUNKS, 8, SPAN), F32),
            pltpu.VMEM((CHUNKS, 8, ROWS), F32),
            pltpu.VMEM((TOK, STATE), BF16),
            pltpu.VMEM((TOK, STATE), BF16),
            pltpu.VMEM((2 * CHUNKS, 2 * SPAN, STATE), F32),
            pltpu.SemaphoreType.DMA((9,)),
            pltpu.SemaphoreType.DMA((8,)),
        ],
        compiler_params=pltpu.CompilerParams(vmem_limit_bytes=FIRST_LIMIT),
        cost_estimate=pl.CostEstimate(flops=800_000_000, bytes_accessed=6_000_000, transcendentals=20_000),
        name="own_states",
    )(x, y, b, c, log)


def scan_kernel(got_ref, out_ref):
    carry = jnp.zeros((SLICE, STATE), F32)
    for k in range(SEQ):
        out_ref[k, :SLICE, :] = carry
        if k < SEQ - 1:
            carry = carry * got_ref[k, 2 * SLICE :, :] + got_ref[k, :SLICE, :]
    carry = jnp.zeros((SLICE, STATE), F32)
    for k in reversed(range(SEQ)):
        out_ref[k, SLICE:, :] = carry
        if k > 0:
            carry = carry * got_ref[k, 2 * SLICE :, :] + got_ref[k, SLICE : 2 * SLICE, :]


def scan_blocks(got):
    return pl.pallas_call(
        scan_kernel,
        in_specs=[pl.BlockSpec(memory_space=pltpu.VMEM)],
        out_shape=jax.ShapeDtypeStruct((SEQ, 2 * SLICE, STATE), F32),
        compiler_params=pltpu.CompilerParams(vmem_limit_bytes=VMEM_LIMIT),
        name="scan_blocks",
    )(got)


def decays(rows_ref, k, mask):
    cin = rows_ref[k, 0:8, :]
    cols = cin.T
    out = []
    for h in range(HEADS_HERE):
        gap = jnp.broadcast_to(cin[h : h + 1, :], (SPAN, SPAN)) - jnp.broadcast_to(
            cols[:, h : h + 1], (SPAN, SPAN)
        )
        out.append(jnp.exp(jnp.where(mask, gap, -1e30)))
    return out


def crosses(xt, y):
    zero = jnp.zeros((WIDTH, SPAN), BF16)
    out = []
    for q in range(HEADS_HERE // 2):
        top = y[2 * q * WIDTH : (2 * q + 1) * WIDTH, :]
        low = y[(2 * q + 1) * WIDTH : (2 * q + 2) * WIDTH, :]
        both = cat([cat([top, zero], 1), cat([zero, low], 1)], 0)
        pair = dot_nn(xt[:, 2 * q * WIDTH : 2 * (q + 1) * WIDTH], both)
        out += [pair[:, :SPAN], pair[:, SPAN:]]
    return out


def inter(near_hi, near_lo, state):
    hi, lo = split2(state)
    return dot_nn(cat([hi, hi, lo], 1), cat([near_hi, near_lo, near_hi], 0))


PER2 = 8


HALF = 256


def by_side(blocks, send_ref, keep_ref):
    second = lax.axis_index("head") % 2 == 1
    for a in range(len(blocks) // 2):
        even, odd = blocks[2 * a], blocks[2 * a + 1]
        send_ref[a] = jnp.where(second, even, odd)
        keep_ref[a] = jnp.where(second, odd, even)


def halves(chunks):
    return [cat([chunks[2 * j], chunks[2 * j + 1]], 1) for j in range(len(chunks) // 2)]


def ascend_kernel(x_ref, y_ref, b_ref, c_ref, rows_ref, lanes_ref, db_ref, send_ref, keep_ref, s_ref, state):
    @pl.when(pl.program_id(0) == 0)
    def _():
        state[...] = jnp.zeros((STATE, ROWS), F32)

    r, l = iotas((SPAN, SPAN))
    mask = l >= r
    own = state[...]
    chunks = []
    for k in range(PER2):
        here = slice(k * SPAN, (k + 1) * SPAN)
        x = x_ref[:, here]
        bt, ct = b_ref[here, :].T, c_ref[here, :].T
        twice = cat([bt, bt], 1)
        total = jnp.zeros((SPAN, SPAN), F32)
        for cross, decay in zip(crosses(x.T, y_ref[:, here]), decays(rows_ref, k, mask)):
            total = total + cross * decay
        hi, lo = split2(total)
        db_ref[:, here] = dot_nt(cat([ct, ct], 1), cat([hi, lo], 1))
        yhi, ylo = split2(y_ref[:, here].astype(F32) * spread_rows(rows_ref[k, 8:16, :]))
        chunks.append(dot_nn(twice, cat([hi, lo], 0)) + inter(yhi, ylo, own))
        s_ref[k * STATE : (k + 1) * STATE, :] = own
        own = own * lanes_ref[k, 0:1, :] + dot_nt(
            twice, wide(x.astype(F32) * spread_rows(rows_ref[k, 16:24, :]))
        )
    state[...] = own
    by_side(halves(chunks), send_ref, keep_ref)


def chunk_specs(per, order):
    return [
        pl.BlockSpec((ROWS, per * SPAN), lambda i: (0, order(i))),
        pl.BlockSpec((ROWS, per * SPAN), lambda i: (0, order(i))),
        pl.BlockSpec((per * SPAN, STATE), lambda i: (order(i), 0)),
        pl.BlockSpec((per * SPAN, STATE), lambda i: (order(i), 0)),
        pl.BlockSpec((per, ROWSET, SPAN), lambda i: (order(i), 0, 0)),
        pl.BlockSpec((per, 8, ROWS), lambda i: (order(i), 0, 0)),
    ]


def side_specs(per, order):
    return [pl.BlockSpec((per // 4, STATE, HALF), lambda i: (order(i), 0, 0))] * 2


def ascend(x, y, b, c, rows, lanes):
    return pl.pallas_call(
        ascend_kernel,
        grid=(CHUNKS // PER2,),
        in_specs=chunk_specs(PER2, lambda i: i),
        out_specs=[pl.BlockSpec((STATE, PER2 * SPAN), lambda i: (0, i))]
        + side_specs(PER2, lambda i: i)
        + [pl.BlockSpec((PER2 * STATE, ROWS), lambda i: (i, 0))],
        out_shape=[jax.ShapeDtypeStruct((STATE, TOK), F32)]
        + [jax.ShapeDtypeStruct((4, STATE, HALF), F32)] * 2
        + [jax.ShapeDtypeStruct((CHUNKS * STATE, ROWS), F32)],
        scratch_shapes=[pltpu.VMEM((STATE, ROWS), F32)],
        compiler_params=pltpu.CompilerParams(vmem_limit_bytes=CHUNK_LIMIT),
        cost_estimate=pl.CostEstimate(flops=3_000_000_000, bytes_accessed=8_000_000, transcendentals=1_000_000),
        name="chunks_ascending",
    )(x, y, b, c, rows, lanes)


PER3 = 8


def descend_kernel(x_ref, y_ref, c_ref, rows_ref, lanes_ref, dbp_ref, send_ref, keep_ref, d_ref, grad):
    @pl.when(pl.program_id(0) == 0)
    def _():
        grad[...] = jnp.zeros((STATE, ROWS), F32)

    back = grad[...]
    chunks = [None] * PER3
    for k in reversed(range(PER3)):
        here = slice(k * SPAN, (k + 1) * SPAN)
        xhi, xlo = split2(x_ref[:, here].astype(F32) * spread_rows(rows_ref[k, 16:24, :]))
        chunks[k] = dbp_ref[:, here] + inter(xhi, xlo, back)
        d_ref[k * STATE : (k + 1) * STATE, :] = back
        ct = c_ref[here, :].T
        back = back * lanes_ref[k, 0:1, :] + dot_nt(
            cat([ct, ct], 1), wide(y_ref[:, here].astype(F32) * spread_rows(rows_ref[k, 8:16, :]))
        )
    grad[...] = back
    by_side(halves(chunks), send_ref, keep_ref)


def descend(x, y, c, rows, lanes, dbp):
    steps = CHUNKS // PER3
    order = lambda i: steps - 1 - i
    specs = chunk_specs(PER3, order)
    tokens = pl.BlockSpec((STATE, PER3 * SPAN), lambda i: (0, order(i)))
    states = pl.BlockSpec((PER3 * STATE, ROWS), lambda i: (order(i), 0))
    return pl.pallas_call(
        descend_kernel,
        grid=(steps,),
        in_specs=specs[:2] + specs[3:] + [tokens],
        out_specs=side_specs(PER3, order) + [states],
        out_shape=[
            jax.ShapeDtypeStruct((4, STATE, HALF), F32),
            jax.ShapeDtypeStruct((4, STATE, HALF), F32),
            jax.ShapeDtypeStruct((CHUNKS * STATE, ROWS), F32),
        ],
        scratch_shapes=[pltpu.VMEM((STATE, ROWS), F32)],
        compiler_params=pltpu.CompilerParams(vmem_limit_bytes=DOWN_LIMIT),
        cost_estimate=pl.CostEstimate(flops=3_000_000_000, bytes_accessed=8_000_000, transcendentals=0),
        name="chunks_descending",
    )(x, y, c, rows, lanes, dbp)


def blocks_of(side, place, row, bound_ref, edge_ref, src, held):
    index = lax.axis_index("head")
    chip, core = index // 2, index % 2
    edge = split2(from_slices(bound_ref, place))
    stack = cat(list(edge), 0)
    for i in range(4):
        to = jnp.bitwise_xor(chip, i)
        block = 2 * to + jnp.bitwise_xor(core, side)
        cols = pl.ds(pl.multiple_of(block * HALF, HALF), HALF)
        scale = cat(
            [spread_rows(edge_ref[2 * block + k, row : row + HEADS_HERE, :]) for k in range(2)], 1
        )
        near_hi, near_lo = split2(src[:, cols].astype(F32) * scale)
        first = dot_nn(stack, near_hi)
        yield i, held[to] + (first[:STATE] + (first[STATE:] + dot_nn(edge[0], near_lo)))


def send_out_kernel(bound_ref, edge_ref, y_ref, held_ref, out_ref):
    for i, block in blocks_of(1, 0, 0, bound_ref, edge_ref, y_ref, held_ref):
        out_ref[i] = block


def send_in_kernel(bound_ref, edge_ref, x_ref, held_ref, far_ref, own_ref):
    for i, block in blocks_of(1, SLICE, HEADS_HERE, bound_ref, edge_ref, x_ref, held_ref):
        if i == 0:
            own_ref[...] = block
        else:
            far_ref[i - 1] = block


def keep_kernel(bound_ref, edge_ref, x_ref, y_ref, in_ref, out_ref, kept_ref):
    for i, block in blocks_of(0, SLICE, HEADS_HERE, bound_ref, edge_ref, x_ref, in_ref):
        kept_ref[i, 0] = block
    for i, block in blocks_of(0, 0, 0, bound_ref, edge_ref, y_ref, out_ref):
        kept_ref[i, 1] = block


def sum_kernel(kept_ref, out_ref, in_ref, *outs):
    second = lax.axis_index("head") % 2
    own_ref, rest = outs[0], outs[1:]
    own_ref[0] = kept_ref[0, 0]
    own_ref[1] = kept_ref[0, 1] + out_ref[0]
    for ref, m in zip(rest, (1 + 2 * second, 3 - 2 * second, 2)):
        ref[0] = kept_ref[m, 0] + in_ref[m - 1]
        ref[1] = kept_ref[m, 1] + out_ref[m]


def in_vmem(name, kernel, shapes, *operands):
    vmem = pl.BlockSpec(memory_space=pltpu.VMEM)
    return pl.pallas_call(
        kernel,
        in_specs=[vmem] * len(operands),
        out_specs=[vmem] * len(shapes),
        out_shape=[jax.ShapeDtypeStruct(shape, F32) for shape in shapes],
        compiler_params=pltpu.CompilerParams(vmem_limit_bytes=PART_LIMIT),
        cost_estimate=pl.CostEstimate(flops=500_000_000, bytes_accessed=3_000_000, transcendentals=0),
        name=name,
    )(*operands)


PER5 = 4


def last_kernel(x_ref, y_ref, b_ref, c_ref, rows_ref, lanes_ref, bound_ref, s_ref, d_ref, dx_ref, dl_ref):
    entering = from_slices(bound_ref, 0)
    leaving = from_slices(bound_ref, SLICE)
    r, l = iotas((SPAN, SPAN))
    mask = l >= r
    later = cat([ones_where(r >= l)] * 3, 0)
    every = jnp.ones((3 * (SPAN + ROWS), SPAN), BF16)
    owner_row, owner_lane = iotas((HEADS_HERE, ROWS))
    owned = owner_lane // WIDTH == owner_row
    for k in range(PER5):
        here = slice(k * SPAN, (k + 1) * SPAN)
        states = slice(k * STATE, (k + 1) * STATE)
        x, y, b, c = x_ref[:, here], y_ref[:, here], b_ref[here, :], c_ref[here, :]
        scores = dot_nt(b, c)
        s = s_ref[states, :] + lanes_ref[k, 1:2, :] * entering
        d = d_ref[states, :] + lanes_ref[k, 2:3, :] * leaving
        dhi, dlo = split2(d)
        shi, slo = split2(s)
        u = dot_nt(cat([dhi.T, dlo.T], 1), cat([b, b], 1)) * spread_rows(rows_ref[k, 16:24, :])
        z = dot_nt(cat([shi.T, slo.T], 1), cat([c, c], 1))
        row, inner = [], []
        for h, (cross, decay) in enumerate(zip(crosses(x.T, y), decays(rows_ref, k, mask))):
            weight = scores * decay
            yh = y[h * WIDTH : (h + 1) * WIDTH, :]
            inner.append(dot_nt(cat([yh, yh], 1), wide(weight)))
            row.append(jnp.sum(weight * cross, axis=0, keepdims=True))
        dx = cat(inner, 0) + u
        dx_ref[:, here] = dx.astype(BF16)
        xf = x.astype(F32)
        pending = (
            cat(row, 0)
            + rows_ref[k, 8 : 8 + HEADS_HERE, :] * head_sums(z * y.astype(F32))
            - head_sums(xf * dx)
        )
        meet = jnp.where(owned, jnp.sum(s * d, axis=0, keepdims=True), 0.0) * cat(
            [rows_ref[k, 24 : 24 + HEADS_HERE, :]] * 2, 1
        )
        through = cat([head_sums(xf * u), meet], 1)
        dl_ref[:, here] = dot_nn(cat(list(split3(pending)), 1), later) + dot_nn(
            cat(list(split3(through)), 1), every
        )


def last_pass(x, y, b, c, rows, lanes, bound, s, d):
    states = pl.BlockSpec((PER5 * STATE, ROWS), lambda i: (i, 0))
    return pl.pallas_call(
        last_kernel,
        grid=(CHUNKS // PER5,),
        in_specs=chunk_specs(PER5, lambda i: i)
        + [
            pl.BlockSpec((SEQ, 2 * SLICE, STATE), lambda i: (0, 0, 0)),
            states,
            states,
        ],
        out_specs=[
            pl.BlockSpec((ROWS, PER5 * SPAN), lambda i: (0, i)),
            pl.BlockSpec((HEADS_HERE, PER5 * SPAN), lambda i: (0, i)),
        ],
        out_shape=[
            jax.ShapeDtypeStruct((ROWS, TOK), BF16),
            jax.ShapeDtypeStruct((HEADS_HERE, TOK), F32),
        ],
        compiler_params=pltpu.CompilerParams(vmem_limit_bytes=LAST_LIMIT),
        cost_estimate=pl.CostEstimate(flops=6_000_000_000, bytes_accessed=12_000_000, transcendentals=1_000_000),
        name="inputs_and_decay",
    )(x, y, b, c, rows, lanes, bound, s, d)


def merge_kernel(own_ref, late_ref, one_ref, two_ref, far_ref, in_ref, out_ref):
    index = lax.axis_index("head")
    group, second = index // 4, index % 2 == 1
    for t, ref in enumerate((in_ref, out_ref)):
        one, two = one_ref[t], two_ref[t]
        own = own_ref[t] + jnp.where(second, two, one)
        if t == 0:
            own = own + late_ref[...]
        ref[pl.ds(group, HALF, stride=2), :] = own.T
        ref[pl.ds(1 - group, HALF, stride=2), :] = (far_ref[t] + jnp.where(second, one, two)).T


def local(inputs, log_decay, in_proj, out_proj, upstream):
    x = jnp.transpose(inputs, (1, 2, 0)).reshape(ROWS, TOK)
    y = jnp.transpose(upstream, (1, 2, 0)).reshape(ROWS, TOK)
    log = jnp.transpose(log_decay)
    b2 = in_proj.reshape(2 * TOK, STATE)
    c2 = out_proj.reshape(2 * TOK, STATE)
    message, rows, edge, lanes, b, c = first_pass(x, y, b2, c2, log)
    got = lax.all_to_all(message, "seq", 0, 0)
    dbp, dc_send, dc_keep, s = ascend(x, y, b, c, rows, lanes)
    got, dbp = lax.optimization_barrier((got, dbp))
    bound = lax.all_to_all(scan_blocks(got), "seq", 0, 0)
    db_send, db_keep, d = descend(x, y, c, rows, lanes, dbp)
    bound, d = lax.optimization_barrier((bound, d))
    pair = [(i, i ^ 1) for i in range(8)]
    block = (STATE, HALF)
    (sent_out,) = in_vmem("out_send", send_out_kernel, [(4, *block)], bound, edge, y, dc_send)
    got_out = lax.ppermute(sent_out, "head", pair)
    db_send, sent_out = lax.optimization_barrier((db_send, sent_out))
    sent_in, sent_own = in_vmem(
        "in_send", send_in_kernel, [(3, *block), block], bound, edge, x, db_send
    )
    got_in = lax.ppermute(sent_in, "head", pair)
    dc_keep, sent_in = lax.optimization_barrier((dc_keep, sent_in))
    (kept,) = in_vmem(
        "keep", keep_kernel, [(4, 2, *block)], bound, edge, x, y, db_keep, dc_keep
    )
    parts = in_vmem("sum_cores", sum_kernel, [(2, *block)] * 4, kept, got_out, got_in)
    hops = [(2, 6), (6, 2), (4, 4)]
    moved = [
        lax.ppermute(part, "head", [(i, i ^ hop[i % 2]) for i in range(8)])
        for part, hop in zip(parts[1:], hops)
    ]
    grad_x, grad_log = last_pass(x, y, b, c, rows, lanes, bound, s, d)
    sent_own, grad_log = lax.optimization_barrier((sent_own, grad_log))
    late = lax.ppermute(sent_own, "head", pair)
    grad_in, grad_out = in_vmem(
        "merge", merge_kernel, [(2 * HALF, STATE)] * 2, parts[0], late, *moved
    )
    return (
        jnp.transpose(grad_x.reshape(HEADS_HERE, WIDTH, TOK), (2, 0, 1)),
        jnp.transpose(grad_log),
        grad_in.reshape(HALF, 2, STATE),
        grad_out.reshape(HALF, 2, STATE),
    )


def solution(mesh):
    in_specs = (
        P("seq", "head", None),
        P("seq", "head"),
        P("seq", None, None),
        P("seq", None, None),
        P("seq", "head", None),
    )
    out_specs = (
        P("seq", "head", None),
        P("seq", "head"),
        P(("seq", "head"), None, None),
        P(("seq", "head"), None, None),
    )
    return jax.shard_map(local, mesh=mesh, in_specs=in_specs, out_specs=out_specs, check_vma=False)
```

```python
import functools

import jax
import jax.numpy as jnp
from jax import lax
from jax.experimental import pallas as pl
from jax.experimental.pallas import tpu as pltpu
from jax.sharding import PartitionSpec as P

HEADS_HERE = 4
WIDTH = 64
STATE = 128
SPAN = 128
TOK = 2048
CHUNKS = TOK // SPAN
ROWS = HEADS_HERE * WIDTH
SEQ = 32
SLICE = ROWS // SEQ
F32 = jnp.float32
BF16 = jnp.bfloat16
FIRST_LIMIT = 60 * 1024 * 1024
PART_LIMIT = 40 * 1024 * 1024
LAST_LIMIT = 40 * 1024 * 1024
CHUNK_LIMIT = 60 * 1024 * 1024
DOWN_LIMIT = 60 * 1024 * 1024
VMEM_LIMIT = 24 * 1024 * 1024


def dot_nn(a, b):
    return lax.dot_general(a, b, (((1,), (0,)), ((), ())), preferred_element_type=F32)


def dot_nt(a, b):
    return lax.dot_general(a, b, (((1,), (1,)), ((), ())), preferred_element_type=F32)


def split2(x):
    hi = x.astype(BF16)
    return hi, (x - hi.astype(F32)).astype(BF16)


def split3(x):
    a = x.astype(BF16)
    rest = x - a.astype(F32)
    b = rest.astype(BF16)
    return a, b, (rest - b.astype(F32)).astype(BF16)


def cat(parts, axis):
    return jnp.concatenate(parts, axis=axis)


def wide(x):
    hi, lo = split2(x)
    return cat([hi, lo], 1)


def iotas(shape):
    return lax.broadcasted_iota(jnp.int32, shape, 0), lax.broadcasted_iota(jnp.int32, shape, 1)


def ones_where(mask):
    return jnp.where(mask, 1.0, 0.0).astype(BF16)


def pad_heads(x):
    return cat([x, jnp.zeros((8 - HEADS_HERE, x.shape[1]), F32)], 0)


def spread_rows(rows):
    return cat(
        [jnp.broadcast_to(rows[h : h + 1, :], (WIDTH, SPAN)) for h in range(HEADS_HERE)], 0
    )


def head_sums(x):
    return cat(
        [
            jnp.sum(x[h * WIDTH : (h + 1) * WIDTH, :], axis=0, keepdims=True)
            for h in range(HEADS_HERE)
        ],
        0,
    )


def by_head(rows):
    lane = lax.broadcasted_iota(jnp.int32, (1, 2 * WIDTH), 1)
    return cat(
        [
            jnp.where(lane < WIDTH, rows[2 * q : 2 * q + 1, :], rows[2 * q + 1 : 2 * q + 2, :])
            for q in range(HEADS_HERE // 2)
        ],
        1,
    )


def to_slices(x, ref, place):
    for a in range(STATE // SLICE):
        for q in range(2):
            ref[2 * a + q, place : place + SLICE, :] = x[
                a * SLICE : (a + 1) * SLICE, q * STATE : (q + 1) * STATE
            ]


def from_slices(ref, place):
    return cat(
        [
            cat([ref[2 * a + q, place : place + SLICE, :] for q in range(2)], 1)
            for a in range(STATE // SLICE)
        ],
        0,
    )


ROWSET = 32


def choose(x, ref, group):
    ref[...] = x.astype(F32)
    return ref[pl.ds(group, SPAN, stride=2), :].astype(BF16)


def row_tables(log_ref, rows_ref, edge_ref, lanes_ref, msg_ref):
    r, c = iotas((SPAN, SPAN))
    tri = cat([ones_where(r <= c), ones_where(r > c), jnp.ones((SPAN, SPAN), BF16)], 1)
    tri = cat([tri] * 3, 0)
    stacked = cat(
        [
            cat(list(split3(pad_heads(log_ref[:, k * SPAN : (k + 1) * SPAN]))), 1)
            for k in range(CHUNKS)
        ],
        0,
    )
    sums = dot_nn(stacked, tri)
    tot = [sums[8 * k : 8 * k + 8, 2 * SPAN :] for k in range(CHUNKS)]
    before = jnp.zeros((8, SPAN), F32)
    for k in range(CHUNKS):
        cin = sums[8 * k : 8 * k + 8, :SPAN]
        rows_ref[k, 0:8, :] = cin
        rows_ref[k, 8:16, :] = jnp.exp(cin)
        rows_ref[k, 16:24, :] = jnp.exp(sums[8 * k : 8 * k + 8, SPAN : 2 * SPAN])
        whole = jnp.exp(tot[k])
        rows_ref[k, 24:32, :] = whole
        edge_ref[k, :HEADS_HERE, :] = jnp.exp(before + cin)[:HEADS_HERE]
        lanes_ref[k, 0:1, :] = by_head(whole)
        lanes_ref[k, 1:2, :] = by_head(jnp.exp(before))
        before = before + tot[k]
    after = jnp.zeros((8, SPAN), F32)
    for k in reversed(range(CHUNKS)):
        edge_ref[k, HEADS_HERE:, :] = jnp.exp(after + sums[8 * k : 8 * k + 8, SPAN : 2 * SPAN])[
            :HEADS_HERE
        ]
        lanes_ref[k, 2:3, :] = by_head(jnp.exp(after))
        lanes_ref[k, 3:8, :] = jnp.zeros((5, ROWS), F32)
        after = after + tot[k]
    to_slices(jnp.broadcast_to(by_head(jnp.exp(before)), (STATE, ROWS)), msg_ref, 2 * SLICE)


def first_kernel(
    x_hbm, y_hbm, b_hbm, c_hbm, log_hbm, msg_hbm, rows_hbm, edge_hbm, lanes_hbm, bs_hbm, cs_hbm,
    x_ref, y_ref, b_ref, c_ref, log_ref, msg_ref, rows_ref, edge_ref, lanes_ref, bs_ref, cs_ref, wide_ref,
    get_sem, put_sem
):
    gets = [pltpu.make_async_copy(log_hbm, log_ref, get_sem.at[0])]
    for q in range(2):
        rows, cols = pl.ds(q * TOK, TOK), pl.ds(q * TOK // 2, TOK // 2)
        for src, dst, part in (
            (b_hbm, b_ref, (rows, slice(None))),
            (x_hbm, x_ref, (slice(None), cols)),
            (c_hbm, c_ref, (rows, slice(None))),
            (y_hbm, y_ref, (slice(None), cols)),
        ):
            gets.append(
                pltpu.make_async_copy(src.at[part], dst.at[part], get_sem.at[len(gets)])
            )
    for copy in gets:
        copy.start()
    puts = []

    def put(src, dst):
        copy = pltpu.make_async_copy(src, dst, put_sem.at[len(puts)])
        copy.start()
        puts.append(copy)

    def put_message(place):
        part = pl.ds(place, SLICE)
        put(msg_ref.at[:, part, :], msg_hbm.at[:, part, :])

    group = lax.axis_index("head") // 4
    gets[0].wait()
    row_tables(log_ref, rows_ref, edge_ref, lanes_ref, msg_ref)
    put(rows_ref, rows_hbm)
    put(edge_ref, edge_hbm)
    put(lanes_ref, lanes_hbm)
    put_message(2 * SLICE)

    def gather(total, base, k, pairs_ref, chosen_ref, src, row):
        got = choose(pairs_ref[2 * k * SPAN : 2 * (k + 1) * SPAN, :], wide_ref.at[base + k], group)
        chosen_ref[k * SPAN : (k + 1) * SPAN, :] = got
        turned = got.T
        near = src[:, k * SPAN : (k + 1) * SPAN].astype(F32) * spread_rows(
            edge_ref[k, row : row + HEADS_HERE, :]
        )
        return total + dot_nt(cat([turned, turned], 1), wide(near))

    own = jnp.zeros((STATE, ROWS), F32)
    back = jnp.zeros((STATE, ROWS), F32)
    for q in range(2):
        chunks = range(q * CHUNKS // 2, (q + 1) * CHUNKS // 2)
        gets[4 * q + 1].wait()
        gets[4 * q + 2].wait()
        for k in chunks:
            own = gather(own, 0, k, b_ref, bs_ref, x_ref, HEADS_HERE)
        if q == 1:
            put(bs_ref, bs_hbm)
            to_slices(own, msg_ref, 0)
            put_message(0)
        gets[4 * q + 3].wait()
        gets[4 * q + 4].wait()
        for k in chunks:
            back = gather(back, CHUNKS, k, c_ref, cs_ref, y_ref, 0)
    put(cs_ref, cs_hbm)
    to_slices(back, msg_ref, SLICE)
    put_message(SLICE)
    for copy in puts:
        copy.wait()


def first_pass(x, y, b, c, log):
    hbm = pl.BlockSpec(memory_space=pltpu.HBM)
    return pl.pallas_call(
        first_kernel,
        in_specs=[hbm] * 5,
        out_specs=[hbm] * 6,
        out_shape=[
            jax.ShapeDtypeStruct((SEQ, 3 * SLICE, STATE), F32),
            jax.ShapeDtypeStruct((CHUNKS, ROWSET, SPAN), F32),
            jax.ShapeDtypeStruct((CHUNKS, 8, SPAN), F32),
            jax.ShapeDtypeStruct((CHUNKS, 8, ROWS), F32),
            jax.ShapeDtypeStruct((TOK, STATE), BF16),
            jax.ShapeDtypeStruct((TOK, STATE), BF16),
        ],
        scratch_shapes=[
            pltpu.VMEM((ROWS, TOK), BF16),
            pltpu.VMEM((ROWS, TOK), BF16),
            pltpu.VMEM((2 * TOK, STATE), BF16),
            pltpu.VMEM((2 * TOK, STATE), BF16),
            pltpu.VMEM((HEADS_HERE, TOK), F32),
            pltpu.VMEM((SEQ, 3 * SLICE, STATE), F32),
            pltpu.VMEM((CHUNKS, ROWSET, SPAN), F32),
            pltpu.VMEM((CHUNKS, 8, SPAN), F32),
            pltpu.VMEM((CHUNKS, 8, ROWS), F32),
            pltpu.VMEM((TOK, STATE), BF16),
            pltpu.VMEM((TOK, STATE), BF16),
            pltpu.VMEM((2 * CHUNKS, 2 * SPAN, STATE), F32),
            pltpu.SemaphoreType.DMA((9,)),
            pltpu.SemaphoreType.DMA((8,)),
        ],
        compiler_params=pltpu.CompilerParams(vmem_limit_bytes=FIRST_LIMIT),
        cost_estimate=pl.CostEstimate(flops=800_000_000, bytes_accessed=6_000_000, transcendentals=20_000),
        name="own_states",
    )(x, y, b, c, log)


def scan_kernel(got_ref, out_ref):
    carry = jnp.zeros((SLICE, STATE), F32)
    for k in range(SEQ):
        out_ref[k, :SLICE, :] = carry
        if k < SEQ - 1:
            carry = carry * got_ref[k, 2 * SLICE :, :] + got_ref[k, :SLICE, :]
    carry = jnp.zeros((SLICE, STATE), F32)
    for k in reversed(range(SEQ)):
        out_ref[k, SLICE:, :] = carry
        if k > 0:
            carry = carry * got_ref[k, 2 * SLICE :, :] + got_ref[k, SLICE : 2 * SLICE, :]


def scan_blocks(got):
    return pl.pallas_call(
        scan_kernel,
        in_specs=[pl.BlockSpec(memory_space=pltpu.VMEM)],
        out_shape=jax.ShapeDtypeStruct((SEQ, 2 * SLICE, STATE), F32),
        compiler_params=pltpu.CompilerParams(vmem_limit_bytes=VMEM_LIMIT),
        name="scan_blocks",
    )(got)


def decays(rows_ref, k, mask):
    cin = rows_ref[k, 0:8, :]
    cols = cin.T
    out = []
    for h in range(HEADS_HERE):
        gap = jnp.broadcast_to(cin[h : h + 1, :], (SPAN, SPAN)) - jnp.broadcast_to(
            cols[:, h : h + 1], (SPAN, SPAN)
        )
        out.append(jnp.exp(jnp.where(mask, gap, -1e30)))
    return out


def crosses(xt, y):
    zero = jnp.zeros((WIDTH, SPAN), BF16)
    out = []
    for q in range(HEADS_HERE // 2):
        top = y[2 * q * WIDTH : (2 * q + 1) * WIDTH, :]
        low = y[(2 * q + 1) * WIDTH : (2 * q + 2) * WIDTH, :]
        both = cat([cat([top, zero], 1), cat([zero, low], 1)], 0)
        pair = dot_nn(xt[:, 2 * q * WIDTH : 2 * (q + 1) * WIDTH], both)
        out += [pair[:, :SPAN], pair[:, SPAN:]]
    return out


def inter(near_hi, near_lo, state):
    hi, lo = split2(state)
    return dot_nn(cat([hi, hi, lo], 1), cat([near_hi, near_lo, near_hi], 0))


PER2 = 8


HALF = 256


def by_side(blocks, send_ref, keep_ref):
    second = lax.axis_index("head") % 2 == 1
    for a in range(len(blocks) // 2):
        even, odd = blocks[2 * a], blocks[2 * a + 1]
        send_ref[a] = jnp.where(second, even, odd)
        keep_ref[a] = jnp.where(second, odd, even)


def halves(chunks):
    return [cat([chunks[2 * j], chunks[2 * j + 1]], 1) for j in range(len(chunks) // 2)]


def ascend_kernel(x_ref, y_ref, b_ref, c_ref, rows_ref, lanes_ref, db_ref, send_ref, keep_ref, s_ref, state):
    @pl.when(pl.program_id(0) == 0)
    def _():
        state[...] = jnp.zeros((STATE, ROWS), F32)

    r, l = iotas((SPAN, SPAN))
    mask = l >= r
    own = state[...]
    chunks = []
    for k in range(PER2):
        here = slice(k * SPAN, (k + 1) * SPAN)
        x = x_ref[:, here]
        bt, ct = b_ref[here, :].T, c_ref[here, :].T
        twice = cat([bt, bt], 1)
        total = jnp.zeros((SPAN, SPAN), F32)
        for cross, decay in zip(crosses(x.T, y_ref[:, here]), decays(rows_ref, k, mask)):
            total = total + cross * decay
        hi, lo = split2(total)
        db_ref[:, here] = dot_nt(cat([ct, ct], 1), cat([hi, lo], 1))
        yhi, ylo = split2(y_ref[:, here].astype(F32) * spread_rows(rows_ref[k, 8:16, :]))
        chunks.append(dot_nn(twice, cat([hi, lo], 0)) + inter(yhi, ylo, own))
        s_ref[k * STATE : (k + 1) * STATE, :] = own
        own = own * lanes_ref[k, 0:1, :] + dot_nt(
            twice, wide(x.astype(F32) * spread_rows(rows_ref[k, 16:24, :]))
        )
    state[...] = own
    by_side(halves(chunks), send_ref, keep_ref)


def chunk_specs(per, order):
    return [
        pl.BlockSpec((ROWS, per * SPAN), lambda i: (0, order(i))),
        pl.BlockSpec((ROWS, per * SPAN), lambda i: (0, order(i))),
        pl.BlockSpec((per * SPAN, STATE), lambda i: (order(i), 0)),
        pl.BlockSpec((per * SPAN, STATE), lambda i: (order(i), 0)),
        pl.BlockSpec((per, ROWSET, SPAN), lambda i: (order(i), 0, 0)),
        pl.BlockSpec((per, 8, ROWS), lambda i: (order(i), 0, 0)),
    ]


def side_specs(per, order):
    return [pl.BlockSpec((per // 4, STATE, HALF), lambda i: (order(i), 0, 0))] * 2


def ascend(x, y, b, c, rows, lanes):
    return pl.pallas_call(
        ascend_kernel,
        grid=(CHUNKS // PER2,),
        in_specs=chunk_specs(PER2, lambda i: i),
        out_specs=[pl.BlockSpec((STATE, PER2 * SPAN), lambda i: (0, i))]
        + side_specs(PER2, lambda i: i)
        + [pl.BlockSpec((PER2 * STATE, ROWS), lambda i: (i, 0))],
        out_shape=[jax.ShapeDtypeStruct((STATE, TOK), F32)]
        + [jax.ShapeDtypeStruct((4, STATE, HALF), F32)] * 2
        + [jax.ShapeDtypeStruct((CHUNKS * STATE, ROWS), F32)],
        scratch_shapes=[pltpu.VMEM((STATE, ROWS), F32)],
        compiler_params=pltpu.CompilerParams(vmem_limit_bytes=CHUNK_LIMIT),
        cost_estimate=pl.CostEstimate(flops=3_000_000_000, bytes_accessed=8_000_000, transcendentals=1_000_000),
        name="chunks_ascending",
    )(x, y, b, c, rows, lanes)


PER3 = 8


def descend_kernel(x_ref, y_ref, c_ref, rows_ref, lanes_ref, dbp_ref, send_ref, keep_ref, d_ref, grad):
    @pl.when(pl.program_id(0) == 0)
    def _():
        grad[...] = jnp.zeros((STATE, ROWS), F32)

    back = grad[...]
    chunks = [None] * PER3
    for k in reversed(range(PER3)):
        here = slice(k * SPAN, (k + 1) * SPAN)
        xhi, xlo = split2(x_ref[:, here].astype(F32) * spread_rows(rows_ref[k, 16:24, :]))
        chunks[k] = dbp_ref[:, here] + inter(xhi, xlo, back)
        d_ref[k * STATE : (k + 1) * STATE, :] = back
        ct = c_ref[here, :].T
        back = back * lanes_ref[k, 0:1, :] + dot_nt(
            cat([ct, ct], 1), wide(y_ref[:, here].astype(F32) * spread_rows(rows_ref[k, 8:16, :]))
        )
    grad[...] = back
    by_side(halves(chunks), send_ref, keep_ref)


def descend(x, y, c, rows, lanes, dbp):
    steps = CHUNKS // PER3
    order = lambda i: steps - 1 - i
    specs = chunk_specs(PER3, order)
    tokens = pl.BlockSpec((STATE, PER3 * SPAN), lambda i: (0, order(i)))
    states = pl.BlockSpec((PER3 * STATE, ROWS), lambda i: (order(i), 0))
    return pl.pallas_call(
        descend_kernel,
        grid=(steps,),
        in_specs=specs[:2] + specs[3:] + [tokens],
        out_specs=side_specs(PER3, order) + [states],
        out_shape=[
            jax.ShapeDtypeStruct((4, STATE, HALF), F32),
            jax.ShapeDtypeStruct((4, STATE, HALF), F32),
            jax.ShapeDtypeStruct((CHUNKS * STATE, ROWS), F32),
        ],
        scratch_shapes=[pltpu.VMEM((STATE, ROWS), F32)],
        compiler_params=pltpu.CompilerParams(vmem_limit_bytes=DOWN_LIMIT),
        cost_estimate=pl.CostEstimate(flops=3_000_000_000, bytes_accessed=8_000_000, transcendentals=0),
        name="chunks_descending",
    )(x, y, c, rows, lanes, dbp)


def blocks_of(side, place, row, bound_ref, edge_ref, src, held):
    index = lax.axis_index("head")
    chip, core = index // 2, index % 2
    edge = split2(from_slices(bound_ref, place))
    stack = cat(list(edge), 0)
    for i in range(4):
        to = jnp.bitwise_xor(chip, i)
        block = 2 * to + jnp.bitwise_xor(core, side)
        cols = pl.ds(pl.multiple_of(block * HALF, HALF), HALF)
        scale = cat(
            [spread_rows(edge_ref[2 * block + k, row : row + HEADS_HERE, :]) for k in range(2)], 1
        )
        near_hi, near_lo = split2(src[:, cols].astype(F32) * scale)
        first = dot_nn(stack, near_hi)
        yield i, held[to] + (first[:STATE] + (first[STATE:] + dot_nn(edge[0], near_lo)))


def send_out_kernel(bound_ref, edge_ref, y_ref, held_ref, far_ref, own_ref):
    for i, block in blocks_of(1, 0, 0, bound_ref, edge_ref, y_ref, held_ref):
        if i == 0:
            own_ref[...] = block
        else:
            far_ref[i - 1] = block


def send_in_kernel(bound_ref, edge_ref, x_ref, held_ref, far_ref, own_ref):
    for i, block in blocks_of(1, SLICE, HEADS_HERE, bound_ref, edge_ref, x_ref, held_ref):
        if i == 0:
            own_ref[...] = block
        else:
            far_ref[i - 1] = block


def keep_kernel(bound_ref, edge_ref, x_ref, y_ref, in_ref, out_ref, kept_ref):
    for i, block in blocks_of(0, SLICE, HEADS_HERE, bound_ref, edge_ref, x_ref, in_ref):
        kept_ref[i, 0] = block
    for i, block in blocks_of(0, 0, 0, bound_ref, edge_ref, y_ref, out_ref):
        kept_ref[i, 1] = block


def sum_kernel(kept_ref, out_ref, in_ref, *outs):
    second = lax.axis_index("head") % 2
    own_ref, rest = outs[0], outs[1:]
    own_ref[0] = kept_ref[0, 0]
    own_ref[1] = kept_ref[0, 1]
    for ref, m in zip(rest, (1 + 2 * second, 3 - 2 * second, 2)):
        ref[0] = kept_ref[m, 0] + in_ref[m - 1]
        ref[1] = kept_ref[m, 1] + out_ref[m - 1]


def in_vmem(name, kernel, shapes, *operands):
    vmem = pl.BlockSpec(memory_space=pltpu.VMEM)
    return pl.pallas_call(
        kernel,
        in_specs=[vmem] * len(operands),
        out_specs=[vmem] * len(shapes),
        out_shape=[jax.ShapeDtypeStruct(shape, F32) for shape in shapes],
        compiler_params=pltpu.CompilerParams(vmem_limit_bytes=PART_LIMIT),
        cost_estimate=pl.CostEstimate(flops=500_000_000, bytes_accessed=3_000_000, transcendentals=0),
        name=name,
    )(*operands)


PER5 = 4


def last_kernel(x_ref, y_ref, b_ref, c_ref, rows_ref, lanes_ref, bound_ref, s_ref, d_ref, dx_ref, dl_ref):
    entering = from_slices(bound_ref, 0)
    leaving = from_slices(bound_ref, SLICE)
    r, l = iotas((SPAN, SPAN))
    mask = l >= r
    later = cat([ones_where(r >= l)] * 3, 0)
    every = jnp.ones((3 * (SPAN + ROWS), SPAN), BF16)
    owner_row, owner_lane = iotas((HEADS_HERE, ROWS))
    owned = owner_lane // WIDTH == owner_row
    for k in range(PER5):
        here = slice(k * SPAN, (k + 1) * SPAN)
        states = slice(k * STATE, (k + 1) * STATE)
        x, y, b, c = x_ref[:, here], y_ref[:, here], b_ref[here, :], c_ref[here, :]
        scores = dot_nt(b, c)
        s = s_ref[states, :] + lanes_ref[k, 1:2, :] * entering
        d = d_ref[states, :] + lanes_ref[k, 2:3, :] * leaving
        dhi, dlo = split2(d)
        shi, slo = split2(s)
        u = dot_nt(cat([dhi.T, dlo.T], 1), cat([b, b], 1)) * spread_rows(rows_ref[k, 16:24, :])
        z = dot_nt(cat([shi.T, slo.T], 1), cat([c, c], 1))
        row, inner = [], []
        for h, (cross, decay) in enumerate(zip(crosses(x.T, y), decays(rows_ref, k, mask))):
            weight = scores * decay
            yh = y[h * WIDTH : (h + 1) * WIDTH, :]
            inner.append(dot_nt(cat([yh, yh], 1), wide(weight)))
            row.append(jnp.sum(weight * cross, axis=0, keepdims=True))
        dx = cat(inner, 0) + u
        dx_ref[:, here] = dx.astype(BF16)
        xf = x.astype(F32)
        pending = (
            cat(row, 0)
            + rows_ref[k, 8 : 8 + HEADS_HERE, :] * head_sums(z * y.astype(F32))
            - head_sums(xf * dx)
        )
        meet = jnp.where(owned, jnp.sum(s * d, axis=0, keepdims=True), 0.0) * cat(
            [rows_ref[k, 24 : 24 + HEADS_HERE, :]] * 2, 1
        )
        through = cat([head_sums(xf * u), meet], 1)
        dl_ref[:, here] = dot_nn(cat(list(split3(pending)), 1), later) + dot_nn(
            cat(list(split3(through)), 1), every
        )


def last_pass(x, y, b, c, rows, lanes, bound, s, d):
    states = pl.BlockSpec((PER5 * STATE, ROWS), lambda i: (i, 0))
    return pl.pallas_call(
        last_kernel,
        grid=(CHUNKS // PER5,),
        in_specs=chunk_specs(PER5, lambda i: i)
        + [
            pl.BlockSpec((SEQ, 2 * SLICE, STATE), lambda i: (0, 0, 0)),
            states,
            states,
        ],
        out_specs=[
            pl.BlockSpec((ROWS, PER5 * SPAN), lambda i: (0, i)),
            pl.BlockSpec((HEADS_HERE, PER5 * SPAN), lambda i: (0, i)),
        ],
        out_shape=[
            jax.ShapeDtypeStruct((ROWS, TOK), BF16),
            jax.ShapeDtypeStruct((HEADS_HERE, TOK), F32),
        ],
        compiler_params=pltpu.CompilerParams(vmem_limit_bytes=LAST_LIMIT),
        cost_estimate=pl.CostEstimate(flops=6_000_000_000, bytes_accessed=12_000_000, transcendentals=1_000_000),
        name="inputs_and_decay",
    )(x, y, b, c, rows, lanes, bound, s, d)


def merge_kernel(own_ref, late_in_ref, late_out_ref, one_ref, two_ref, far_ref, in_ref, out_ref):
    index = lax.axis_index("head")
    group, second = index // 4, index % 2 == 1
    for t, ref in enumerate((in_ref, out_ref)):
        one, two = one_ref[t], two_ref[t]
        own = own_ref[t] + jnp.where(second, two, one)
        own = own + (late_out_ref if t else late_in_ref)[...]
        ref[pl.ds(group, HALF, stride=2), :] = own.T
        ref[pl.ds(1 - group, HALF, stride=2), :] = (far_ref[t] + jnp.where(second, one, two)).T


def local(inputs, log_decay, in_proj, out_proj, upstream):
    x = jnp.transpose(inputs, (1, 2, 0)).reshape(ROWS, TOK)
    y = jnp.transpose(upstream, (1, 2, 0)).reshape(ROWS, TOK)
    log = jnp.transpose(log_decay)
    b2 = in_proj.reshape(2 * TOK, STATE)
    c2 = out_proj.reshape(2 * TOK, STATE)
    message, rows, edge, lanes, b, c = first_pass(x, y, b2, c2, log)
    got = lax.all_to_all(message, "seq", 0, 0)
    dbp, dc_send, dc_keep, s = ascend(x, y, b, c, rows, lanes)
    got, dbp = lax.optimization_barrier((got, dbp))
    bound = lax.all_to_all(scan_blocks(got), "seq", 0, 0)
    db_send, db_keep, d = descend(x, y, c, rows, lanes, dbp)
    bound, d = lax.optimization_barrier((bound, d))
    pair = [(i, i ^ 1) for i in range(8)]
    block = (STATE, HALF)
    sent_out, own_out = in_vmem(
        "out_send", send_out_kernel, [(3, *block), block], bound, edge, y, dc_send
    )
    got_out = lax.ppermute(sent_out, "head", pair)
    db_send, sent_out = lax.optimization_barrier((db_send, sent_out))
    sent_in, sent_own = in_vmem(
        "in_send", send_in_kernel, [(3, *block), block], bound, edge, x, db_send
    )
    got_in = lax.ppermute(sent_in, "head", pair)
    dc_keep, sent_in = lax.optimization_barrier((dc_keep, sent_in))
    (kept,) = in_vmem(
        "keep", keep_kernel, [(4, 2, *block)], bound, edge, x, y, db_keep, dc_keep
    )
    parts = in_vmem("sum_cores", sum_kernel, [(2, *block)] * 4, kept, got_out, got_in)
    hops = [(2, 6), (6, 2), (4, 4)]
    moved = [
        lax.ppermute(part, "head", [(i, i ^ hop[i % 2]) for i in range(8)])
        for part, hop in zip(parts[1:], hops)
    ]
    grad_x, grad_log = last_pass(x, y, b, c, rows, lanes, bound, s, d)
    sent_own, own_out, grad_log = lax.optimization_barrier((sent_own, own_out, grad_log))
    late = [lax.ppermute(part, "head", pair) for part in (sent_own, own_out)]
    grad_in, grad_out = in_vmem(
        "merge", merge_kernel, [(2 * HALF, STATE)] * 2, parts[0], *late, *moved
    )
    return (
        jnp.transpose(grad_x.reshape(HEADS_HERE, WIDTH, TOK), (2, 0, 1)),
        jnp.transpose(grad_log),
        grad_in.reshape(HALF, 2, STATE),
        grad_out.reshape(HALF, 2, STATE),
    )


def solution(mesh):
    in_specs = (
        P("seq", "head", None),
        P("seq", "head"),
        P("seq", None, None),
        P("seq", None, None),
        P("seq", "head", None),
    )
    out_specs = (
        P("seq", "head", None),
        P("seq", "head"),
        P(("seq", "head"), None, None),
        P(("seq", "head"), None, None),
    )
    return jax.shard_map(local, mesh=mesh, in_specs=in_specs, out_specs=out_specs, check_vma=False)
```
